32 devices in a mesh: section: 2 (over x), dp: 16 (over z, y, core).
Axes of the slice: x: 2, y: 2, z: 4, core: 2. Of those that a mesh axis runs over, the one named last changes fastest.
Arguments:
- section_data: bfloat16 [2, 2, 16, 640, 512], P('section', None, 'dp'), may hold values from -6 to 6
- lang_feat: bfloat16 [2, 16, 77, 512], P(None, 'dp'), may hold values from -6 to 6
- lang_ids: int32 [2, 16, 77], P(None, 'dp'), may hold values from 0 to 49407, as said below
- view_mask: int32 [2, 16, 5], P(None, 'dp'), may hold values from 0 to 1, as said below
- norm_gains: float32 [2, 2, 512], P('section'), may hold values from 0.5 to 1.5
- shifts: float32 [2, 4, 512], P('section'), may hold values from -1.2 to 1.2
- fc1_bias: float32 [2, 2048], P('section'), may hold values from -1.2 to 1.2
- w_qkv: bfloat16 [2, 512, 1536], P('section'), may hold values from -0.375 to 0.375
- w_out: bfloat16 [2, 512, 512], P('section'), may hold values from -0.75 to 0.75
- w_fc1: bfloat16 [2, 512, 2048], P('section'), may hold values from -0.25 to 0.25
- w_fc2: bfloat16 [2, 2048, 512], P('section'), may hold values from -0.125 to 0.125
Outputs:
- section_results: bfloat16 [2, 2, 16, 640, 512], P('section', None, 'dp')
- gain_grad: float32 [2, 2, 512], P('section')
- shift_grad: float32 [2, 4, 512], P('section')
- fc1_bias_grad: float32 [2, 2048], P('section')
- qkv_grad: float32 [2, 512, 1536], P('section')
- out_grad: float32 [2, 512, 512], P('section')
- fc1_grad: float32 [2, 512, 2048], P('section')
- fc2_grad: float32 [2, 2048, 512], P('section')
The draws below stay inside these ranges and needn't reach their ends.
Inputs may be any that keep to these rules, and one draw needn't show every extreme that they name: `view_mask`: at most 2 of an item's 5 views are occluded, and in every micro-batch some item has exactly 2 occluded. `lang_ids`: in each item the nonzero ids come first and the zeros (padding) after them; the first id is never zero, and in every micro-batch some item has no padding.
All inputs are finite; a program needn't handle non-finite values.
Results may differ from the reference program's by a relative error of at most 0.025.
The reference program's roundings to bfloat16 on the way count: a program that leaves them out, or rounds other values in their place, can miss the bound.
Values may be sent and summed in bfloat16 or wider, within the bound.
A program may use at most 256 MiB of HBM per device.

```python
import jax
import jax.numpy as jnp
from jax import lax

D = 512
HEADS = 8
HEAD = 64
FF = 2048
VIEWS = 5
PATCH = 128
LANG = 77
VOCAB = 49408
MICRO = 2
BATCH = 16
ROWS = 640
KEYS = 717


def draw_lang_ids(key, part):
    key = jax.random.fold_in(key, 7)
    key_length, key_full, key_tokens = jax.random.split(key, 3)
    lengths = jax.random.randint(key_length, (MICRO, BATCH), 1, LANG + 1)
    full_item = jax.random.randint(key_full, (MICRO, 1), 0, BATCH)
    lengths = jnp.where(jnp.arange(BATCH)[None, :] == full_item, LANG, lengths)
    tokens = jax.random.randint(key_tokens, (MICRO, BATCH, LANG), 1, VOCAB)
    places = jnp.arange(LANG)
    return jnp.where(places[None, None, :] < lengths[:, :, None], tokens, 0).astype(jnp.int32)


def draw_view_mask(key, part):
    key = jax.random.fold_in(key, 13)
    key_count, key_pick, key_order = jax.random.split(key, 3)
    missing = jax.random.randint(key_count, (MICRO, BATCH), 0, 3)
    chosen = jax.random.randint(key_pick, (MICRO, 1), 0, BATCH)
    missing = jnp.where(jnp.arange(BATCH)[None, :] == chosen, 2, missing)
    scores = jax.random.randint(key_order, (MICRO, BATCH, VIEWS), 0, 1 << 20) * VIEWS + jnp.arange(VIEWS)
    ordering = jnp.argsort(jnp.argsort(scores, axis=-1, stable=True), axis=-1, stable=True)
    return (ordering >= missing[:, :, None]).astype(jnp.int32)


def levels(stream_key, dims, cuts, low, top_value):
    loudness, own = 1.0, jax.random.fold_in(stream_key, 6)
    for axis_at, blocks in cuts:
        steps = jnp.exp(jax.random.uniform(jax.random.fold_in(own, axis_at), (blocks,), jnp.float32, low / len(cuts), top_value / len(cuts)))
        loudness = loudness * jnp.repeat(steps, dims[axis_at] // blocks).reshape([-1 if axis == axis_at else 1 for axis in range(len(dims))])
    return loudness


def gaussian(own_key, dims, deviation, most, cuts=(), kind=jnp.bfloat16):
    entries = deviation * jax.random.normal(own_key, dims, jnp.float32)
    if cuts:
        entries = entries * levels(own_key, dims, cuts, -0.22, 0.18)
    return jnp.clip(entries, -most, most).astype(kind)


def setup_inputs(seed: int = 0) -> dict:
    seeds = jax.random.split(jax.random.key(seed), 12)
    return {
        "section_data": gaussian(seeds[0], (2, MICRO, BATCH, ROWS, D), 1.0, 6.0, ((0, 2), (2, 16))),
        "lang_feat": gaussian(seeds[1], (MICRO, BATCH, LANG, D), 1.0, 6.0, ((1, 16),)),
        "lang_ids": draw_lang_ids(jax.random.fold_in(seeds[11], 71), 0),
        "view_mask": draw_view_mask(jax.random.fold_in(seeds[11], 71), 0),
        "norm_gains": jnp.clip(1.0 + 0.1 * jax.random.normal(seeds[4], (2, 2, D), jnp.float32), 0.5, 1.5),
        "shifts": gaussian(seeds[5], (2, 4, D), 0.2, 1.2, ((0, 2),), jnp.float32),
        "fc1_bias": gaussian(seeds[6], (2, FF), 0.2, 1.2, ((0, 2),), jnp.float32),
        "w_qkv": gaussian(seeds[7], (2, D, 3 * D), (D // 2) ** -0.5, 0.375, ((0, 2),)),
        "w_out": gaussian(seeds[8], (2, D, D), (D // 8) ** -0.5, 0.75, ((0, 2),)),
        "w_fc1": gaussian(seeds[9], (2, D, FF), D ** -0.5, 0.25, ((0, 2),)),
        "w_fc2": gaussian(seeds[10], (2, FF, D), FF ** -0.5, 0.125, ((0, 2),)),
    }


@jax.custom_vjp
def low(v):
    return lax.optimization_barrier(v.astype(jnp.bfloat16)).astype(jnp.float32)

@jax.custom_vjp
def low_back(v):
    return v

def low_keep(v):
    return (low(v), None)

def low_pass(kept, grad):
    return (grad,)

def back_keep(v):
    return (v, None)

def back_low(kept, grad):
    return (low(grad),)
low.defvjp(low_keep, low_pass)
low_back.defvjp(back_keep, back_low)
epsilon = 1e-05
highest = lax.Precision.HIGHEST

def ln_affine(values, gain_row, shift_row):
    average = lax.optimization_barrier(jnp.mean(values, -1, keepdims=True))
    centred = values - average
    spread = lax.optimization_barrier(jnp.mean(centred * centred, -1, keepdims=True))
    return centred * lax.rsqrt(spread + epsilon) * gain_row + shift_row

def matmul(left, right):
    return jnp.dot(left, right, precision=highest, preferred_element_type=jnp.float32)

def softmax_rows(scores):
    top_score = lax.optimization_barrier(jnp.max(scores, -1, keepdims=True))
    weights_raw = jnp.exp(scores - top_score)
    return weights_raw / lax.optimization_barrier(jnp.sum(weights_raw, -1, keepdims=True))

def layer_apply(hidden, params, lang_rows, allowed):
    gain_rows, shift_rows, bias_ff, weight_qkv, weight_out, weight_up, weight_down = params
    row_count = hidden.shape[0]
    scaling = HEAD ** (-0.5)
    normed = low(ln_affine(hidden, gain_rows[0], shift_rows[0]))
    qkv_rows = low(low_back(matmul(normed, weight_qkv)))
    queries = qkv_rows[:, :D].reshape(row_count, HEADS, HEAD)
    keys_all = qkv_rows[:, D:2 * D].reshape(row_count, HEADS, HEAD)
    values_all = qkv_rows[:, 2 * D:].reshape(row_count, HEADS, HEAD)
    if lang_rows is None:
        view_queries = queries.reshape(VIEWS, PATCH, HEADS, HEAD)
        view_keys = keys_all.reshape(VIEWS, PATCH, HEADS, HEAD)
        view_values = values_all.reshape(VIEWS, PATCH, HEADS, HEAD)
        scores = low_back(jnp.einsum('vqhe,vkhe->vhqk', view_queries, view_keys, precision=highest) * scaling)
        probs = low(softmax_rows(scores))
        attended = jnp.einsum('vhqk,vkhe->vqhe', probs, view_values, precision=highest).reshape(row_count, D)
    else:
        lang_normed = low(ln_affine(lang_rows, gain_rows[0], shift_rows[0]))
        lang_kv = low(low_back(matmul(lang_normed, weight_qkv[:, D:])))
        lang_count = lang_rows.shape[0]
        keys_all = jnp.concatenate([keys_all, lang_kv[:, :D].reshape(lang_count, HEADS, HEAD)], 0)
        values_all = jnp.concatenate([values_all, lang_kv[:, D:].reshape(lang_count, HEADS, HEAD)], 0)
        scores = low_back(jnp.einsum('qhe,khe->hqk', queries, keys_all, precision=highest) * scaling)
        scores = jnp.where(allowed[None, None, :], scores, -jnp.inf)
        probs = low(softmax_rows(scores))
        attended = jnp.einsum('hqk,khe->qhe', probs, values_all, precision=highest).reshape(row_count, D)
    attended = low(low_back(attended))
    hidden_mid = hidden + low_back(matmul(attended, weight_out) + shift_rows[1])
    normed_mid = low(ln_affine(hidden_mid, gain_rows[1], shift_rows[2]))
    pre_act = low_back(matmul(normed_mid, weight_up) + bias_ff)
    activ = low(jax.nn.gelu(pre_act, approximate=False))
    return hidden_mid + low_back(matmul(activ, weight_down) + shift_rows[3])

def per_item(first_params, second_params, operands):
    item_rows, item_lang, item_allowed = operands
    middle = layer_apply(item_rows, first_params, None, None)
    middle = low(low_back(middle))
    return layer_apply(middle, second_params, item_lang, item_allowed)

def reference(section_data, lang_feat, lang_ids, view_mask, norm_gains, shifts, fc1_bias, w_qkv, w_out, w_fc1, w_fc2):
    item_count = MICRO * BATCH
    inputs = section_data[0].astype(jnp.float32).reshape(item_count, ROWS, D)
    cotangent = section_data[1].astype(jnp.float32).reshape(item_count, ROWS, D)
    lang_rows = lang_feat.astype(jnp.float32).reshape(item_count, LANG, D)
    present = jnp.repeat(view_mask > 0, PATCH, axis=-1)
    allowed = jnp.concatenate([present, lang_ids != 0], -1).reshape(item_count, KEYS)

    def section_params(number):
        return (norm_gains[number].astype(jnp.float32), shifts[number].astype(jnp.float32), fc1_bias[number].astype(jnp.float32), w_qkv[number].astype(jnp.float32), w_out[number].astype(jnp.float32), w_fc1[number].astype(jnp.float32), w_fc2[number].astype(jnp.float32))
    checked = jax.checkpoint(per_item)

    def whole(item_inputs, first_params, second_params):
        return lax.map(lambda operands: checked(first_params, second_params, operands), (item_inputs, lang_rows, allowed))
    outputs, pull_back = jax.vjp(whole, inputs, section_params(0), section_params(1))
    grad_inputs, grad_first, grad_second = pull_back(cotangent)
    full_shape = (MICRO, BATCH, ROWS, D)
    section_results = jnp.stack([grad_inputs.reshape(full_shape), outputs.reshape(full_shape)]).astype(jnp.bfloat16)

    def paired(number):
        return jnp.stack([grad_first[number], grad_second[number]])
    return (section_results, paired(0), paired(1), paired(2), paired(3), paired(4), paired(5), paired(6))
```

```python
import functools

import jax
import jax.numpy as jnp
from jax import lax
from jax.experimental import pallas as pl
from jax.experimental.pallas import tpu as pltpu
from jax.sharding import PartitionSpec as P

HEADS = 8
HEAD = 64
VIEWS = 5
BLK = 128
EPS = 1e-05
MASKED = -1e30
SCALE = HEAD**-0.5
LOG2E = 1.4426950408889634
MESH = pl.DeviceIdType.MESH
bf16 = jnp.bfloat16
f32 = jnp.float32
VMEM_LIMIT = 64 * 2**20 - 2**19


def dot(a, b, ca, cb):
    return lax.dot_general(a, b, (((ca,), (cb,)), ((), ())), preferred_element_type=f32)


def normalise(v):
    centred = v - jnp.mean(v, -1, keepdims=True)
    r = lax.rsqrt(jnp.mean(centred * centred, -1, keepdims=True) + EPS)
    return centred * r, r


def norm_back(v, grad, gain):
    xhat, r = normalise(v)
    gm = grad * gain
    along = jnp.mean(gm * xhat, -1, keepdims=True)
    dv = r * (gm - jnp.mean(gm, -1, keepdims=True) - xhat * along)
    return dv, jnp.sum(grad * xhat, 0, keepdims=True), jnp.sum(grad, 0, keepdims=True)


def gelu_pair(x):
    phi = 0.5 * (1.0 + lax.erf(x * 0.7071067811865476))
    density = jnp.exp2(x * x * (-0.5 * LOG2E)) * 0.3989422804014327
    return x * phi, phi + x * density


def blk(i):
    return pl.ds(pl.multiple_of(i * BLK, BLK), BLK)


def step_kernel(sd, lf, ids, vm, ng, sh, fb, wq_h, wo_h, w1_h, w2_h,
                res, og2, og1, ogq, ogo, osm,
                h, dy, wq, wo, w1, w2, nT, qT, kvT, kv, PT, linv, attT, hm, nm, act, gg, gb, dOT, ob,
                bias, g2, g1, gq, go, sm, sb,
                in_sem, w_sem, res_sem, act_send, act_recv, grad_send, grad_recv, out_sem):
    sec = lax.axis_index("section")
    D = wo.shape[0]
    FF = w1.shape[1]
    R = h.shape[1]
    NB = R // BLK
    LROWS = lf.shape[2]
    KP = kvT.shape[2]
    LP = KP - R
    micro = h.shape[0]
    peer = {"section": 1 - sec}

    def w_copy(k):
        src, dst = ((wq_h, wq), (wo_h, wo), (w1_h, w1), (w2_h, w2))[k]
        return pltpu.make_async_copy(src.at[0], dst, w_sem.at[k])

    def in_copy(m, dst):
        return pltpu.make_async_copy(sd.at[0, m, 0], dst.at[m], in_sem.at[m])

    def res_copy(m, i):
        return pltpu.make_async_copy(ob.at[m, blk(i)], res.at[0, m, 0, blk(i)], res_sem.at[m, i])

    def act_copy(m, i):
        return pltpu.make_async_remote_copy(
            src_ref=ob.at[m, blk(i)], dst_ref=h.at[m, blk(i)], send_sem=act_send.at[m, i],
            recv_sem=act_recv.at[m, i], device_id=peer, device_id_type=MESH)

    def grad_copy(m, i):
        return pltpu.make_async_remote_copy(
            src_ref=ob.at[m, blk(i)], dst_ref=dy.at[m, blk(i)], send_sem=grad_send.at[m, i],
            recv_sem=grad_recv.at[m, i], device_id=peer, device_id_type=MESH)

    gain0, gain1 = ng[0, 0:1], ng[0, 1:2]
    shift = [sh[0, k:k + 1] for k in range(4)]

    def qkv_phase(m, joint):
        def body(i, c):
            if joint:
                act_copy(m, i).wait_recv()
            xhat, _ = normalise(h[m, blk(i)].astype(f32))
            n = (xhat * gain0 + shift[0]).astype(bf16)
            nT[m, :, blk(i)] = n.T
            rows = dot(n, wq[...], 1, 0).astype(bf16)
            qT[m, :, blk(i)] = rows[:, :D].T
            kvT[m, :, blk(i)] = rows[:, D:].T
            kv[m, blk(i), :] = rows[:, D:]
            return c
        lax.fori_loop(0, NB, body, 0)

    def lang_phase(m):
        xhat = lang_xhat(m)
        n = (xhat * gain0 + shift[0]).astype(bf16)
        nT[m, :, R:KP] = n.T
        rows = dot(n, wq[:, D:], 1, 0).astype(bf16)
        kvT[m, :, R:KP] = rows.T
        kv[m, R:KP, :] = rows
        for v in range(VIEWS):
            seen = (vm[m, 0, v] > 0).astype(f32)
            bias[m, v * BLK:(v + 1) * BLK, :] = jnp.full((BLK, BLK), MASKED, f32) * (1.0 - seen)
        count = jnp.sum((ids[m] != 0).astype(jnp.int32), -1, keepdims=True)
        place = lax.broadcasted_iota(jnp.int32, (LP, BLK), 0)
        bias[m, R:KP, :] = jnp.where(place < count, 0.0, MASKED)

    def lang_xhat(m):
        rows = jnp.concatenate([lf[m, 0].astype(f32), jnp.zeros((LP - LROWS, D), f32)], 0)
        return normalise(rows)[0]

    def paired(block):
        zero = jnp.zeros((HEAD, block.shape[1]), block.dtype)
        return jnp.concatenate([jnp.concatenate([block[:HEAD], zero], 0),
                                jnp.concatenate([zero, block[HEAD:]], 0)], 1)

    def joint_attention(m):
        def body(hp, c):
            q2 = paired(qT[m, blk(hp), :])
            s = dot(kv[m, :, blk(hp)], q2, 1, 0)
            s = s + jnp.concatenate([bias[m]] * (2 * NB), 1)
            top = jnp.max(s, 0, keepdims=True) * (SCALE * LOG2E)
            p = jnp.exp2(s * (SCALE * LOG2E) - top)
            inv = 1.0 / jnp.sum(p, 0, keepdims=True)
            pb = p.astype(bf16)
            for j in range(2):
                head = 2 * hp + j
                PT[head] = pb[:, j * R:(j + 1) * R]
                linv[m, head] = inv[:, j * R:(j + 1) * R]
                rows = pl.ds(pl.multiple_of(head * HEAD, HEAD), HEAD)
                vT = kvT[m, pl.ds(pl.multiple_of(D + head * HEAD, HEAD), HEAD), :]
                out = dot(vT, pb[:, j * R:(j + 1) * R], 1, 0) * inv[:, j * R:(j + 1) * R]
                attT[m, rows, :] = out.astype(bf16)
            return c
        lax.fori_loop(0, HEADS // 2, body, 0)

    def view_attention(m):
        def body(hp, c):
            vrow = pl.ds(pl.multiple_of(D + hp * BLK, BLK), BLK)
            for v in range(NB):
                col = slice(v * BLK, (v + 1) * BLK)
                q2 = paired(qT[m, blk(hp), col])
                s = dot(kv[m, col, blk(hp)], q2, 1, 0)
                top = jnp.max(s, 0, keepdims=True) * (SCALE * LOG2E)
                p = jnp.exp2(s * (SCALE * LOG2E) - top)
                inv = 1.0 / jnp.sum(p, 0, keepdims=True)
                pb = p.astype(bf16)
                PT[4 * m + hp, col, 0:2 * BLK] = pb
                for j in range(2):
                    linv[m, 2 * hp + j, :, col] = inv[:, j * BLK:(j + 1) * BLK]
                out = dot(kvT[m, vrow, col], pb, 1, 0) * inv
                attT[m, blk(hp), col] = jnp.concatenate(
                    [out[:HEAD, :BLK], out[HEAD:, BLK:]], 0).astype(bf16)
            return c
        lax.fori_loop(0, HEADS // 2, body, 0)

    def mlp_phase(m, joint):
        def body(i, c):
            mid = h[m, blk(i)].astype(f32) + dot(attT[m, :, blk(i)], wo[...], 0, 0) + shift[1]
            hm[m, blk(i)] = mid
            xhat, _ = normalise(mid)
            n = (xhat * gain1 + shift[2]).astype(bf16)
            nm[m, blk(i)] = n
            for k in range(0, FF, 256):
                a, slope = gelu_pair(dot(n, w1[:, k:k + 256], 1, 0) + fb[:, k:k + 256])
                act[m, blk(i), k:k + 256] = a.astype(bf16)
                gg[m, blk(i), k:k + 256] = slope.astype(bf16)
            out = mid + dot(act[m, blk(i)], w2[...], 1, 0) + shift[3]
            ob[m, blk(i)] = out.astype(bf16)
            if joint:
                res_copy(m, i).start()
            else:
                act_copy(m, i).start()
            return c
        lax.fori_loop(0, NB, body, 0)

    def mlp_back(m, joint):
        def body(i, c):
            if not joint:
                grad_copy(m, i).wait_recv()
            d = dy[m, blk(i)]
            parts = []
            for k in range(0, FF, 512):
                gp = (dot(d, w2[k:k + 512], 1, 1) * gg[m, blk(i), k:k + 512].astype(f32)).astype(bf16)
                gg[m, blk(i), k:k + 512] = gp
                sb[:, k:k + 512] += jnp.sum(gp.astype(f32), 0, keepdims=True)
            gn = dot(gg[m, blk(i)], w1[...], 1, 1)
            d32 = d.astype(f32)
            dv, dgain, dshift = norm_back(hm[m, blk(i)], gn, gain1)
            mid = d32 + dv
            hm[m, blk(i)] = mid
            low = mid.astype(bf16)
            gb[m, blk(i)] = low
            sm[1:2] += dgain
            sm[4:5] += dshift
            sm[5:6] += jnp.sum(d32, 0, keepdims=True)
            sm[3:4] += jnp.sum(low.astype(f32), 0, keepdims=True)
            return c
        lax.fori_loop(0, NB, body, 0)
        dOT[...] = dot(wo[...], gb[m], 1, 1).astype(bf16)

    def joint_attention_back(m):
        def body(hp, c):
            inv = jnp.concatenate([linv[m, 2 * hp], linv[m, 2 * hp + 1]], 1)
            block = dOT[blk(hp), :].astype(f32)
            d0 = (block[:HEAD] * inv[:, :R]).astype(bf16)
            d1 = (block[HEAD:] * inv[:, R:]).astype(bf16)
            zero = jnp.zeros((HEAD, R), bf16)
            d2 = jnp.concatenate([jnp.concatenate([d0, zero], 0), jnp.concatenate([zero, d1], 0)], 1)
            vcol = pl.ds(pl.multiple_of(D + hp * BLK, BLK), BLK)
            dp = dot(kv[m, :, vcol], d2, 1, 0)
            pb = jnp.concatenate([PT[2 * hp], PT[2 * hp + 1]], 1)
            p = pb.astype(f32)
            inner = jnp.sum(p * dp, 0, keepdims=True) * inv
            ds = (p * (dp - inner)).astype(bf16)
            for j in range(2):
                head = 2 * hp + j
                side = slice(j * R, (j + 1) * R)
                rows = pl.ds(pl.multiple_of(head * HEAD, HEAD), HEAD)
                vrows = pl.ds(pl.multiple_of(D + head * HEAD, HEAD), HEAD)
                kvT[m, vrows, :] = dot((d0, d1)[j], PT[head], 1, 1).astype(bf16)
                dq = dot(kvT[m, rows, :], ds[:, side], 1, 0) * SCALE
                kvT[m, rows, :] = (dot(qT[m, rows, :], ds[:, side], 1, 1) * SCALE).astype(bf16)
                qT[m, rows, :] = dq.astype(bf16)
            return c
        lax.fori_loop(0, HEADS // 2, body, 0)

    def view_attention_back(m):
        def body(hp, c):
            vrow = pl.ds(pl.multiple_of(D + hp * BLK, BLK), BLK)
            for v in range(NB):
                col = slice(v * BLK, (v + 1) * BLK)
                inv = jnp.concatenate([linv[m, 2 * hp, :, col], linv[m, 2 * hp + 1, :, col]], 1)
                d2 = (paired(dOT[blk(hp), col]).astype(f32) * inv).astype(bf16)
                dp = dot(kv[m, col, vrow], d2, 1, 0)
                pb = PT[4 * m + hp, col, 0:2 * BLK]
                p = pb.astype(f32)
                inner = jnp.sum(p * dp, 0, keepdims=True) * inv
                ds = (p * (dp - inner)).astype(bf16)
                kvT[m, vrow, col] = dot(d2, pb, 1, 1).astype(bf16)
                q2 = paired(qT[m, blk(hp), col])
                dq = dot(kvT[m, blk(hp), col], ds, 1, 0) * SCALE
                kvT[m, blk(hp), col] = (dot(q2, ds, 1, 1) * SCALE).astype(bf16)
                qT[m, blk(hp), col] = jnp.concatenate([dq[:HEAD, :BLK], dq[HEAD:, BLK:]], 0).astype(bf16)
            return c
        lax.fori_loop(0, HEADS // 2, body, 0)

    def qkv_back(m, joint):
        def body(i, c):
            gn = dot(qT[m, :, blk(i)], wq[:, :D], 0, 1) + dot(kvT[m, :, blk(i)], wq[:, D:], 0, 1)
            dv, dgain, dshift = norm_back(h[m, blk(i)].astype(f32), gn, gain0)
            sm[0:1] += dgain
            sm[2:3] += dshift
            out = (hm[m, blk(i)] + dv).astype(bf16)
            if joint:
                res_copy(m, i).wait()
            else:
                act_copy(m, i).wait_send()
            ob[m, blk(i)] = out
            if joint:
                grad_copy(m, i).start()
            else:
                res_copy(m, i).start()
            return c
        lax.fori_loop(0, NB, body, 0)
        if joint:
            gn = dot(kvT[m, :, R:KP], wq[:, D:], 0, 1)
            sm[0:1] += jnp.sum(gn * lang_xhat(m), 0, keepdims=True)
            sm[2:3] += jnp.sum(gn, 0, keepdims=True)

    def mlp_weights(ms, add):
        for k in range(0, FF, 512):
            t = sum(dot(act[m, :, k:k + 512], dy[m], 0, 0) for m in ms)
            g2[k:k + 512] = (t + g2[k:k + 512].astype(f32) if add else t).astype(bf16)
        for k in range(0, FF, 1024):
            t = sum(dot(nm[m], gg[m, :, k:k + 1024], 0, 0) for m in ms)
            g1[:, k:k + 1024] = (t + g1[:, k:k + 1024].astype(f32) if add else t).astype(bf16)

    def attention_weights(ms, add, joint):
        t = sum(dot(attT[m], gb[m], 1, 0) for m in ms)
        go[...] = (t + go[...].astype(f32) if add else t).astype(bf16)
        t = sum(dot(nT[m, :, 0:R], qT[m], 1, 1) for m in ms)
        gq[:, 0:D] = (t + gq[:, 0:D].astype(f32) if add else t).astype(bf16)
        keys = KP if joint else R
        t = sum(dot(nT[m, :, 0:keys], kvT[m, :, 0:keys], 1, 1) for m in ms)
        gq[:, D:3 * D] = (t + gq[:, D:3 * D].astype(f32) if add else t).astype(bf16)

    barrier = pltpu.get_barrier_semaphore()
    pl.semaphore_signal(barrier, inc=1, device_id=peer, device_id_type=MESH)
    pl.semaphore_wait(barrier, 1)
    sm[...] = jnp.zeros_like(sm)
    sb[...] = jnp.zeros_like(sb)

    @pl.when(sec == 0)
    def _():
        for m in range(micro):
            in_copy(m, h).start()
            if m == 0:
                for k in range(4):
                    w_copy(k).start()

        def forward(m, c):
            in_copy(m, h).wait()

            @pl.when(m == 0)
            def _():
                w_copy(0).wait()
            qkv_phase(m, False)
            view_attention(m)

            @pl.when(m == 0)
            def _():
                for k in range(1, 4):
                    w_copy(k).wait()
            mlp_phase(m, False)
            return c
        lax.fori_loop(0, micro, forward, 0)

        def backward(m, add):
            mlp_back(m, False)
            mlp_weights([m], add)
            view_attention_back(m)
            qkv_back(m, False)
            attention_weights([m], add, False)
        for m in range(micro):
            backward(m, m > 0)
        for m in range(micro):
            for i in range(NB):
                res_copy(m, i).wait()

    @pl.when(sec == 1)
    def _():
        for k in range(4):
            w_copy(k).start()
        for m in range(micro):
            in_copy(m, dy).start()
        for k in range(4):
            w_copy(k).wait()
        for m in range(micro):
            in_copy(m, dy).wait()

        def languages(m, c):
            lang_phase(m)
            return c
        lax.fori_loop(0, micro, languages, 0)

        def item(m, c):
            qkv_phase(m, True)
            joint_attention(m)
            mlp_phase(m, True)
            mlp_back(m, True)
            joint_attention_back(m)
            qkv_back(m, True)
            return c
        lax.fori_loop(0, micro, item, 0)
        mlp_weights(range(micro), False)
        attention_weights(range(micro), False, True)
        for m in range(micro):
            for i in range(NB):
                grad_copy(m, i).wait_send()

    copies = [pltpu.make_async_copy(s, d, out_sem.at[k]) for k, (s, d) in enumerate(
        ((g2, og2), (g1, og1), (gq, ogq), (go, ogo)))]
    for copy in copies:
        copy.start()
    osm[0:6] = sm[0:6]
    for k in range(FF // D):
        osm[6 + k:7 + k] = sb[:, k * D:(k + 1) * D]
    for copy in copies:
        copy.wait()


def local(section_data, lang_feat, lang_ids, view_mask, norm_gains, shifts, fc1_bias, w_qkv, w_out, w_fc1, w_fc2):
    micro, rows, D = section_data.shape[1], section_data.shape[3], section_data.shape[4]
    FF = w_fc1.shape[2]
    lang = lang_feat.shape[2]
    KP = rows + -(-lang // 16) * 16
    NB = rows // BLK
    hbm = pl.BlockSpec(memory_space=pl.ANY)
    vmem = pl.BlockSpec(memory_space=pltpu.VMEM)
    smem = pl.BlockSpec(memory_space=pltpu.SMEM)
    V = pltpu.VMEM
    dma = pltpu.SemaphoreType.DMA
    sds = jax.ShapeDtypeStruct
    outs = pl.pallas_call(
        step_kernel,
        out_shape=(
            sds(section_data.shape, bf16), sds((FF, D), bf16), sds((D, FF), bf16),
            sds((D, 3 * D), bf16), sds((D, D), bf16), sds((16, D), f32)),
        in_specs=[hbm, vmem, vmem, smem, vmem, vmem, vmem, hbm, hbm, hbm, hbm],
        out_specs=(hbm, hbm, hbm, hbm, hbm, vmem),
        scratch_shapes=[
            V((micro, rows, D), bf16),
            V((micro, rows, D), bf16),
            V((D, 3 * D), bf16), V((D, D), bf16), V((D, FF), bf16), V((FF, D), bf16),
            V((micro, D, KP), bf16),
            V((micro, D, rows), bf16),
            V((micro, 2 * D, KP), bf16),
            V((micro, KP, 2 * D), bf16),
            V((HEADS, KP, rows), bf16),
            V((micro, HEADS, 1, rows), f32),
            V((micro, D, rows), bf16),
            V((micro, rows, D), f32),
            V((micro, rows, D), bf16),
            V((micro, rows, FF), bf16),
            V((micro, rows, FF), bf16),
            V((micro, rows, D), bf16),
            V((D, rows), bf16),
            V((micro, rows, D), bf16),
            V((micro, KP, BLK), f32),
            V((FF, D), bf16), V((D, FF), bf16), V((D, 3 * D), bf16), V((D, D), bf16),
            V((8, D), f32), V((1, FF), f32),
            dma((micro,)), dma((4,)), dma((micro, NB)),
            dma((micro, NB)), dma((micro, NB)), dma((micro, NB)), dma((micro, NB)), dma((4,)),
        ],
        compiler_params=pltpu.CompilerParams(
            collective_id=0, has_side_effects=True, vmem_limit_bytes=VMEM_LIMIT),
        name="two_layers",
    )(section_data, lang_feat, lang_ids, view_mask, norm_gains, shifts, fc1_bias, w_qkv, w_out, w_fc1, w_fc2)
    res, g2, g1, gq, go, sm = outs
    sm = lax.psum(sm, "dp")
    g2, g1, gq, go = lax.psum((g2, g1, gq, go), "dp")
    return (
        res,
        sm[0:2][None],
        sm[2:6][None],
        sm[6:6 + FF // D].reshape(1, FF),
        gq.astype(f32)[None],
        go.astype(f32)[None],
        g1.astype(f32)[None],
        g2.astype(f32)[None],
    )


def solution(mesh):
    weights = P("section", None, None)
    rows = P("section", None, "dp", None, None)
    return jax.shard_map(
        local,
        mesh=mesh,
        in_specs=(rows, P(None, "dp", None, None), P(None, "dp", None), P(None, "dp", None), weights, weights,
                  P("section", None), weights, weights, weights, weights),
        out_specs=(rows, weights, weights, P("section", None), weights, weights, weights, weights),
        check_vma=False,
    )
```

```python
import functools

import jax
import jax.numpy as jnp
from jax import lax
from jax.experimental import pallas as pl
from jax.experimental.pallas import tpu as pltpu
from jax.sharding import PartitionSpec as P

HEADS = 8
HEAD = 64
VIEWS = 5
BLK = 128
EPS = 1e-05
MASKED = -1e30
SCALE = HEAD**-0.5
LOG2E = 1.4426950408889634
MESH = pl.DeviceIdType.MESH
bf16 = jnp.bfloat16
f32 = jnp.float32
VMEM_LIMIT = 64 * 2**20 - 2**19


def dot(a, b, ca, cb):
    return lax.dot_general(a, b, (((ca,), (cb,)), ((), ())), preferred_element_type=f32)


def normalise(v):
    centred = v - jnp.mean(v, -1, keepdims=True)
    r = lax.rsqrt(jnp.mean(centred * centred, -1, keepdims=True) + EPS)
    return centred * r, r


def norm_back(v, grad, gain):
    xhat, r = normalise(v)
    gm = grad * gain
    along = jnp.mean(gm * xhat, -1, keepdims=True)
    dv = r * (gm - jnp.mean(gm, -1, keepdims=True) - xhat * along)
    return dv, jnp.sum(grad * xhat, 0, keepdims=True), jnp.sum(grad, 0, keepdims=True)


def gelu_pair(x):
    phi = 0.5 * (1.0 + lax.erf(x * 0.7071067811865476))
    density = jnp.exp2(x * x * (-0.5 * LOG2E)) * 0.3989422804014327
    return x * phi, phi + x * density


def blk(i):
    return pl.ds(pl.multiple_of(i * BLK, BLK), BLK)


def step_kernel(sd, lf, ids, vm, ng, sh, fb, wq_h, wo_h, w1_h, w2_h,
                res, oA, oB, oS,
                h, dy, wq, wo, w1, w2, nT, qT, kvT, kv, PT, linv, attT, hm, nm, act, gg, gb, dOT, ob,
                bias, sm, sb, stage, gA, gB, gS, *rest):
    ring = len(rest) > 8
    if ring:
        sibA, sibB, sibS, hopA, hopB, hopS = rest[:6]
        rest = rest[6:]
    (in_sem, w_sem, res_sem, act_send, act_recv, grad_send, grad_recv, out_sem), rest = rest[:8], rest[8:]
    sec = lax.axis_index("section")
    NC = gA.shape[0]
    D = wo.shape[0]
    FF = w1.shape[1]
    R = h.shape[1]
    NB = R // BLK
    LROWS = lf.shape[2]
    KP = kvT.shape[2]
    LP = KP - R
    micro = h.shape[0]
    peer = {"section": 1 - sec}

    def w_copy(k):
        src, dst = ((wq_h, wq), (wo_h, wo), (w1_h, w1), (w2_h, w2))[k]
        return pltpu.make_async_copy(src.at[0], dst, w_sem.at[k])

    def in_copy(m, dst):
        return pltpu.make_async_copy(sd.at[0, m, 0], dst.at[m], in_sem.at[m])

    def res_copy(m, i):
        return pltpu.make_async_copy(ob.at[m, blk(i)], res.at[0, m, 0, blk(i)], res_sem.at[m, i])

    def act_copy(m, i):
        return pltpu.make_async_remote_copy(
            src_ref=ob.at[m, blk(i)], dst_ref=h.at[m, blk(i)], send_sem=act_send.at[m, i],
            recv_sem=act_recv.at[m, i], device_id=peer, device_id_type=MESH)

    def grad_copy(m, i):
        return pltpu.make_async_remote_copy(
            src_ref=ob.at[m, blk(i)], dst_ref=dy.at[m, blk(i)], send_sem=grad_send.at[m, i],
            recv_sem=grad_recv.at[m, i], device_id=peer, device_id_type=MESH)

    gain0, gain1 = ng[0, 0:1], ng[0, 1:2]
    shift = [sh[0, k:k + 1] for k in range(4)]

    def qkv_phase(m, joint):
        def body(i, c):
            if joint:
                act_copy(m, i).wait_recv()
            xhat, _ = normalise(h[m, blk(i)].astype(f32))
            n = (xhat * gain0 + shift[0]).astype(bf16)
            nT[m, :, blk(i)] = n.T
            rows = dot(n, wq[...], 1, 0).astype(bf16)
            qT[m, :, blk(i)] = rows[:, :D].T
            kvT[m, :, blk(i)] = rows[:, D:].T
            kv[m, blk(i), :] = rows[:, D:]
            return c
        lax.fori_loop(0, NB, body, 0)

    def lang_phase(m):
        xhat = lang_xhat(m)
        n = (xhat * gain0 + shift[0]).astype(bf16)
        nT[m, :, R:KP] = n.T
        rows = dot(n, wq[:, D:], 1, 0).astype(bf16)
        kvT[m, :, R:KP] = rows.T
        kv[m, R:KP, :] = rows
        for v in range(VIEWS):
            seen = (vm[m, 0, v] > 0).astype(f32)
            bias[m, v * BLK:(v + 1) * BLK, :] = jnp.full((BLK, BLK), MASKED, f32) * (1.0 - seen)
        count = jnp.sum((ids[m] != 0).astype(jnp.int32), -1, keepdims=True)
        place = lax.broadcasted_iota(jnp.int32, (LP, BLK), 0)
        bias[m, R:KP, :] = jnp.where(place < count, 0.0, MASKED)

    def lang_xhat(m):
        rows = jnp.concatenate([lf[m, 0].astype(f32), jnp.zeros((LP - LROWS, D), f32)], 0)
        return normalise(rows)[0]

    def paired(block):
        zero = jnp.zeros((HEAD, block.shape[1]), block.dtype)
        return jnp.concatenate([jnp.concatenate([block[:HEAD], zero], 0),
                                jnp.concatenate([zero, block[HEAD:]], 0)], 1)

    def joint_attention(m):
        def body(hp, c):
            q2 = paired(qT[m, blk(hp), :])
            s = dot(kv[m, :, blk(hp)], q2, 1, 0)
            s = s + jnp.concatenate([bias[m]] * (2 * NB), 1)
            top = jnp.max(s, 0, keepdims=True) * (SCALE * LOG2E)
            p = jnp.exp2(s * (SCALE * LOG2E) - top)
            inv = 1.0 / jnp.sum(p, 0, keepdims=True)
            pb = p.astype(bf16)
            for j in range(2):
                head = 2 * hp + j
                PT[head] = pb[:, j * R:(j + 1) * R]
                linv[m, head] = inv[:, j * R:(j + 1) * R]
                rows = pl.ds(pl.multiple_of(head * HEAD, HEAD), HEAD)
                vT = kvT[m, pl.ds(pl.multiple_of(D + head * HEAD, HEAD), HEAD), :]
                out = dot(vT, pb[:, j * R:(j + 1) * R], 1, 0) * inv[:, j * R:(j + 1) * R]
                attT[m, rows, :] = out.astype(bf16)
            return c
        lax.fori_loop(0, HEADS // 2, body, 0)

    def view_attention(m):
        def body(hp, c):
            vrow = pl.ds(pl.multiple_of(D + hp * BLK, BLK), BLK)
            for v in range(NB):
                col = slice(v * BLK, (v + 1) * BLK)
                q2 = paired(qT[m, blk(hp), col])
                s = dot(kv[m, col, blk(hp)], q2, 1, 0)
                top = jnp.max(s, 0, keepdims=True) * (SCALE * LOG2E)
                p = jnp.exp2(s * (SCALE * LOG2E) - top)
                inv = 1.0 / jnp.sum(p, 0, keepdims=True)
                pb = p.astype(bf16)
                PT[4 * m + hp, col, 0:2 * BLK] = pb
                for j in range(2):
                    linv[m, 2 * hp + j, :, col] = inv[:, j * BLK:(j + 1) * BLK]
                out = dot(kvT[m, vrow, col], pb, 1, 0) * inv
                attT[m, blk(hp), col] = jnp.concatenate(
                    [out[:HEAD, :BLK], out[HEAD:, BLK:]], 0).astype(bf16)
            return c
        lax.fori_loop(0, HEADS // 2, body, 0)

    def mlp_phase(m, joint):
        def body(i, c):
            mid = h[m, blk(i)].astype(f32) + dot(attT[m, :, blk(i)], wo[...], 0, 0) + shift[1]
            hm[m, blk(i)] = mid
            xhat, _ = normalise(mid)
            n = (xhat * gain1 + shift[2]).astype(bf16)
            nm[m, blk(i)] = n
            for k in range(0, FF, 256):
                a, slope = gelu_pair(dot(n, w1[:, k:k + 256], 1, 0) + fb[:, k:k + 256])
                act[m, blk(i), k:k + 256] = a.astype(bf16)
                gg[m, blk(i), k:k + 256] = slope.astype(bf16)
            out = mid + dot(act[m, blk(i)], w2[...], 1, 0) + shift[3]
            ob[m, blk(i)] = out.astype(bf16)
            if joint:
                res_copy(m, i).start()
            else:
                act_copy(m, i).start()
            return c
        lax.fori_loop(0, NB, body, 0)

    def mlp_back(m, joint):
        def body(i, c):
            if not joint:
                grad_copy(m, i).wait_recv()
            d = dy[m, blk(i)]
            parts = []
            for k in range(0, FF, 512):
                gp = (dot(d, w2[k:k + 512], 1, 1) * gg[m, blk(i), k:k + 512].astype(f32)).astype(bf16)
                gg[m, blk(i), k:k + 512] = gp
                sb[:, k:k + 512] += jnp.sum(gp.astype(f32), 0, keepdims=True)
            gn = dot(gg[m, blk(i)], w1[...], 1, 1)
            d32 = d.astype(f32)
            dv, dgain, dshift = norm_back(hm[m, blk(i)], gn, gain1)
            mid = d32 + dv
            hm[m, blk(i)] = mid
            low = mid.astype(bf16)
            gb[m, blk(i)] = low
            sm[1:2] += dgain
            sm[4:5] += dshift
            sm[5:6] += jnp.sum(d32, 0, keepdims=True)
            sm[3:4] += jnp.sum(low.astype(f32), 0, keepdims=True)
            return c
        lax.fori_loop(0, NB, body, 0)
        dOT[...] = dot(wo[...], gb[m], 1, 1).astype(bf16)

    def joint_attention_back(m):
        def body(hp, c):
            inv = jnp.concatenate([linv[m, 2 * hp], linv[m, 2 * hp + 1]], 1)
            block = dOT[blk(hp), :].astype(f32)
            d0 = (block[:HEAD] * inv[:, :R]).astype(bf16)
            d1 = (block[HEAD:] * inv[:, R:]).astype(bf16)
            zero = jnp.zeros((HEAD, R), bf16)
            d2 = jnp.concatenate([jnp.concatenate([d0, zero], 0), jnp.concatenate([zero, d1], 0)], 1)
            vcol = pl.ds(pl.multiple_of(D + hp * BLK, BLK), BLK)
            dp = dot(kv[m, :, vcol], d2, 1, 0)
            pb = jnp.concatenate([PT[2 * hp], PT[2 * hp + 1]], 1)
            p = pb.astype(f32)
            inner = jnp.sum(p * dp, 0, keepdims=True) * inv
            ds = (p * (dp - inner)).astype(bf16)
            for j in range(2):
                head = 2 * hp + j
                side = slice(j * R, (j + 1) * R)
                rows = pl.ds(pl.multiple_of(head * HEAD, HEAD), HEAD)
                vrows = pl.ds(pl.multiple_of(D + head * HEAD, HEAD), HEAD)
                kvT[m, vrows, :] = dot((d0, d1)[j], PT[head], 1, 1).astype(bf16)
                dq = dot(kvT[m, rows, :], ds[:, side], 1, 0) * SCALE
                kvT[m, rows, :] = (dot(qT[m, rows, :], ds[:, side], 1, 1) * SCALE).astype(bf16)
                qT[m, rows, :] = dq.astype(bf16)
            return c
        lax.fori_loop(0, HEADS // 2, body, 0)

    def view_attention_back(m):
        def body(hp, c):
            vrow = pl.ds(pl.multiple_of(D + hp * BLK, BLK), BLK)
            for v in range(NB):
                col = slice(v * BLK, (v + 1) * BLK)
                inv = jnp.concatenate([linv[m, 2 * hp, :, col], linv[m, 2 * hp + 1, :, col]], 1)
                d2 = (paired(dOT[blk(hp), col]).astype(f32) * inv).astype(bf16)
                dp = dot(kv[m, col, vrow], d2, 1, 0)
                pb = PT[4 * m + hp, col, 0:2 * BLK]
                p = pb.astype(f32)
                inner = jnp.sum(p * dp, 0, keepdims=True) * inv
                ds = (p * (dp - inner)).astype(bf16)
                kvT[m, vrow, col] = dot(d2, pb, 1, 1).astype(bf16)
                q2 = paired(qT[m, blk(hp), col])
                dq = dot(kvT[m, blk(hp), col], ds, 1, 0) * SCALE
                kvT[m, blk(hp), col] = (dot(q2, ds, 1, 1) * SCALE).astype(bf16)
                qT[m, blk(hp), col] = jnp.concatenate([dq[:HEAD, :BLK], dq[HEAD:, BLK:]], 0).astype(bf16)
            return c
        lax.fori_loop(0, HEADS // 2, body, 0)

    def qkv_back(m, joint):
        def body(i, c):
            gn = dot(qT[m, :, blk(i)], wq[:, :D], 0, 1) + dot(kvT[m, :, blk(i)], wq[:, D:], 0, 1)
            dv, dgain, dshift = norm_back(h[m, blk(i)].astype(f32), gn, gain0)
            sm[0:1] += dgain
            sm[2:3] += dshift
            out = (hm[m, blk(i)] + dv).astype(bf16)
            if joint:
                res_copy(m, i).wait()
            else:
                act_copy(m, i).wait_send()
            ob[m, blk(i)] = out
            if joint:
                grad_copy(m, i).start()
            else:
                res_copy(m, i).start()
            return c
        lax.fori_loop(0, NB, body, 0)
        if joint:
            gn = dot(kvT[m, :, R:KP], wq[:, D:], 0, 1)
            sm[0:1] += jnp.sum(gn * lang_xhat(m), 0, keepdims=True)
            sm[2:3] += jnp.sum(gn, 0, keepdims=True)

    def put(ref, first, count, lo, t, add):
        t = t.reshape(count, t.shape[0] // count, D)
        view = (slice(first, first + count), slice(lo, lo + t.shape[1]))
        ref[view] = (t + ref[view].astype(f32) if add else t).astype(bf16)

    deep, thin = FF // NC, D // NC

    def mlp_weights(ms, add):
        for k in range(0, FF, 512):
            t = sum(dot(act[m, :, k:k + 512], dy[m], 0, 0) for m in ms)
            put(gA, k // deep, 512 // deep, 0, t, add)
        for k in range(0, FF, 1024):
            t = sum(dot(nm[m], gg[m, :, k:k + 1024], 0, 0) for m in ms)
            for j in range(1024 // D):
                put(gA, 0, NC, deep + (k // D + j) * thin, t[:, j * D:(j + 1) * D], add)

    def attention_weights(ms, add, joint):
        t = sum(dot(attT[m], gb[m], 1, 0) for m in ms)
        put(gB, 0, NC, 3 * thin, t, add)
        t = sum(dot(nT[m, :, 0:R], qT[m], 1, 1) for m in ms)
        put(gB, 0, NC, 0, t, add)
        keys = KP if joint else R
        t = sum(dot(nT[m, :, 0:keys], kvT[m, :, 0:keys], 1, 1) for m in ms)
        put(gB, 0, NC, thin, t[:, :D], add)
        put(gB, 0, NC, 2 * thin, t[:, D:], add)

    def small_sums():
        per = gS.shape[1]
        for i in range(6 + FF // D):
            for j in range(D // BLK):
                row = i * (D // BLK) + j
                src = sm[i:i + 1, j * BLK:(j + 1) * BLK] if i < 6 else sb[:, (i - 6) * D + j * BLK:(i - 6) * D + (j + 1) * BLK]
                stage[row:row + 1] = src
        for k in range(stage.shape[0] // per):
            gS[k] = stage[k * per:(k + 1) * per].astype(bf16)

    if ring:
        (sib_send, sib_recv, hop_send, hop_recv, all_send, all_recv, pair_send, pair_recv, own_sem) = rest
        dp = lax.axis_index("dp")
        n = lax.axis_size("dp") // 2
        core = lax.rem(dp, 2)
        chip = dp // 2
        line, side = chip // 2, lax.rem(chip, 2)
        pos = jnp.where(side == 0, line, n - 1 - line)

        def at(position):
            return 2 * jnp.where(position < n // 2, 2 * position, 2 * (n - 1 - position) + 1) + core
        towards = [{"dp": at(lax.rem(pos + 1, n))}, {"dp": at(lax.rem(pos + n - 1, n))}]
        sibling = {"dp": 2 * chip + 1 - core}
        G, S, H, O = (gA, gB, gS), (sibA, sibB, sibS), (hopA, hopB, hopS), (oA, oB, oS)

        def place(d, s):
            return lax.rem(pos + n - s, n) if d == 0 else lax.rem(pos + s, n)

        def remote(src, dst, send, recv, to):
            return pltpu.make_async_remote_copy(src_ref=src, dst_ref=dst, send_sem=send, recv_sem=recv,
                                                device_id=to, device_id_type=MESH)

        def sib_copy(x, d, s):
            k = d * n + place(d, s)
            return remote(G[x].at[(1 - core) * 2 * n + k], S[x].at[k], sib_send.at[x, d, s], sib_recv.at[x, d, s], sibling)

        def hop_copy(x, d, s):
            return remote(S[x].at[d * n + place(d, s)], H[x].at[d, s], hop_send.at[x, d, s], hop_recv.at[x, d, s], towards[d])

        def home(d, s):
            return core * 2 * n + d * n + place(d, s)

        def all_copy(x, d, s):
            k = place(d, n - 1) if s is None else place(d, s)
            index = core * 2 * n + d * n + k
            src = S[x].at[d * n + k] if s is None else O[x].at[index]
            t = 0 if s is None else s + 1
            return remote(src, O[x].at[index], all_send.at[x, d, t], all_recv.at[x, d, t], towards[d])

        def pair_copy(x, d, s):
            k = place(d, n - 1) if s is None else place(d, s)
            index = core * 2 * n + d * n + k
            src = S[x].at[d * n + k] if s is None else O[x].at[index]
            t = 0 if s is None else s + 1
            return remote(src, O[x].at[index], pair_send.at[x, d, t], pair_recv.at[x, d, t], sibling)

        def own_copy(x, d):
            k = place(d, n - 1)
            return pltpu.make_async_copy(S[x].at[d * n + k], O[x].at[core * 2 * n + d * n + k], own_sem.at[x, d])

        def exchange(xs):
            def body(s, c):
                for x in xs:
                    for d in range(2):
                        sib_copy(x, d, s).start()
                return c
            lax.fori_loop(0, n, body, 0)

        def reduce_step(xs, s, first=False, last=False):
            for d in range(2):
                for x in xs:
                    k = place(d, s)
                    sib_copy(x, d, s).wait_recv()
                    total = G[x][home(d, s)].astype(f32) + S[x][d * n + k].astype(f32)
                    if not first:
                        hop_copy(x, d, s - 1).wait_recv()
                        total = total + H[x][d, s - 1].astype(f32)
                    S[x][d * n + k] = total.astype(bf16)
                    if last:
                        all_copy(x, d, None).start()
                        pair_copy(x, d, None).start()
                        own_copy(x, d).start()
                    else:
                        hop_copy(x, d, s).start()

        def gather_step(xs, s, last=False):
            for d in range(2):
                for x in xs:
                    all_arrival(x, d, s).wait_recv()
                    if not last:
                        all_copy(x, d, s).start()
                    pair_copy(x, d, s).start()

        def all_arrival(x, d, s):
            index = core * 2 * n + d * n + place(d, s)
            return remote(O[x].at[index], O[x].at[index], all_send.at[x, d, s], all_recv.at[x, d, s], towards[d])

        def settle():
            for x in range(3):
                for d in range(2):
                    own_copy(x, d).wait()
                    all_copy(x, d, None).wait_send()
                    pair_copy(x, d, None).wait()

                    def body(s, c):
                        sib_copy(x, d, s).wait_send()
                        return c
                    lax.fori_loop(0, n, body, 0)

                    def body(s, c):
                        hop_copy(x, d, s).wait_send()
                        pair_copy(x, d, s).wait()
                        return c
                    lax.fori_loop(0, n - 1, body, 0)

                    def body(s, c):
                        all_copy(x, d, s).wait_send()
                        return c
                    lax.fori_loop(0, n - 2, body, 0)

    barrier = pltpu.get_barrier_semaphore()
    greeted = [peer] + ([sibling] + towards if ring else [])
    for device in greeted:
        pl.semaphore_signal(barrier, inc=1, device_id=device, device_id_type=MESH)
    pl.semaphore_wait(barrier, len(greeted))
    sm[...] = jnp.zeros_like(sm)
    sb[...] = jnp.zeros_like(sb)

    @pl.when(sec == 0)
    def _():
        for m in range(micro):
            in_copy(m, h).start()
            if m == 0:
                for k in range(4):
                    w_copy(k).start()

        def forward(m, c):
            in_copy(m, h).wait()

            @pl.when(m == 0)
            def _():
                w_copy(0).wait()
            qkv_phase(m, False)
            view_attention(m)

            @pl.when(m == 0)
            def _():
                for k in range(1, 4):
                    w_copy(k).wait()
            mlp_phase(m, False)
            return c
        lax.fori_loop(0, micro, forward, 0)

        def backward(m, add):
            mlp_back(m, False)
            mlp_weights([m], add)
            view_attention_back(m)
            qkv_back(m, False)
            attention_weights([m], add, False)
        for m in range(micro):
            backward(m, m > 0)
        for m in range(micro):
            for i in range(NB):
                res_copy(m, i).wait()

    @pl.when(sec == 1)
    def _():
        for k in range(4):
            w_copy(k).start()
        for m in range(micro):
            in_copy(m, dy).start()
        for k in range(4):
            w_copy(k).wait()
        for m in range(micro):
            in_copy(m, dy).wait()

        def languages(m, c):
            lang_phase(m)
            return c
        lax.fori_loop(0, micro, languages, 0)

        def item(m, c):
            qkv_phase(m, True)
            joint_attention(m)
            mlp_phase(m, True)
            mlp_back(m, True)
            joint_attention_back(m)
            qkv_back(m, True)
            return c
        lax.fori_loop(0, micro, item, 0)
        mlp_weights(range(micro), False)
        attention_weights(range(micro), False, True)
        for m in range(micro):
            for i in range(NB):
                grad_copy(m, i).wait_send()

    small_sums()
    if ring:
        exchange((0,))
        exchange((1, 2))
        both = (0, 1, 2)
        reduce_step(both, 0, first=True)

        def body(s, c):
            reduce_step(both, s)
            return c
        lax.fori_loop(1, n - 1, body, 0)
        reduce_step(both, n - 1, last=True)

        def body(s, c):
            gather_step(both, s)
            return c
        lax.fori_loop(0, n - 2, body, 0)
        gather_step(both, n - 2, last=True)
        settle()
    else:
        copies = [pltpu.make_async_copy(s, d, out_sem.at[k]) for k, (s, d) in enumerate(
            ((gA, oA), (gB, oB), (gS, oS)))]
        for copy in copies:
            copy.start()
        for copy in copies:
            copy.wait()


def local(section_data, lang_feat, lang_ids, view_mask, norm_gains, shifts, fc1_bias, w_qkv, w_out, w_fc1, w_fc2):
    micro, rows, D = section_data.shape[1], section_data.shape[3], section_data.shape[4]
    FF = w_fc1.shape[2]
    lang = lang_feat.shape[2]
    KP = rows + -(-lang // 16) * 16
    NB = rows // BLK
    hbm = pl.BlockSpec(memory_space=pl.ANY)
    vmem = pl.BlockSpec(memory_space=pltpu.VMEM)
    smem = pl.BlockSpec(memory_space=pltpu.SMEM)
    V = pltpu.VMEM
    dma = pltpu.SemaphoreType.DMA
    sds = jax.ShapeDtypeStruct
    n = lax.axis_size("dp") // 2
    ring = lax.axis_size("dp") % 4 == 0 and n >= 4 and D % (4 * n * 16) == 0
    NC = 4 * n if ring else 32
    packed = ((NC, (FF // NC) + FF // D * (D // NC), D), (NC, 4 * (D // NC), D), (NC, 16, BLK))
    scratch = [
        V((micro, rows, D), bf16),
        V((micro, rows, D), bf16),
        V((D, 3 * D), bf16), V((D, D), bf16), V((D, FF), bf16), V((FF, D), bf16),
        V((micro, D, KP), bf16),
        V((micro, D, rows), bf16),
        V((micro, 2 * D, KP), bf16),
        V((micro, KP, 2 * D), bf16),
        V((HEADS, KP, rows), bf16),
        V((micro, HEADS, 1, rows), f32),
        V((micro, D, rows), bf16),
        V((micro, rows, D), f32),
        V((micro, rows, D), bf16),
        V((micro, rows, FF), bf16),
        V((micro, rows, FF), bf16),
        V((micro, rows, D), bf16),
        V((D, rows), bf16),
        V((micro, rows, D), bf16),
        V((micro, KP, BLK), f32),
        V((8, D), f32), V((1, FF), f32), V((-(-(6 * D + FF) // (16 * BLK)) * 16, BLK), f32),
        V(packed[0], bf16), V(packed[1], bf16), V(packed[2], bf16),
    ]
    if ring:
        scratch += [V((2 * n,) + shape[1:], bf16) for shape in packed]
        scratch += [V((2, n - 1) + shape[1:], bf16) for shape in packed]
    scratch += [dma((micro,)), dma((4,)), dma((micro, NB)),
                dma((micro, NB)), dma((micro, NB)), dma((micro, NB)), dma((micro, NB)), dma((3,))]
    if ring:
        scratch += [dma((3, 2, n))] * 8 + [dma((3, 2))]
    res, gA, gB, gS = pl.pallas_call(
        step_kernel,
        out_shape=(sds(section_data.shape, bf16),) + tuple(sds(shape, bf16) for shape in packed),
        in_specs=[hbm, vmem, vmem, smem, vmem, vmem, vmem, hbm, hbm, hbm, hbm],
        out_specs=(hbm, hbm, hbm, hbm),
        scratch_shapes=scratch,
        compiler_params=pltpu.CompilerParams(
            collective_id=0, has_side_effects=True, vmem_limit_bytes=VMEM_LIMIT),
        name="two_layers",
    )(section_data, lang_feat, lang_ids, view_mask, norm_gains, shifts, fc1_bias, w_qkv, w_out, w_fc1, w_fc2)
    if not ring:
        gA, gB, gS = lax.psum((gA, gB, gS), "dp")
    return (res,) + unpack(gA, gB, gS, D, FF)


def unpack_kernel(a, b, s, gain, shift, b1, gq, go, g1, g2):
    group = a.shape[0]
    D = go.shape[2]
    FF = g1.shape[2]
    thin, deep = go.shape[1] // group, g2.shape[1] // group
    for c in range(group):
        row = slice(c * thin, (c + 1) * thin)
        g2[0, c * deep:(c + 1) * deep] = a[c, 0:deep].astype(f32)
        for j in range(FF // D):
            g1[0, row, j * D:(j + 1) * D] = a[c, deep + j * thin:deep + (j + 1) * thin].astype(f32)
        for j in range(3):
            gq[0, row, j * D:(j + 1) * D] = b[c, j * thin:(j + 1) * thin].astype(f32)
        go[0, row] = b[c, 3 * thin:4 * thin].astype(f32)

    @pl.when(pl.program_id(0) == 0)
    def _():
        width = D // BLK
        for i in range(6 + FF // D):
            for j in range(width):
                at = i * width + j
                part = s[at // 16, at % 16:at % 16 + 1].astype(f32)
                if i < 2:
                    gain[0, i:i + 1, j * BLK:(j + 1) * BLK] = part
                elif i < 6:
                    shift[0, i - 2:i - 1, j * BLK:(j + 1) * BLK] = part
                else:
                    b1[0:1, (i - 6) * D + j * BLK:(i - 6) * D + (j + 1) * BLK] = part


def unpack(gA, gB, gS, D, FF):
    NC = gA.shape[0]
    group = NC // 8
    sds = jax.ShapeDtypeStruct

    def per_group(shape):
        return pl.BlockSpec((group,) + shape[1:], lambda i: (i,) + (0,) * (len(shape) - 1))

    def rows(total, width):
        return pl.BlockSpec((1, total // 8, width), lambda i: (0, i, 0))

    def once(*shape):
        return pl.BlockSpec(shape, lambda i: (0,) * len(shape))
    return pl.pallas_call(
        unpack_kernel,
        grid=(8,),
        in_specs=[per_group(gA.shape), per_group(gB.shape), once(*gS.shape)],
        out_specs=(once(1, 2, D), once(1, 4, D), once(1, FF), rows(D, 3 * D), rows(D, D), rows(D, FF), rows(FF, D)),
        out_shape=(sds((1, 2, D), f32), sds((1, 4, D), f32), sds((1, FF), f32), sds((1, D, 3 * D), f32),
                   sds((1, D, D), f32), sds((1, D, FF), f32), sds((1, FF, D), f32)),
        compiler_params=pltpu.CompilerParams(vmem_limit_bytes=VMEM_LIMIT),
        name="unpack",
    )(gA, gB, gS)


def solution(mesh):
    weights = P("section", None, None)
    rows = P("section", None, "dp", None, None)
    return jax.shard_map(
        local,
        mesh=mesh,
        in_specs=(rows, P(None, "dp", None, None), P(None, "dp", None), P(None, "dp", None), weights, weights,
                  P("section", None), weights, weights, weights, weights),
        out_specs=(rows, weights, weights, P("section", None), weights, weights, weights, weights),
        check_vma=False,
    )
```

```python
import functools

import jax
import jax.numpy as jnp
from jax import lax
from jax.experimental import pallas as pl
from jax.experimental.pallas import tpu as pltpu
from jax.sharding import PartitionSpec as P

HEADS = 8
HEAD = 64
VIEWS = 5
BLK = 128
EPS = 1e-05
MASKED = -1e30
SCALE = HEAD**-0.5
LOG2E = 1.4426950408889634
MESH = pl.DeviceIdType.MESH
bf16 = jnp.bfloat16
f32 = jnp.float32
VMEM_LIMIT = 64 * 2**20 - 2**19
SMALL = 6
AFTER_DOWN = (1,)
AFTER_BLOCK = ()
AFTER_UP = (11,)
AFTER_GRAD = ()
AFTER_HALF = (2, 21)
AFTER_VIEWS = (12, 3)
AFTER_QKV = (31, 13, 22, 4)
BEFORE = AFTER_DOWN + AFTER_BLOCK + AFTER_UP + AFTER_GRAD + AFTER_HALF + AFTER_VIEWS + AFTER_QKV
REST = (14, 61, 41, 32, 51, 23, 5, 62, 33, 24, 42, 6, 15, 34, 25, 52, 43, 35, 16, 44, 63, 26, 7, 45, 64, 53, 36, 54, 65, 27, 46, 55, 66, 56, 67, 37, 17, 8, 47, 28, 48, 18, 68, 57, 38, 58)


def dot(a, b, ca, cb):
    return lax.dot_general(a, b, (((ca,), (cb,)), ((), ())), preferred_element_type=f32)


def normalise(v):
    centred = v - jnp.mean(v, -1, keepdims=True)
    r = lax.rsqrt(jnp.mean(centred * centred, -1, keepdims=True) + EPS)
    return centred * r, r


def norm_back(v, grad, gain):
    xhat, r = normalise(v)
    gm = grad * gain
    along = jnp.mean(gm * xhat, -1, keepdims=True)
    dv = r * (gm - jnp.mean(gm, -1, keepdims=True) - xhat * along)
    return dv, jnp.sum(grad * xhat, 0, keepdims=True), jnp.sum(grad, 0, keepdims=True)


def gelu_pair(x):
    phi = 0.5 * (1.0 + lax.erf(x * 0.7071067811865476))
    density = jnp.exp2(x * x * (-0.5 * LOG2E)) * 0.3989422804014327
    return x * phi, phi + x * density


def blk(i):
    return pl.ds(pl.multiple_of(i * BLK, BLK), BLK)


def step_kernel(sd, lf, ids, vm, ng, sh, fb, wq_h, wo_h, w1_h, w2_h,
                res, O, OS,
                h, dy, wq, wo, w1, w2, nT, qT, kvT, kv, PT, linv, attT, hm, nm, act, gg, gb, dOT, ob,
                bias, lx, sm, sb, G, GS, *rest):
    tree = len(rest) > 8
    if tree:
        V, VS, rest = rest[0], rest[1], rest[2:]
    (in_sem, w_sem, res_sem, act_send, act_recv, grad_send, grad_recv, out_sem), rest = rest[:8], rest[8:]
    sec = lax.axis_index("section")
    D = wo.shape[0]
    FF = w1.shape[1]
    R = h.shape[1]
    NB = R // BLK
    LROWS = lf.shape[1]
    KP = kvT.shape[2]
    LP = KP - R
    micro = h.shape[0]
    peer = {"section": 1 - sec}

    def w_copy(k):
        src, dst = ((wq_h, wq), (wo_h, wo), (w1_h, w1), (w2_h, w2))[k]
        return pltpu.make_async_copy(src.at[0], dst, w_sem.at[k])

    def in_copy(m, dst):
        return pltpu.make_async_copy(sd.at[0, m, 0], dst.at[m], in_sem.at[m])

    def res_copy(m):
        return pltpu.make_async_copy(ob.at[m], res.at[0, m, 0], res_sem.at[m])

    def act_copy(m, i):
        return pltpu.make_async_remote_copy(
            src_ref=ob.at[m, blk(i)], dst_ref=h.at[m, blk(i)], send_sem=act_send.at[m, i],
            recv_sem=act_recv.at[m, i], device_id=peer, device_id_type=MESH)

    def grad_copy(m, i):
        return pltpu.make_async_remote_copy(
            src_ref=ob.at[m, blk(i)], dst_ref=dy.at[m, blk(i)], send_sem=grad_send.at[m, i],
            recv_sem=grad_recv.at[m, i], device_id=peer, device_id_type=MESH)

    gain0, gain1 = ng[0, 0:1], ng[0, 1:2]
    shift = [sh[0, k:k + 1] for k in range(4)]

    def qkv_block(m, i):
        xhat, _ = normalise(h[m, blk(i)].astype(f32))
        n = (xhat * gain0 + shift[0]).astype(bf16)
        nT[m, :, blk(i)] = n.T
        rows = dot(n, wq[...], 1, 0).astype(bf16)
        qT[m, :, blk(i)] = rows[:, :D].T
        kvT[m, :, blk(i)] = rows[:, D:].T
        kv[m, blk(i), :] = rows[:, D:]

    def joint_qkv(m):
        def body(i, c):
            act_copy(m, i).wait_recv()
            qkv_block(m, i)
            return c
        lax.fori_loop(0, NB, body, 0, unroll=True)

    def lang_phase(m):
        rows = jnp.concatenate([lf[0].astype(f32)[:, m, :], jnp.zeros((LP - LROWS, D), f32)], 0)
        xhat, _ = normalise(rows)
        lx[m] = xhat
        n = (xhat * gain0 + shift[0]).astype(bf16)
        nT[m, :, R:KP] = n.T
        rows = dot(n, wq[:, D:], 1, 0).astype(bf16)
        kvT[m, :, R:KP] = rows.T
        kv[m, R:KP, :] = rows
        for v in range(VIEWS):
            seen = (vm[m, 0, v] > 0).astype(f32)
            bias[m, v * BLK:(v + 1) * BLK, :] = jnp.full((BLK, BLK), MASKED, f32) * (1.0 - seen)
        count = jnp.sum((ids[m] != 0).astype(jnp.int32), -1, keepdims=True)
        place = lax.broadcasted_iota(jnp.int32, (LP, BLK), 0)
        bias[m, R:KP, :] = jnp.where(place < count, 0.0, MASKED)

    def paired(block):
        zero = jnp.zeros((HEAD, block.shape[1]), block.dtype)
        return jnp.concatenate([jnp.concatenate([block[:HEAD], zero], 0),
                                jnp.concatenate([zero, block[HEAD:]], 0)], 1)

    def joint_attention(m):
        def body(hp, c):
            q2 = paired(qT[m, blk(hp), :])
            s = dot(kv[m, :, blk(hp)], q2, 1, 0)
            s = s + jnp.concatenate([bias[m]] * (2 * NB), 1)
            top = jnp.max(s, 0, keepdims=True) * (SCALE * LOG2E)
            p = jnp.exp2(s * (SCALE * LOG2E) - top)
            inv = 1.0 / jnp.sum(p, 0, keepdims=True)
            pb = p.astype(bf16)
            for j in range(2):
                head = 2 * hp + j
                PT[head] = pb[:, j * R:(j + 1) * R]
                linv[m, head] = inv[:, j * R:(j + 1) * R]
                rows = pl.ds(pl.multiple_of(head * HEAD, HEAD), HEAD)
                vT = kvT[m, pl.ds(pl.multiple_of(D + head * HEAD, HEAD), HEAD), :]
                out = dot(vT, pb[:, j * R:(j + 1) * R], 1, 0) * inv[:, j * R:(j + 1) * R]
                attT[m, rows, :] = out.astype(bf16)
            return c
        lax.fori_loop(0, HEADS // 2, body, 0)

    def view_attention(m, v):
        col = blk(v)
        for hp in range(HEADS // 2):
            pair = slice(hp * BLK, (hp + 1) * BLK)
            q2 = paired(qT[m, pair, col])
            s = dot(kv[m, col, pair], q2, 1, 0)
            top = jnp.max(s, 0, keepdims=True) * (SCALE * LOG2E)
            p = jnp.exp2(s * (SCALE * LOG2E) - top)
            inv = 1.0 / jnp.sum(p, 0, keepdims=True)
            pb = p.astype(bf16)
            PT[4 * m + hp, col, 0:2 * BLK] = pb
            for j in range(2):
                linv[m, 2 * hp + j, :, col] = inv[:, j * BLK:(j + 1) * BLK]
            out = dot(kvT[m, D + hp * BLK:D + (hp + 1) * BLK, col], pb, 1, 0) * inv
            attT[m, pair, col] = jnp.concatenate([out[:HEAD, :BLK], out[HEAD:, BLK:]], 0).astype(bf16)

    def mlp_block(m, i):
        mid = h[m, blk(i)].astype(f32) + dot(attT[m, :, blk(i)], wo[...], 0, 0) + shift[1]
        hm[m, blk(i)] = mid
        xhat, _ = normalise(mid)
        n = (xhat * gain1 + shift[2]).astype(bf16)
        nm[m, blk(i)] = n
        for k in range(0, FF, 256):
            a, slope = gelu_pair(dot(n, w1[:, k:k + 256], 1, 0) + fb[:, k:k + 256])
            act[m, blk(i), k:k + 256] = a.astype(bf16)
            gg[m, blk(i), k:k + 256] = slope.astype(bf16)
        out = mid + dot(act[m, blk(i)], w2[...], 1, 0) + shift[3]
        ob[m, blk(i)] = out.astype(bf16)

    def joint_mlp(m):
        hm[m] = h[m].astype(f32) + dot(attT[m], wo[...], 0, 0) + shift[1]
        for i in range(NB):
            row = slice(i * BLK, (i + 1) * BLK)
            xhat, _ = normalise(hm[m, row])
            nm[m, row] = (xhat * gain1 + shift[2]).astype(bf16)
        for k in range(0, FF, 256):
            a, slope = gelu_pair(dot(nm[m], w1[:, k:k + 256], 1, 0) + fb[:, k:k + 256])
            act[m, :, k:k + 256] = a.astype(bf16)
            gg[m, :, k:k + 256] = slope.astype(bf16)
        ob[m] = (hm[m] + dot(act[m], w2[...], 1, 0) + shift[3]).astype(bf16)
        res_copy(m).start()

    def mid_back(m, row, gn):
        dv, dgain, dshift = norm_back(hm[m, row], gn, gain1)
        d32 = dy[m, row].astype(f32)
        mid = d32 + dv
        hm[m, row] = mid
        low = mid.astype(bf16)
        gb[m, row] = low
        sm[1:2] += dgain
        sm[4:5] += dshift
        sm[5:6] += jnp.sum(d32, 0, keepdims=True)
        sm[3:4] += jnp.sum(low.astype(f32), 0, keepdims=True)

    def pre_back(m, row, width):
        d = dy[m, row]
        for k in range(0, FF, width):
            gp = (dot(d, w2[k:k + width], 1, 1) * gg[m, row, k:k + width].astype(f32)).astype(bf16)
            gg[m, row, k:k + width] = gp
            sb[:, k:k + width] += jnp.sum(gp.astype(f32), 0, keepdims=True)

    def mlp_back_block(m, i):
        pre_back(m, blk(i), 512)
        mid_back(m, blk(i), dot(gg[m, blk(i)], w1[...], 1, 1))

    def joint_mlp_back(m):
        pre_back(m, slice(0, R), 256)
        gn = dot(gg[m], w1[...], 1, 1)
        for i in range(NB):
            row = slice(i * BLK, (i + 1) * BLK)
            mid_back(m, row, gn[row])

    def att_grad(m):
        dOT[...] = dot(wo[...], gb[m], 1, 1).astype(bf16)

    def joint_attention_back(m):
        def body(hp, c):
            inv = jnp.concatenate([linv[m, 2 * hp], linv[m, 2 * hp + 1]], 1)
            block = dOT[blk(hp), :].astype(f32)
            d0 = (block[:HEAD] * inv[:, :R]).astype(bf16)
            d1 = (block[HEAD:] * inv[:, R:]).astype(bf16)
            zero = jnp.zeros((HEAD, R), bf16)
            d2 = jnp.concatenate([jnp.concatenate([d0, zero], 0), jnp.concatenate([zero, d1], 0)], 1)
            vcol = pl.ds(pl.multiple_of(D + hp * BLK, BLK), BLK)
            dp = dot(kv[m, :, vcol], d2, 1, 0)
            pb = jnp.concatenate([PT[2 * hp], PT[2 * hp + 1]], 1)
            p = pb.astype(f32)
            inner = jnp.sum(p * dp, 0, keepdims=True) * inv
            ds = (p * (dp - inner)).astype(bf16)
            for j in range(2):
                head = 2 * hp + j
                side = slice(j * R, (j + 1) * R)
                rows = pl.ds(pl.multiple_of(head * HEAD, HEAD), HEAD)
                vrows = pl.ds(pl.multiple_of(D + head * HEAD, HEAD), HEAD)
                kvT[m, vrows, :] = dot((d0, d1)[j], PT[head], 1, 1).astype(bf16)
                dq = dot(kvT[m, rows, :], ds[:, side], 1, 0) * SCALE
                kvT[m, rows, :] = (dot(qT[m, rows, :], ds[:, side], 1, 1) * SCALE).astype(bf16)
                qT[m, rows, :] = dq.astype(bf16)
            return c
        lax.fori_loop(0, HEADS // 2, body, 0)

    def view_attention_back(m, first, last):
        def body(hp, c):
            vrow = pl.ds(pl.multiple_of(D + hp * BLK, BLK), BLK)
            pair = blk(hp)
            for v in range(NB):
                col = slice(v * BLK, (v + 1) * BLK)
                inv = jnp.concatenate([linv[m, 2 * hp, :, col], linv[m, 2 * hp + 1, :, col]], 1)
                d2 = (paired(dOT[pair, col]).astype(f32) * inv).astype(bf16)
                dp = dot(kv[m, col, vrow], d2, 1, 0)
                pb = PT[4 * m + hp, col, 0:2 * BLK]
                p = pb.astype(f32)
                inner = jnp.sum(p * dp, 0, keepdims=True) * inv
                ds = (p * (dp - inner)).astype(bf16)
                q2 = paired(qT[m, pair, col])
                dv = dot(d2, pb, 1, 1).astype(bf16)
                dq = dot(kvT[m, pair, col], ds, 1, 0) * SCALE
                dk = (dot(q2, ds, 1, 1) * SCALE).astype(bf16)
                kvT[m, vrow, col] = dv
                kvT[m, pair, col] = dk
                qT[m, pair, col] = jnp.concatenate([dq[:HEAD, :BLK], dq[HEAD:, BLK:]], 0).astype(bf16)
            return c
        lax.fori_loop(first, last, body, 0)

    def qkv_back(m, joint):
        gn = dot(qT[m], wq[:, :D], 0, 1) + dot(kvT[m, :, 0:R], wq[:, D:], 0, 1)
        if joint:
            res_copy(m).wait()
        for i in range(NB):
            row = slice(i * BLK, (i + 1) * BLK)
            dv, dgain, dshift = norm_back(h[m, row].astype(f32), gn[row], gain0)
            sm[0:1] += dgain
            sm[2:3] += dshift
            ob[m, row] = (hm[m, row] + dv).astype(bf16)
            if joint:
                grad_copy(m, i).start()
        if joint:
            gn = dot(kvT[m, :, R:KP], wq[:, D:], 0, 1)
            sm[0:1] += jnp.sum(gn * lx[m], 0, keepdims=True)
            sm[2:3] += jnp.sum(gn, 0, keepdims=True)
        else:
            res_copy(m).start()

    UP, QKV, OUT = FF // D, 2 * (FF // D), 2 * (FF // D) + 3

    def cols(k):
        return pl.ds(pl.multiple_of(k * D, D), D)

    def put(u, t):
        G[u] = (G[u].astype(f32) + t).astype(bf16)

    def down_weights(ms, unroll=1):
        def body(k, c):
            put(k, sum(dot(act[m, :, cols(k)], dy[m], 0, 0) for m in ms))
            return c
        lax.fori_loop(0, FF // D, body, 0, unroll=unroll)

    def up_weights(ms, unroll=1):
        def body(k, c):
            put(UP + k, sum(dot(nm[m], gg[m, :, cols(k)], 0, 0) for m in ms))
            return c
        lax.fori_loop(0, FF // D, body, 0, unroll=unroll)

    def attention_weights(ms, joint):
        keys = KP if joint else R
        put(QKV, sum(dot(nT[m, :, 0:R], qT[m], 1, 1) for m in ms))

        def body(k, c):
            put(QKV + 1 + k, sum(dot(nT[m, :, 0:keys], kvT[m, cols(k), 0:keys], 1, 1) for m in ms))
            return c
        lax.fori_loop(0, 2, body, 0)
        put(OUT, sum(dot(attT[m], gb[m], 1, 0) for m in ms))

    def small_sums():
        rows = [sm[i:i + 1] for i in range(6)] + [sb[:, k * D:(k + 1) * D] for k in range(FF // D)]
        GS[...] = jnp.zeros_like(GS)
        parts = [row[:, j * BLK:(j + 1) * BLK] for row in rows for j in range(D // BLK)]
        parts += [jnp.zeros((1, BLK), f32)] * (-len(parts) % 16)
        GS[0:len(parts)] = jnp.concatenate(parts, 0).astype(bf16)

    units = OUT + 1
    if tree:
        (t_send, t_recv, o_sem) = rest
        dp = lax.axis_index("dp")
        bits = lax.axis_size("dp").bit_length() - 1
        bit = [lax.rem(dp // (1 << k), 2) for k in range(bits)]
        partner = [{"dp": dp + (1 - 2 * bit[k]) * (1 << k)} for k in range(bits)]

        def refs(u):
            return (GS, VS, OS) if u is None else (G.at[u], V.at[u], O.at[u])

        def offset(rows, k):
            return sum((bit[j] * (rows >> (j + 1)) for j in range(k + 1)), 0)

        def tree_copy(u, k):
            g, v, o = refs(u)
            rows = g.shape[0]
            x = units if u is None else u
            if k < bits:
                size = rows >> (k + 1)
                src = g.at[pl.ds(pl.multiple_of(offset(rows, k - 1) + (1 - bit[k]) * size, 16), size)]
                dst = v.at[pl.ds(rows - (rows >> k), size)]
                to = partner[k]
            else:
                j = 2 * bits - 1 - k
                size = rows >> (j + 1)
                part = pl.ds(pl.multiple_of(offset(rows, j), 16), size)
                src, dst = (g if k == bits else o).at[part], o.at[part]
                to = partner[j]
            return pltpu.make_async_remote_copy(src_ref=src, dst_ref=dst, send_sem=t_send.at[x, k],
                                                recv_sem=t_recv.at[x, k], device_id=to, device_id_type=MESH)

        def own_copy(u):
            g, _, o = refs(u)
            rows = g.shape[0]
            part = pl.ds(pl.multiple_of(offset(rows, bits - 1), 16), rows >> bits)
            return pltpu.make_async_copy(g.at[part], o.at[part], o_sem.at[units if u is None else u])

        def event(u, k):
            g, v, _ = refs(u)
            rows = g.shape[0]
            if k > 0:
                tree_copy(u, k - 1).wait_recv()
            if 0 < k <= bits:
                size = rows >> k
                step = min(size, 32)
                first = offset(rows, k - 1)

                def add(i, c):
                    mine = pl.ds(pl.multiple_of(first + i * step, 16), step)
                    theirs = pl.ds(pl.multiple_of(rows - (rows >> (k - 1)) + i * step, 16), step)
                    g[mine, :] = (g[mine, :].astype(f32) + v[theirs, :].astype(f32)).astype(bf16)
                    return c
                lax.fori_loop(0, size // step, add, 0)
            if k == bits:
                own_copy(u).start()
            elif k == bits + 1:
                own_copy(u).wait()
            if k < 2 * bits:
                tree_copy(u, k).start()

        def settle():
            def body(u, c):
                for k in range(2 * bits):
                    tree_copy(u, k).wait_send()
                return c
            lax.fori_loop(0, units, body, 0)
            for k in range(2 * bits):
                tree_copy(None, k).wait_send()

    def group(first, count, k):
        if tree:
            def body(u, c):
                event(u, k)
                return c
            lax.fori_loop(first, first + count, body, 0)

    def run(tokens):
        for token in tokens:
            g, k = token // 10, token % 10
            if not tree:
                continue
            if g == SMALL:
                event(None, k)
            else:
                group(2 * g, 2, k)

    @pl.when(sec == 0)
    def _():
        for m in range(micro):
            in_copy(m, h).start()
            if m == 0:
                for k in range(4):
                    w_copy(k).start()

    @pl.when(sec == 1)
    def _():
        for k in range(4):
            w_copy(k).start()
        for m in range(micro):
            in_copy(m, dy).start()

    barrier = pltpu.get_barrier_semaphore()
    greeted = [peer] + (partner if tree else [])
    for device in greeted:
        pl.semaphore_signal(barrier, inc=1, device_id=device, device_id_type=MESH)
    sm[...] = jnp.zeros_like(sm)
    sb[...] = jnp.zeros_like(sb)
    pl.semaphore_wait(barrier, len(greeted))

    @pl.when(sec == 0)
    def _():
        def forward(m, c):
            in_copy(m, h).wait()

            @pl.when(m == 0)
            def _():
                for k in range(4):
                    w_copy(k).wait()

            def view(i, c):
                qkv_block(m, i)
                view_attention(m, i)
                mlp_block(m, i)

                @pl.when((m > 0) & (i == 0))
                def _():
                    for j in range(NB):
                        act_copy(m - 1, j).wait_send()
                act_copy(m, i).start()
                return c
            lax.fori_loop(0, NB, view, 0)
            return c
        lax.fori_loop(0, micro, forward, 0)
        for j in range(NB):
            act_copy(micro - 1, j).wait_send()

        G[...] = jnp.zeros_like(G)

        def backward(m, c):
            final = m == micro - 1

            def when_final(tokens, first=None):
                if tree:
                    @pl.when(final)
                    def _():
                        if first is not None:
                            group(first, 4, 0)
                        run(tokens)

            def body(i, c):
                grad_copy(m, i).wait_recv()

                @pl.when(i == NB - 1)
                def _():
                    down_weights([m], 2)
                    when_final(AFTER_DOWN, 0)
                mlp_back_block(m, i)
                return c
            lax.fori_loop(0, NB, body, 0)
            when_final(AFTER_BLOCK)
            up_weights([m])
            when_final(AFTER_UP, UP)
            att_grad(m)
            when_final(AFTER_GRAD)
            view_attention_back(m, 0, 2)
            when_final(AFTER_HALF)
            view_attention_back(m, 2, 4)
            when_final(AFTER_VIEWS)
            qkv_back(m, False)
            when_final(AFTER_QKV)
            attention_weights([m], False)
            return c
        lax.fori_loop(0, micro, backward, 0)

    @pl.when(sec == 1)
    def _():
        for k in range(4):
            w_copy(k).wait()
        for m in range(micro):
            in_copy(m, dy).wait()
        for m in range(micro):
            lang_phase(m)

        def item(m, c):
            joint_qkv(m)
            joint_attention(m)
            joint_mlp(m)
            joint_mlp_back(m)
            att_grad(m)
            joint_attention_back(m)
            qkv_back(m, True)
            return c
        lax.fori_loop(0, micro, item, 0)
        G[...] = jnp.zeros_like(G)
        down_weights(range(micro))
        group(0, 4, 0)
        up_weights(range(micro))
        group(UP, 4, 0)
        run(BEFORE)
        attention_weights(range(micro), True)

    small_sums()
    if tree:
        group(QKV, 4, 0)
        event(None, 0)
        run(REST)
        settle()
    else:
        copies = [pltpu.make_async_copy(G, O, out_sem.at[0]), pltpu.make_async_copy(GS, OS, out_sem.at[1])]
        for copy in copies:
            copy.start()
        for copy in copies:
            copy.wait()

    @pl.when(sec == 0)
    def _():
        for m in range(micro):
            res_copy(m).wait()

    @pl.when(sec == 1)
    def _():
        for m in range(micro):
            for i in range(NB):
                grad_copy(m, i).wait_send()


def local(section_data, lang_feat, lang_ids, view_mask, norm_gains, shifts, fc1_bias, w_qkv, w_out, w_fc1, w_fc2):
    micro, rows, D = section_data.shape[1], section_data.shape[3], section_data.shape[4]
    FF = w_fc1.shape[2]
    lang = lang_feat.shape[2]
    lang_rows = jnp.transpose(lang_feat, (1, 2, 0, 3))
    KP = rows + -(-lang // 16) * 16
    NB = rows // BLK
    hbm = pl.BlockSpec(memory_space=pl.ANY)
    vmem = pl.BlockSpec(memory_space=pltpu.VMEM)
    smem = pl.BlockSpec(memory_space=pltpu.SMEM)
    V = pltpu.VMEM
    dma = pltpu.SemaphoreType.DMA
    sds = jax.ShapeDtypeStruct
    tree = lax.axis_size("dp") == 16 and D % 256 == 0
    units = 2 * (FF // D) + 4
    packed = ((units, D, D), (256, BLK))
    scratch = [
        V((micro, rows, D), bf16),
        V((micro, rows, D), bf16),
        V((D, 3 * D), bf16), V((D, D), bf16), V((D, FF), bf16), V((FF, D), bf16),
        V((micro, D, KP), bf16),
        V((micro, D, rows), bf16),
        V((micro, 2 * D, KP), bf16),
        V((micro, KP, 2 * D), bf16),
        V((HEADS, KP, rows), bf16),
        V((micro, HEADS, 1, rows), f32),
        V((micro, D, rows), bf16),
        V((micro, rows, D), f32),
        V((micro, rows, D), bf16),
        V((micro, rows, FF), bf16),
        V((micro, rows, FF), bf16),
        V((micro, rows, D), bf16),
        V((D, rows), bf16),
        V((micro, rows, D), bf16),
        V((micro, KP, BLK), f32),
        V((micro, KP - rows, D), f32),
        V((8, D), f32), V((1, FF), f32),
    ] + [V(shape, bf16) for shape in packed]
    if tree:
        scratch += [V((units, D - D // 16, D), bf16), V((256 - 16, BLK), bf16)]
    scratch += [dma((micro,)), dma((4,)), dma((micro,)),
                dma((micro, NB)), dma((micro, NB)), dma((micro, NB)), dma((micro, NB)), dma((4,))]
    if tree:
        scratch += [dma((units + 1, 8)), dma((units + 1, 8)), dma((units + 1,))]
    res, *grads = pl.pallas_call(
        step_kernel,
        out_shape=(sds(section_data.shape, bf16),) + tuple(sds(shape, bf16) for shape in packed),
        in_specs=[hbm, vmem, vmem, smem, vmem, vmem, vmem, hbm, hbm, hbm, hbm],
        out_specs=(hbm,) * 3,
        scratch_shapes=scratch,
        compiler_params=pltpu.CompilerParams(
            collective_id=0, has_side_effects=True, vmem_limit_bytes=VMEM_LIMIT),
        name="two_layers",
    )(section_data, lang_rows, lang_ids, view_mask, norm_gains, shifts, fc1_bias, w_qkv, w_out, w_fc1, w_fc2)
    if not tree:
        grads = lax.psum(grads, "dp")
    return unpack(res, *grads, D, FF)


def unpack_kernel(res, O, small, out_res, gain, shift, b1, gq, go, g1, g2,
                  low, wide, rows, in_sem, out_sem, res_sem):
    units, D = O.shape[0], O.shape[1]
    UP = g1.shape[2] // D
    micro = res.shape[1]
    into = [pltpu.make_async_copy(res.at[0, m, 0], rows.at[m], res_sem.at[0, m]) for m in range(micro)]
    out = [pltpu.make_async_copy(rows.at[m], out_res.at[0, m, 0], res_sem.at[1, m]) for m in range(micro)]
    loads = [pltpu.make_async_copy(O.at[u], low.at[u], in_sem.at[u]) for u in range(units)]
    for copy in loads + into:
        copy.start()
    width = D // BLK
    for i in range(6 + UP):
        for j in range(width):
            at = i * width + j
            part = small[at:at + 1].astype(f32)
            if i < 2:
                gain[0, i:i + 1, j * BLK:(j + 1) * BLK] = part
            elif i < 6:
                shift[0, i - 2:i - 1, j * BLK:(j + 1) * BLK] = part
            else:
                b1[0:1, (i - 6) * D + j * BLK:(i - 6) * D + (j + 1) * BLK] = part
    stores = []
    for u in range(units):
        loads[u].wait()
        wide[u] = low[u].astype(f32)
        if u < UP:
            dst = g2.at[0, pl.ds(u * D, D)]
        elif u < 2 * UP:
            dst = g1.at[0, :, pl.ds((u - UP) * D, D)]
        elif u < 2 * UP + 3:
            dst = gq.at[0, :, pl.ds((u - 2 * UP) * D, D)]
        else:
            dst = go.at[0]
        stores.append(pltpu.make_async_copy(wide.at[u], dst, out_sem.at[u]))
        stores[-1].start()
        if u < micro:
            into[u].wait()
            out[u].start()
    for copy in stores + out:
        copy.wait()


def unpack(res, O, small, D, FF):
    sds = jax.ShapeDtypeStruct
    units = O.shape[0]
    hbm = pl.BlockSpec(memory_space=pl.ANY)
    vmem = pl.BlockSpec(memory_space=pltpu.VMEM)
    V = pltpu.VMEM
    dma = pltpu.SemaphoreType.DMA
    return pl.pallas_call(
        unpack_kernel,
        in_specs=[hbm, hbm, vmem],
        out_specs=(hbm, vmem, vmem, vmem, hbm, hbm, hbm, hbm),
        out_shape=(sds(res.shape, bf16), sds((1, 2, D), f32), sds((1, 4, D), f32), sds((1, FF), f32),
                   sds((1, D, 3 * D), f32), sds((1, D, D), f32), sds((1, D, FF), f32), sds((1, FF, D), f32)),
        scratch_shapes=[V(O.shape, bf16), V(O.shape, f32), V((res.shape[1],) + res.shape[3:], bf16),
                        dma((units,)), dma((units,)), dma((2, res.shape[1]))],
        compiler_params=pltpu.CompilerParams(vmem_limit_bytes=VMEM_LIMIT),
        name="unpack",
    )(res, O, small)


def solution(mesh):
    weights = P("section", None, None)
    rows = P("section", None, "dp", None, None)
    return jax.shard_map(
        local,
        mesh=mesh,
        in_specs=(rows, P(None, "dp", None, None), P(None, "dp", None), P(None, "dp", None), weights, weights,
                  P("section", None), weights, weights, weights, weights),
        out_specs=(rows, weights, weights, P("section", None), weights, weights, weights, weights),
        check_vma=False,
    )
```

```python
import functools

import jax
import jax.numpy as jnp
from jax import lax
from jax.experimental import pallas as pl
from jax.experimental.pallas import tpu as pltpu
from jax.sharding import PartitionSpec as P

HEADS = 8
HEAD = 64
VIEWS = 5
BLK = 128
EPS = 1e-05
MASKED = -1e30
SCALE = HEAD**-0.5
LOG2E = 1.4426950408889634
MESH = pl.DeviceIdType.MESH
bf16 = jnp.bfloat16
f32 = jnp.float32
VMEM_LIMIT = 64 * 2**20 - 2**19
KEPT_BYTES = 15 * 2**19
GROUPS = 6
LINE_FIRST = (1, 3)
AFTER_DOWN = ()
AFTER_BLOCK = ()
AFTER_UP = (11,)
AFTER_GRAD = ()
AFTER_HALF = (21, 31)
AFTER_VIEWS = ()
AFTER_QKV = (12, 1)
BEFORE = AFTER_DOWN + AFTER_BLOCK + AFTER_UP + AFTER_GRAD + AFTER_HALF + AFTER_VIEWS + AFTER_QKV
REST = (22, 32, 51, 2, 23, 41, 52, 3, 24, 61, 42, 62, 53, 33, 4, 25, 63, 43, 13, 34, 54, 5, 26, 64, 44, 35, 65, 55, 14, 6, 45, 15, 56, 36, 46, 16, 66, 57, 7, 37, 27, 47, 67, 17, 8, 38, 68, 28, 48, 58, 18)


def dot(a, b, ca, cb):
    return lax.dot_general(a, b, (((ca,), (cb,)), ((), ())), preferred_element_type=f32)


def normalise(v):
    centred = v - jnp.mean(v, -1, keepdims=True)
    r = lax.rsqrt(jnp.mean(centred * centred, -1, keepdims=True) + EPS)
    return centred * r, r


def norm_back(v, grad, gain):
    xhat, r = normalise(v)
    gm = grad * gain
    along = jnp.mean(gm * xhat, -1, keepdims=True)
    dv = r * (gm - jnp.mean(gm, -1, keepdims=True) - xhat * along)
    return dv, jnp.sum(grad * xhat, 0, keepdims=True), jnp.sum(grad, 0, keepdims=True)


def gelu_pair(x):
    phi = 0.5 * (1.0 + lax.erf(x * 0.7071067811865476))
    density = jnp.exp2(x * x * (-0.5 * LOG2E)) * 0.3989422804014327
    return x * phi, phi + x * density


def blk(i):
    return pl.ds(pl.multiple_of(i * BLK, BLK), BLK)


def step_kernel(sd, lf, ids, vm, ng, sh, fb, wq_h, wo_h, w1_h, w2_h,
                ob, G, GS,
                h, dy, wq, wo, w1, w2, nT, qT, kvT, kv, PT, linv, attT, hm, nm, act, gg, gb, dOT,
                bias, lx, sm, sb, *rest):
    tree = len(rest) > 6
    if tree:
        V, VS, rest = rest[0], rest[1], rest[2:]
    (in_sem, w_sem, act_send, act_recv, grad_send, grad_recv), rest = rest[:6], rest[6:]
    sec = lax.axis_index("section")
    D = wo.shape[0]
    FF = w1.shape[1]
    R = h.shape[1]
    NB = R // BLK
    LROWS = lf.shape[1]
    KP = kvT.shape[2]
    LP = KP - R
    micro = h.shape[0]
    peer = {"section": 1 - sec}

    def w_copy(k):
        src, dst = ((wq_h, wq), (wo_h, wo), (w1_h, w1), (w2_h, w2))[k]
        return pltpu.make_async_copy(src.at[0], dst, w_sem.at[k])

    def in_copy(m, dst):
        return pltpu.make_async_copy(sd.at[0, m, 0], dst.at[m], in_sem.at[m])

    def act_copy(m, i):
        return pltpu.make_async_remote_copy(
            src_ref=ob.at[m, blk(i)], dst_ref=h.at[m, blk(i)], send_sem=act_send.at[m, i],
            recv_sem=act_recv.at[m, i], device_id=peer, device_id_type=MESH)

    def grad_copy(m, i):
        return pltpu.make_async_remote_copy(
            src_ref=h.at[m, blk(i)], dst_ref=dy.at[m, blk(i)], send_sem=grad_send.at[m, i],
            recv_sem=grad_recv.at[m, i], device_id=peer, device_id_type=MESH)

    gain0, gain1 = ng[0, 0:1], ng[0, 1:2]
    shift = [sh[0, k:k + 1] for k in range(4)]

    def qkv_block(m, i):
        xhat, _ = normalise(h[m, blk(i)].astype(f32))
        n = (xhat * gain0 + shift[0]).astype(bf16)
        nT[m, :, blk(i)] = n.T
        rows = dot(n, wq[...], 1, 0).astype(bf16)
        qT[m, :, blk(i)] = rows[:, :D].T
        kvT[m, :, blk(i)] = rows[:, D:].T
        kv[m, blk(i), :] = rows[:, D:]

    def joint_qkv(m):
        def body(i, c):
            act_copy(m, i).wait_recv()
            qkv_block(m, i)
            return c
        lax.fori_loop(0, NB, body, 0, unroll=True)

    def lang_phase(m):
        rows = jnp.concatenate([lf[0].astype(f32)[:, m, :], jnp.zeros((LP - LROWS, D), f32)], 0)
        xhat, _ = normalise(rows)
        lx[m] = xhat
        n = (xhat * gain0 + shift[0]).astype(bf16)
        nT[m, :, R:KP] = n.T
        rows = dot(n, wq[:, D:], 1, 0).astype(bf16)
        kvT[m, :, R:KP] = rows.T
        kv[m, R:KP, :] = rows
        for v in range(VIEWS):
            seen = (vm[m, 0, v] > 0).astype(f32)
            bias[m, v * BLK:(v + 1) * BLK, :] = (jnp.full((BLK, BLK), MASKED, f32) * (1.0 - seen)).astype(bf16)
        count = jnp.sum((ids[m] != 0).astype(jnp.int32), -1, keepdims=True)
        place = lax.broadcasted_iota(jnp.int32, (LP, BLK), 0)
        bias[m, R:KP, :] = jnp.where(place < count, 0.0, MASKED).astype(bf16)

    def paired(block):
        zero = jnp.zeros((HEAD, block.shape[1]), block.dtype)
        return jnp.concatenate([jnp.concatenate([block[:HEAD], zero], 0),
                                jnp.concatenate([zero, block[HEAD:]], 0)], 1)

    def joint_attention(m):
        def body(hp, c):
            q2 = paired(qT[m, blk(hp), :])
            s = dot(kv[m, :, blk(hp)], q2, 1, 0)
            s = s + jnp.concatenate([bias[m].astype(f32)] * (2 * NB), 1)
            top = jnp.max(s, 0, keepdims=True) * (SCALE * LOG2E)
            p = jnp.exp2(s * (SCALE * LOG2E) - top)
            inv = 1.0 / jnp.sum(p, 0, keepdims=True)
            pb = p.astype(bf16)
            for j in range(2):
                head = 2 * hp + j
                PT[head] = pb[:, j * R:(j + 1) * R]
                linv[m, head] = inv[:, j * R:(j + 1) * R]
                rows = pl.ds(pl.multiple_of(head * HEAD, HEAD), HEAD)
                vT = kvT[m, pl.ds(pl.multiple_of(D + head * HEAD, HEAD), HEAD), :]
                out = dot(vT, pb[:, j * R:(j + 1) * R], 1, 0) * inv[:, j * R:(j + 1) * R]
                attT[m, rows, :] = out.astype(bf16)
            return c
        lax.fori_loop(0, HEADS // 2, body, 0)

    def view_attention(m, v):
        col = blk(v)
        for hp in range(HEADS // 2):
            pair = slice(hp * BLK, (hp + 1) * BLK)
            q2 = paired(qT[m, pair, col])
            s = dot(kv[m, col, pair], q2, 1, 0)
            top = jnp.max(s, 0, keepdims=True) * (SCALE * LOG2E)
            p = jnp.exp2(s * (SCALE * LOG2E) - top)
            inv = 1.0 / jnp.sum(p, 0, keepdims=True)
            pb = p.astype(bf16)
            PT[4 * m + hp, col, 0:2 * BLK] = pb
            for j in range(2):
                linv[m, 2 * hp + j, :, col] = inv[:, j * BLK:(j + 1) * BLK]
            out = dot(kvT[m, D + hp * BLK:D + (hp + 1) * BLK, col], pb, 1, 0) * inv
            attT[m, pair, col] = jnp.concatenate([out[:HEAD, :BLK], out[HEAD:, BLK:]], 0).astype(bf16)

    def mlp_block(m, i):
        mid = h[m, blk(i)].astype(f32) + dot(attT[m, :, blk(i)], wo[...], 0, 0) + shift[1]
        hm[m, blk(i)] = mid
        xhat, _ = normalise(mid)
        n = (xhat * gain1 + shift[2]).astype(bf16)
        nm[m, blk(i)] = n
        for k in range(0, FF, 256):
            a, slope = gelu_pair(dot(n, w1[:, k:k + 256], 1, 0) + fb[:, k:k + 256])
            act[m, blk(i), k:k + 256] = a.astype(bf16)
            gg[m, blk(i), k:k + 256] = slope.astype(bf16)
        out = mid + dot(act[m, blk(i)], w2[...], 1, 0) + shift[3]
        ob[m, blk(i)] = out.astype(bf16)

    def joint_mlp(m):
        hm[m] = h[m].astype(f32) + dot(attT[m], wo[...], 0, 0) + shift[1]
        for i in range(NB):
            row = slice(i * BLK, (i + 1) * BLK)
            xhat, _ = normalise(hm[m, row])
            nm[m, row] = (xhat * gain1 + shift[2]).astype(bf16)
        for k in range(0, FF, 256):
            a, slope = gelu_pair(dot(nm[m], w1[:, k:k + 256], 1, 0) + fb[:, k:k + 256])
            act[m, :, k:k + 256] = a.astype(bf16)
            gg[m, :, k:k + 256] = slope.astype(bf16)
        ob[m] = (hm[m] + dot(act[m], w2[...], 1, 0) + shift[3]).astype(bf16)

    def mid_back(m, row, gn):
        dv, dgain, dshift = norm_back(hm[m, row], gn, gain1)
        d32 = dy[m, row].astype(f32)
        mid = d32 + dv
        hm[m, row] = mid
        low = mid.astype(bf16)
        gb[m, row] = low
        sm[1:2] += dgain
        sm[4:5] += dshift
        sm[5:6] += jnp.sum(d32, 0, keepdims=True)
        sm[3:4] += jnp.sum(low.astype(f32), 0, keepdims=True)

    def pre_back(m, row, width):
        d = dy[m, row]
        for k in range(0, FF, width):
            gp = (dot(d, w2[k:k + width], 1, 1) * gg[m, row, k:k + width].astype(f32)).astype(bf16)
            gg[m, row, k:k + width] = gp
            sb[:, k:k + width] += jnp.sum(gp.astype(f32), 0, keepdims=True)

    def mlp_back_block(m, i):
        pre_back(m, blk(i), 512)
        mid_back(m, blk(i), dot(gg[m, blk(i)], w1[...], 1, 1))

    def joint_mlp_back(m):
        pre_back(m, slice(0, R), 256)
        gn = dot(gg[m], w1[...], 1, 1)
        for i in range(NB):
            row = slice(i * BLK, (i + 1) * BLK)
            mid_back(m, row, gn[row])

    def att_grad(m):
        dOT[...] = dot(wo[...], gb[m], 1, 1).astype(bf16)

    def joint_attention_back(m):
        def body(hp, c):
            inv = jnp.concatenate([linv[m, 2 * hp], linv[m, 2 * hp + 1]], 1)
            block = dOT[blk(hp), :].astype(f32)
            d0 = (block[:HEAD] * inv[:, :R]).astype(bf16)
            d1 = (block[HEAD:] * inv[:, R:]).astype(bf16)
            zero = jnp.zeros((HEAD, R), bf16)
            d2 = jnp.concatenate([jnp.concatenate([d0, zero], 0), jnp.concatenate([zero, d1], 0)], 1)
            vcol = pl.ds(pl.multiple_of(D + hp * BLK, BLK), BLK)
            dp = dot(kv[m, :, vcol], d2, 1, 0)
            pb = jnp.concatenate([PT[2 * hp], PT[2 * hp + 1]], 1)
            p = pb.astype(f32)
            inner = jnp.sum(p * dp, 0, keepdims=True) * inv
            ds = (p * (dp - inner)).astype(bf16)
            for j in range(2):
                head = 2 * hp + j
                side = slice(j * R, (j + 1) * R)
                rows = pl.ds(pl.multiple_of(head * HEAD, HEAD), HEAD)
                vrows = pl.ds(pl.multiple_of(D + head * HEAD, HEAD), HEAD)
                kvT[m, vrows, :] = dot((d0, d1)[j], PT[head], 1, 1).astype(bf16)
                dq = dot(kvT[m, rows, :], ds[:, side], 1, 0) * SCALE
                kvT[m, rows, :] = (dot(qT[m, rows, :], ds[:, side], 1, 1) * SCALE).astype(bf16)
                qT[m, rows, :] = dq.astype(bf16)
            return c
        lax.fori_loop(0, HEADS // 2, body, 0)

    def view_attention_back(m, first, last):
        def body(hp, c):
            vrow = pl.ds(pl.multiple_of(D + hp * BLK, BLK), BLK)
            pair = blk(hp)
            for v in range(NB):
                col = slice(v * BLK, (v + 1) * BLK)
                inv = jnp.concatenate([linv[m, 2 * hp, :, col], linv[m, 2 * hp + 1, :, col]], 1)
                d2 = (paired(dOT[pair, col]).astype(f32) * inv).astype(bf16)
                dp = dot(kv[m, col, vrow], d2, 1, 0)
                pb = PT[4 * m + hp, col, 0:2 * BLK]
                p = pb.astype(f32)
                inner = jnp.sum(p * dp, 0, keepdims=True) * inv
                ds = (p * (dp - inner)).astype(bf16)
                q2 = paired(qT[m, pair, col])
                dv = dot(d2, pb, 1, 1).astype(bf16)
                dq = dot(kvT[m, pair, col], ds, 1, 0) * SCALE
                dk = (dot(q2, ds, 1, 1) * SCALE).astype(bf16)
                kvT[m, vrow, col] = dv
                kvT[m, pair, col] = dk
                qT[m, pair, col] = jnp.concatenate([dq[:HEAD, :BLK], dq[HEAD:, BLK:]], 0).astype(bf16)
            return c
        lax.fori_loop(first, last, body, 0)

    def qkv_back(m, joint):
        gn = dot(qT[m], wq[:, :D], 0, 1) + dot(kvT[m, :, 0:R], wq[:, D:], 0, 1)
        for i in range(NB):
            row = slice(i * BLK, (i + 1) * BLK)
            dv, dgain, dshift = norm_back(h[m, row].astype(f32), gn[row], gain0)
            sm[0:1] += dgain
            sm[2:3] += dshift
            out = (hm[m, row] + dv).astype(bf16)
            if joint:
                h[m, row] = out
                grad_copy(m, i).start()
            else:
                ob[m, row] = out
        if joint:
            gn = dot(kvT[m, :, R:KP], wq[:, D:], 0, 1)
            sm[0:1] += jnp.sum(gn * lx[m], 0, keepdims=True)
            sm[2:3] += jnp.sum(gn, 0, keepdims=True)

    UP, QKV, OUT = FF // D, 2 * (FF // D), 2 * (FF // D) + 3

    def cols(k):
        return pl.ds(pl.multiple_of(k * D, D), D)

    def put(u, t):
        G[u] = (G[u].astype(f32) + t).astype(bf16)

    def down_weights(ms, first, count, unroll=1):
        def body(k, c):
            put(k, sum(dot(act[m, :, cols(k)], dy[m], 0, 0) for m in ms))
            return c
        lax.fori_loop(first, first + count, body, 0, unroll=unroll)

    def up_weights(ms, first, count, unroll=1):
        def body(k, c):
            put(UP + k, sum(dot(nm[m], gg[m, :, cols(k)], 0, 0) for m in ms))
            return c
        lax.fori_loop(first, first + count, body, 0, unroll=unroll)

    def attention_weights(ms, joint):
        keys = KP if joint else R
        put(QKV, sum(dot(nT[m, :, 0:R], qT[m], 1, 1) for m in ms))

        def body(k, c):
            put(QKV + 1 + k, sum(dot(nT[m, :, 0:keys], kvT[m, cols(k), 0:keys], 1, 1) for m in ms))
            return c
        lax.fori_loop(0, 2, body, 0)
        put(OUT, sum(dot(attT[m], gb[m], 1, 0) for m in ms))

    def small_sums():
        rows = [sm[i:i + 1] for i in range(6)] + [sb[:, k * D:(k + 1) * D] for k in range(FF // D)]
        GS[...] = jnp.zeros_like(GS)
        parts = [row[:, j * BLK:(j + 1) * BLK] for row in rows for j in range(D // BLK)]
        parts += [jnp.zeros((1, BLK), f32)] * (-len(parts) % 16)
        GS[0:len(parts)] = jnp.concatenate(parts, 0).astype(bf16)

    if tree:
        (t_send, t_recv, free) = rest
        dp = lax.axis_index("dp")
        bits = lax.axis_size("dp").bit_length() - 1
        bit = [lax.rem(dp // (1 << k), 2) for k in range(bits)]
        partner = [{"dp": dp + (1 - 2 * bit[k]) * (1 << k)} for k in range(bits)]

        def refs(g):
            if g == GROUPS:
                return GS, VS
            two = pl.ds(2 * g, 2)
            return G.at[two], V.at[two]

        def order(g):
            return (0,) + tuple(range(2, bits)) + (1,) if g in LINE_FIRST else tuple(range(bits))

        def rows_of(ref, first, size):
            part = pl.ds(first, size)
            return ref.at[:, part] if len(ref.shape) == 3 else ref.at[part]

        def height(g):
            return GS.shape[0] if g == GROUPS else D

        def offset(g, k):
            total = sum((bit[order(g)[j]] * (height(g) >> (j + 1)) for j in range(k + 1)), 0)
            return pl.multiple_of(total, 16)

        def tree_copy(g, k):
            mine, theirs = refs(g)
            rows = height(g)
            if k < bits:
                size = rows >> (k + 1)
                away = 1 - bit[order(g)[k]]
                src = rows_of(mine, pl.multiple_of(offset(g, k - 1) + away * size, 16), size)
                dst = rows_of(theirs, rows - (rows >> k), size)
                to = partner[order(g)[k]]
            else:
                j = 2 * bits - 1 - k
                size = rows >> (j + 1)
                src = dst = rows_of(mine, offset(g, j), size)
                to = partner[order(g)[j]]
            return pltpu.make_async_remote_copy(src_ref=src, dst_ref=dst, send_sem=t_send.at[g, k],
                                                recv_sem=t_recv.at[g, k], device_id=to, device_id_type=MESH)

        def event(g, k):
            rows = height(g)
            if k > 0:
                tree_copy(g, k - 1).wait_recv()
            if 0 < k <= bits:
                tree_copy(g, k - 1).wait_send()
                pl.semaphore_signal(free.at[g, k - 1], inc=1, device_id=partner[order(g)[k - 1]], device_id_type=MESH)
                size = rows >> k
                step = min(size, 64)
                first = offset(g, k - 1)

                def add(i, c):
                    here = pl.ds(pl.multiple_of(first + i * step, 16), step)
                    there = pl.ds(pl.multiple_of(rows - (rows >> (k - 1)) + i * step, 16), step)
                    if g == GROUPS:
                        GS[here, :] = (GS[here, :].astype(f32) + VS[there, :].astype(f32)).astype(bf16)
                    else:
                        for u in (2 * g, 2 * g + 1):
                            G[u, here, :] = (G[u, here, :].astype(f32) + V[u, there, :].astype(f32)).astype(bf16)
                    return c
                lax.fori_loop(0, size // step, add, 0)
            if bits <= k < 2 * bits:
                pl.semaphore_wait(free.at[g, 2 * bits - 1 - k], 1)
            if k < 2 * bits:
                tree_copy(g, k).start()

        def settle():
            for g in range(GROUPS + 1):
                for k in range(bits, 2 * bits):
                    tree_copy(g, k).wait_send()

    def run(tokens):
        if tree:
            for token in tokens:
                event(token // 10, token % 10)

    @pl.when(sec == 0)
    def _():
        in_copy(0, h).start()
        for k in range(4):
            w_copy(k).start()
        for m in range(1, micro):
            in_copy(m, h).start()

    @pl.when(sec == 1)
    def _():
        for k in range(4):
            w_copy(k).start()
        for m in range(micro):
            in_copy(m, dy).start()

    barrier = pltpu.get_barrier_semaphore()
    greeted = [peer] + (partner if tree else [])
    for device in greeted:
        pl.semaphore_signal(barrier, inc=1, device_id=device, device_id_type=MESH)
    sm[...] = jnp.zeros_like(sm)
    sb[...] = jnp.zeros_like(sb)

    @pl.when(sec == 0)
    def _():
        def forward(m, c):
            in_copy(m, h).wait()

            @pl.when(m == 0)
            def _():
                w_copy(0).wait()

            def view(i, c):
                qkv_block(m, i)
                view_attention(m, i)

                @pl.when((m == 0) & (i == 0))
                def _():
                    for k in range(1, 4):
                        w_copy(k).wait()
                mlp_block(m, i)

                @pl.when((m == 0) & (i == 0))
                def _():
                    pl.semaphore_wait(barrier, len(greeted))

                @pl.when((m > 0) & (i == 0))
                def _():
                    for j in range(NB):
                        act_copy(m - 1, j).wait_send()
                act_copy(m, i).start()
                return c
            lax.fori_loop(0, NB, view, 0)
            return c
        lax.fori_loop(0, micro, forward, 0)
        for j in range(NB):
            act_copy(micro - 1, j).wait_send()

        G[...] = jnp.zeros_like(G)

        def backward(m, c):
            final = m == micro - 1

            def when_final(tokens):
                if tree and tokens:
                    @pl.when(final)
                    def _():
                        run(tokens)

            def body(i, c):
                grad_copy(m, i).wait_recv()

                @pl.when(i == NB - 1)
                def _():
                    down_weights([m], 0, 2, 2)
                    when_final((0,))
                    down_weights([m], 2, 2, 2)
                    when_final((10,) + AFTER_DOWN)
                mlp_back_block(m, i)
                return c
            lax.fori_loop(0, NB, body, 0)
            when_final(AFTER_BLOCK)
            up_weights([m], 0, 2)
            when_final((20,))
            up_weights([m], 2, 2)
            when_final((30,) + AFTER_UP)
            att_grad(m)
            when_final(AFTER_GRAD)
            view_attention_back(m, 0, 2)
            when_final(AFTER_HALF)
            view_attention_back(m, 2, 4)
            when_final(AFTER_VIEWS)
            qkv_back(m, False)
            when_final(AFTER_QKV)
            attention_weights([m], False)
            return c
        lax.fori_loop(0, micro, backward, 0)

    @pl.when(sec == 1)
    def _():
        for k in range(4):
            w_copy(k).wait()
        for m in range(micro):
            in_copy(m, dy).wait()
        pl.semaphore_wait(barrier, len(greeted))
        for m in range(micro):
            lang_phase(m)

        def item(m, c):
            joint_qkv(m)
            joint_attention(m)
            joint_mlp(m)
            joint_mlp_back(m)
            att_grad(m)
            joint_attention_back(m)
            qkv_back(m, True)
            return c
        lax.fori_loop(0, micro, item, 0)
        G[...] = jnp.zeros_like(G)
        down_weights(range(micro), 0, 4)
        run((0, 10))
        up_weights(range(micro), 0, 4)
        run((20, 30) + BEFORE)
        attention_weights(range(micro), True)

    small_sums()
    if tree:
        run((40, 50, 60) + REST)
        settle()

    @pl.when(sec == 1)
    def _():
        for m in range(micro):
            for i in range(NB):
                grad_copy(m, i).wait_send()


def local(section_data, lang_feat, lang_ids, view_mask, norm_gains, shifts, fc1_bias, w_qkv, w_out, w_fc1, w_fc2):
    micro, rows, D = section_data.shape[1], section_data.shape[3], section_data.shape[4]
    FF = w_fc1.shape[2]
    lang = lang_feat.shape[2]
    lang_rows = jnp.transpose(lang_feat, (1, 2, 0, 3))
    KP = rows + -(-lang // 16) * 16
    NB = rows // BLK
    hbm = pl.BlockSpec(memory_space=pl.ANY)
    vmem = pl.BlockSpec(memory_space=pltpu.VMEM)
    smem = pl.BlockSpec(memory_space=pltpu.SMEM)
    V = pltpu.VMEM
    dma = pltpu.SemaphoreType.DMA
    sds = jax.ShapeDtypeStruct
    units = 2 * (FF // D) + 4
    tree = lax.axis_size("dp") == 16 and D % 256 == 0 and units == 2 * GROUPS
    kept = ((micro, rows, D), (units, D, D), (256, BLK))
    scratch = [
        V((micro, rows, D), bf16),
        V((micro, rows, D), bf16),
        V((D, 3 * D), bf16), V((D, D), bf16), V((D, FF), bf16), V((FF, D), bf16),
        V((micro, D, KP), bf16),
        V((micro, D, rows), bf16),
        V((micro, 2 * D, KP), bf16),
        V((micro, KP, 2 * D), bf16),
        V((HEADS, KP, rows), bf16),
        V((micro, HEADS, 1, rows), f32),
        V((micro, D, rows), bf16),
        V((micro, rows, D), f32),
        V((micro, rows, D), bf16),
        V((micro, rows, FF), bf16),
        V((micro, rows, FF), bf16),
        V((micro, rows, D), bf16),
        V((D, rows), bf16),
        V((micro, KP, BLK), bf16),
        V((micro, KP - rows, D), f32),
        V((8, D), f32), V((1, FF), f32),
    ]
    if tree:
        scratch += [V((units, D - D // 16, D), bf16), V((256 - 16, BLK), bf16)]
    scratch += [dma((micro,)), dma((4,)),
                dma((micro, NB)), dma((micro, NB)), dma((micro, NB)), dma((micro, NB))]
    if tree:
        scratch += [dma((units // 2 + 1, 8)), dma((units // 2 + 1, 8)),
                    pltpu.SemaphoreType.REGULAR((units // 2 + 1, 4))]
    res, *grads = pl.pallas_call(
        step_kernel,
        out_shape=tuple((V if tree else sds)(shape, bf16) for shape in kept),
        in_specs=[hbm, vmem, vmem, smem, vmem, vmem, vmem, hbm, hbm, hbm, hbm],
        out_specs=(vmem,) * 3,
        scratch_shapes=scratch,
        compiler_params=pltpu.CompilerParams(
            collective_id=0, has_side_effects=True, vmem_limit_bytes=VMEM_LIMIT - (KEPT_BYTES if tree else 0)),
        name="two_layers",
    )(section_data, lang_rows, lang_ids, view_mask, norm_gains, shifts, fc1_bias, w_qkv, w_out, w_fc1, w_fc2)
    if not tree:
        grads = lax.psum(grads, "dp")
    return unpack(res, *grads, section_data.shape, FF)


def unpack_kernel(rows, low, small, out_res, gain, shift, b1, gq, go, g1, g2, wide, out_sem, res_sem):
    units, D = low.shape[0], low.shape[1]
    UP = g1.shape[2] // D
    micro = rows.shape[0]
    out = [pltpu.make_async_copy(rows.at[m], out_res.at[0, m, 0], res_sem.at[m]) for m in range(micro)]
    for copy in out:
        copy.start()
    width = D // BLK
    for i in range(6 + UP):
        for j in range(width):
            at = i * width + j
            part = small[at:at + 1].astype(f32)
            if i < 2:
                gain[0, i:i + 1, j * BLK:(j + 1) * BLK] = part
            elif i < 6:
                shift[0, i - 2:i - 1, j * BLK:(j + 1) * BLK] = part
            else:
                b1[0:1, (i - 6) * D + j * BLK:(i - 6) * D + (j + 1) * BLK] = part
    stores = []
    for u in range(units):
        wide[u] = low[u].astype(f32)
        if u < UP:
            dst = g2.at[0, pl.ds(u * D, D)]
        elif u < 2 * UP:
            dst = g1.at[0, :, pl.ds((u - UP) * D, D)]
        elif u < 2 * UP + 3:
            dst = gq.at[0, :, pl.ds((u - 2 * UP) * D, D)]
        else:
            dst = go.at[0]
        stores.append(pltpu.make_async_copy(wide.at[u], dst, out_sem.at[u]))
        stores[-1].start()
    for copy in stores + out:
        copy.wait()


def unpack(rows, low, small, shape, FF):
    sds = jax.ShapeDtypeStruct
    units, D = low.shape[0], low.shape[1]
    hbm = pl.BlockSpec(memory_space=pl.ANY)
    vmem = pl.BlockSpec(memory_space=pltpu.VMEM)
    dma = pltpu.SemaphoreType.DMA
    return pl.pallas_call(
        unpack_kernel,
        in_specs=[vmem, vmem, vmem],
        out_specs=(hbm, vmem, vmem, vmem, hbm, hbm, hbm, hbm),
        out_shape=(sds(shape, bf16), sds((1, 2, D), f32), sds((1, 4, D), f32), sds((1, FF), f32),
                   sds((1, D, 3 * D), f32), sds((1, D, D), f32), sds((1, D, FF), f32), sds((1, FF, D), f32)),
        scratch_shapes=[pltpu.VMEM(low.shape, f32), dma((units,)), dma((rows.shape[0],))],
        compiler_params=pltpu.CompilerParams(vmem_limit_bytes=32 * 2**20),
        name="unpack",
    )(rows, low, small)


def solution(mesh):
    weights = P("section", None, None)
    rows = P("section", None, "dp", None, None)
    return jax.shard_map(
        local,
        mesh=mesh,
        in_specs=(rows, P(None, "dp", None, None), P(None, "dp", None), P(None, "dp", None), weights, weights,
                  P("section", None), weights, weights, weights, weights),
        out_specs=(rows, weights, weights, P("section", None), weights, weights, weights, weights),
        check_vma=False,
    )
```

```python
import functools

import jax
import jax.numpy as jnp
from jax import lax
from jax.experimental import pallas as pl
from jax.experimental.pallas import tpu as pltpu
from jax.sharding import PartitionSpec as P

HEADS = 8
HEAD = 64
VIEWS = 5
BLK = 128
EPS = 1e-05
MASKED = -1e30
SCALE = HEAD**-0.5
LOG2E = 1.4426950408889634
MESH = pl.DeviceIdType.MESH
bf16 = jnp.bfloat16
f32 = jnp.float32
VMEM_LIMIT = 64 * 2**20 - 2**19
KEPT_BYTES = 15 * 2**19
UNITS = 12
LINE_FIRST = (3, 4)
AFTER_DOWN = ()
AFTER_DOWN2 = ()
AFTER_BLOCK = (11, 31, 21)
AFTER_UP = ()
AFTER_UP2 = (41, 51)
AFTER_GRAD = (61, 12)
AFTER_HALF = (22, 32)
AFTER_VIEWS = (13,)
AFTER_QKV = (23, 42, 62)
BEFORE = (AFTER_DOWN + AFTER_DOWN2 + AFTER_BLOCK + AFTER_UP + AFTER_UP2 + AFTER_GRAD + AFTER_HALF + AFTER_VIEWS + AFTER_QKV)
REST = (1, 52, 14, 24, 91, 101, 111, 71, 81, 63, 43, 33, 121, 53, 15, 2, 25, 64, 92, 54, 16, 3, 102, 65, 26, 55, 112, 93, 4, 72, 103, 66, 94, 82, 56, 44, 5, 34, 122, 113, 104, 95, 17, 73, 18, 114, 27, 83, 105, 28, 6, 123, 74, 67, 115, 68, 96, 84, 124, 57, 45, 75, 35, 58, 106, 85, 125, 7, 116, 8, 46, 97, 76, 98, 36, 107, 86, 126, 108, 117, 47, 118, 77, 48, 37, 78, 87, 38, 127, 88, 128)


def dot(a, b, ca, cb):
    return lax.dot_general(a, b, (((ca,), (cb,)), ((), ())), preferred_element_type=f32)


def normalise(v):
    centred = v - jnp.mean(v, -1, keepdims=True)
    r = lax.rsqrt(jnp.mean(centred * centred, -1, keepdims=True) + EPS)
    return centred * r, r


def norm_back(v, grad, gain):
    xhat, r = normalise(v)
    gm = grad * gain
    along = jnp.mean(gm * xhat, -1, keepdims=True)
    dv = r * (gm - jnp.mean(gm, -1, keepdims=True) - xhat * along)
    return dv, jnp.sum(grad * xhat, 0, keepdims=True), jnp.sum(grad, 0, keepdims=True)


def gelu_pair(x):
    phi = 0.5 + 0.5 * lax.erf(x * 0.7071067811865476)
    gelu = x * phi
    return gelu, phi + (x * 0.3989422804014327) * jnp.exp2(x * (x * (-0.5 * LOG2E)))


def blk(i):
    return pl.ds(pl.multiple_of(i * BLK, BLK), BLK)


def step_kernel(sd, lf, ids, vm, ng, sh, fb, wq_h, wo_h, w1_h, w2_h,
                ob, G, GS,
                h, dy, wq, wo, w1, w2, nT, qT, kvT, kv, PT, linv, attT, hm, nm, act, gg, gb, dOT,
                bias, lx, sm, sb, *rest):
    tree = len(rest) > 6
    if tree:
        V, VS, rest = rest[0], rest[1], rest[2:]
    (in_sem, w_sem, act_send, act_recv, grad_send, grad_recv), rest = rest[:6], rest[6:]
    sec = lax.axis_index("section")
    D = wo.shape[0]
    FF = w1.shape[1]
    R = h.shape[1]
    NB = R // BLK
    LROWS = lf.shape[1]
    KP = kvT.shape[2]
    LP = KP - R
    micro = h.shape[0]
    peer = {"section": 1 - sec}

    def w_copy(k):
        src, dst = ((wq_h, wq), (wo_h, wo), (w1_h, w1), (w2_h, w2))[k]
        return pltpu.make_async_copy(src.at[0], dst, w_sem.at[k])

    def in_copy(m, dst):
        return pltpu.make_async_copy(sd.at[0, m, 0], dst.at[m], in_sem.at[m])

    def act_copy(m, i):
        return pltpu.make_async_remote_copy(
            src_ref=ob.at[m, blk(i)], dst_ref=h.at[m, blk(i)], send_sem=act_send.at[m, i],
            recv_sem=act_recv.at[m, i], device_id=peer, device_id_type=MESH)

    def grad_copy(m, i):
        return pltpu.make_async_remote_copy(
            src_ref=h.at[m, blk(i)], dst_ref=dy.at[m, blk(i)], send_sem=grad_send.at[m, i],
            recv_sem=grad_recv.at[m, i], device_id=peer, device_id_type=MESH)

    gain0, gain1 = ng[0, 0:1], ng[0, 1:2]
    shift = [sh[0, k:k + 1] for k in range(4)]

    def qkv_block(m, i):
        xhat, _ = normalise(h[m, blk(i)].astype(f32))
        n = (xhat * gain0 + shift[0]).astype(bf16)
        nT[m, :, blk(i)] = n.T
        rows = dot(n, wq[...], 1, 0).astype(bf16)
        qT[m, :, blk(i)] = rows[:, :D].T
        kvT[m, :, blk(i)] = rows[:, D:].T
        kv[m, blk(i), :] = rows[:, D:]

    def joint_qkv(m):
        def body(i, c):
            act_copy(m, i).wait_recv()
            qkv_block(m, i)
            return c
        lax.fori_loop(0, NB, body, 0, unroll=True)

    def lang_phase(m):
        rows = jnp.concatenate([lf[0].astype(f32)[:, m, :], jnp.zeros((LP - LROWS, D), f32)], 0)
        xhat, _ = normalise(rows)
        lx[m] = xhat
        n = (xhat * gain0 + shift[0]).astype(bf16)
        nT[m, :, R:KP] = n.T
        rows = dot(n, wq[:, D:], 1, 0).astype(bf16)
        kvT[m, :, R:KP] = rows.T
        kv[m, R:KP, :] = rows
        for v in range(VIEWS):
            seen = (vm[m, 0, v] > 0).astype(f32)
            bias[m, v * BLK:(v + 1) * BLK, :] = (jnp.full((BLK, BLK), MASKED, f32) * (1.0 - seen)).astype(bf16)
        count = jnp.sum((ids[m] != 0).astype(jnp.int32), -1, keepdims=True)
        place = lax.broadcasted_iota(jnp.int32, (LP, BLK), 0)
        bias[m, R:KP, :] = jnp.where(place < count, 0.0, MASKED).astype(bf16)

    def paired(block):
        zero = jnp.zeros((HEAD, block.shape[1]), block.dtype)
        return jnp.concatenate([jnp.concatenate([block[:HEAD], zero], 0),
                                jnp.concatenate([zero, block[HEAD:]], 0)], 1)

    def joint_attention(m):
        def body(hp, c):
            q2 = paired(qT[m, blk(hp), :])
            s = dot(kv[m, :, blk(hp)], q2, 1, 0)
            s = s + jnp.concatenate([bias[m].astype(f32)] * (2 * NB), 1)
            top = jnp.max(s, 0, keepdims=True) * (SCALE * LOG2E)
            p = jnp.exp2(s * (SCALE * LOG2E) - top)
            inv = 1.0 / jnp.sum(p, 0, keepdims=True)
            pb = p.astype(bf16)
            for j in range(2):
                head = 2 * hp + j
                PT[head] = pb[:, j * R:(j + 1) * R]
                linv[m, head] = inv[:, j * R:(j + 1) * R]
                rows = pl.ds(pl.multiple_of(head * HEAD, HEAD), HEAD)
                vT = kvT[m, pl.ds(pl.multiple_of(D + head * HEAD, HEAD), HEAD), :]
                out = dot(vT, pb[:, j * R:(j + 1) * R], 1, 0) * inv[:, j * R:(j + 1) * R]
                attT[m, rows, :] = out.astype(bf16)
            return c
        lax.fori_loop(0, HEADS // 2, body, 0)

    def view_attention(m, v):
        col = blk(v)
        for hp in range(HEADS // 2):
            pair = slice(hp * BLK, (hp + 1) * BLK)
            q2 = paired(qT[m, pair, col])
            s = dot(kv[m, col, pair], q2, 1, 0)
            top = jnp.max(s, 0, keepdims=True) * (SCALE * LOG2E)
            p = jnp.exp2(s * (SCALE * LOG2E) - top)
            inv = 1.0 / jnp.sum(p, 0, keepdims=True)
            pb = p.astype(bf16)
            PT[4 * m + hp, col, 0:2 * BLK] = pb
            for j in range(2):
                linv[m, 2 * hp + j, :, col] = inv[:, j * BLK:(j + 1) * BLK]
            out = dot(kvT[m, D + hp * BLK:D + (hp + 1) * BLK, col], pb, 1, 0) * inv
            attT[m, pair, col] = jnp.concatenate([out[:HEAD, :BLK], out[HEAD:, BLK:]], 0).astype(bf16)

    def mlp_block(m, i, late):
        mid = h[m, blk(i)].astype(f32) + dot(attT[m, :, blk(i)], wo[...], 0, 0) + shift[1]
        hm[m, blk(i)] = mid
        xhat, _ = normalise(mid)
        n = (xhat * gain1 + shift[2]).astype(bf16)
        nm[m, blk(i)] = n
        for k in range(0, FF, 256):
            a, slope = gelu_pair(dot(n, w1[:, k:k + 256], 1, 0) + fb[:, k:k + 256])
            act[m, blk(i), k:k + 256] = a.astype(bf16)
            gg[m, blk(i), k:k + 256] = slope.astype(bf16)
        late()
        out = mid + dot(act[m, blk(i)], w2[...], 1, 0) + shift[3]
        ob[m, blk(i)] = out.astype(bf16)

    def joint_mlp(m):
        hm[m] = h[m].astype(f32) + dot(attT[m], wo[...], 0, 0) + shift[1]
        for i in range(NB):
            row = slice(i * BLK, (i + 1) * BLK)
            xhat, _ = normalise(hm[m, row])
            nm[m, row] = (xhat * gain1 + shift[2]).astype(bf16)
        for k in range(0, FF, 256):
            a, slope = gelu_pair(dot(nm[m], w1[:, k:k + 256], 1, 0) + fb[:, k:k + 256])
            act[m, :, k:k + 256] = a.astype(bf16)
            gg[m, :, k:k + 256] = slope.astype(bf16)
        ob[m] = (hm[m] + dot(act[m], w2[...], 1, 0) + shift[3]).astype(bf16)

    def mid_back(m, row, gn):
        dv, dgain, dshift = norm_back(hm[m, row], gn, gain1)
        d32 = dy[m, row].astype(f32)
        mid = d32 + dv
        hm[m, row] = mid
        low = mid.astype(bf16)
        gb[m, row] = low
        sm[1:2] += dgain
        sm[4:5] += dshift
        sm[5:6] += jnp.sum(d32, 0, keepdims=True)
        sm[3:4] += jnp.sum(low.astype(f32), 0, keepdims=True)

    def pre_back(m, row, width):
        d = dy[m, row]
        for k in range(0, FF, width):
            gp = (dot(d, w2[k:k + width], 1, 1) * gg[m, row, k:k + width].astype(f32)).astype(bf16)
            gg[m, row, k:k + width] = gp
            sb[:, k:k + width] += jnp.sum(gp.astype(f32), 0, keepdims=True)

    def mlp_back_block(m, i):
        pre_back(m, blk(i), 512)
        mid_back(m, blk(i), dot(gg[m, blk(i)], w1[...], 1, 1))

    def joint_mlp_back(m):
        pre_back(m, slice(0, R), 256)
        gn = dot(gg[m], w1[...], 1, 1)
        for i in range(NB):
            row = slice(i * BLK, (i + 1) * BLK)
            mid_back(m, row, gn[row])

    def att_grad(m):
        dOT[...] = dot(wo[...], gb[m], 1, 1).astype(bf16)

    def joint_attention_back(m):
        def body(hp, c):
            pair = blk(hp)
            inv = jnp.concatenate([linv[m, 2 * hp], linv[m, 2 * hp + 1]], 1)
            d2 = (paired(dOT[pair, :]).astype(f32) * inv).astype(bf16)
            vcol = pl.ds(pl.multiple_of(D + hp * BLK, BLK), BLK)
            dp = dot(kv[m, :, vcol], d2, 1, 0)
            pb = jnp.concatenate([PT[2 * hp], PT[2 * hp + 1]], 1)
            p = pb.astype(f32)
            inner = jnp.sum(p * dp, 0, keepdims=True) * inv
            ds = (p * (dp - inner)).astype(bf16)
            q2 = paired(qT[m, pair, :])
            kvT[m, vcol, :] = dot(d2, pb, 1, 1).astype(bf16)
            dq = dot(kvT[m, pair, :], ds, 1, 0) * SCALE
            dq0, dq1 = dq[:HEAD, :R], dq[HEAD:, R:]
            kvT[m, pair, :] = (dot(q2, ds, 1, 1) * SCALE).astype(bf16)
            qT[m, pair, :] = jnp.concatenate([dq0, dq1], 0).astype(bf16)
            return c
        lax.fori_loop(0, HEADS // 2, body, 0)

    def view_attention_back(m, first, last):
        def body(hp, c):
            vrow = pl.ds(pl.multiple_of(D + hp * BLK, BLK), BLK)
            pair = blk(hp)
            for v in range(NB):
                col = slice(v * BLK, (v + 1) * BLK)
                inv = jnp.concatenate([linv[m, 2 * hp, :, col], linv[m, 2 * hp + 1, :, col]], 1)
                d2 = (paired(dOT[pair, col]).astype(f32) * inv).astype(bf16)
                dp = dot(kv[m, col, vrow], d2, 1, 0)
                pb = PT[4 * m + hp, col, 0:2 * BLK]
                p = pb.astype(f32)
                inner = jnp.sum(p * dp, 0, keepdims=True) * inv
                ds = (p * (dp - inner)).astype(bf16)
                q2 = paired(qT[m, pair, col])
                dv = dot(d2, pb, 1, 1).astype(bf16)
                dq = dot(kvT[m, pair, col], ds, 1, 0) * SCALE
                dk = (dot(q2, ds, 1, 1) * SCALE).astype(bf16)
                kvT[m, vrow, col] = dv
                kvT[m, pair, col] = dk
                qT[m, pair, col] = jnp.concatenate([dq[:HEAD, :BLK], dq[HEAD:, BLK:]], 0).astype(bf16)
            return c
        lax.fori_loop(first, last, body, 0)

    def qkv_back(m, joint):
        for first, last in ((0, 1), (1, NB)):
            rows = slice(first * BLK, last * BLK)
            gn = dot(qT[m, :, rows], wq[:, :D], 0, 1) + dot(kvT[m, :, rows], wq[:, D:], 0, 1)
            for i in range(first, last):
                row = slice(i * BLK, (i + 1) * BLK)
                part = gn[(i - first) * BLK:(i - first + 1) * BLK]
                dv, dgain, dshift = norm_back(h[m, row].astype(f32), part, gain0)
                sm[0:1] += dgain
                sm[2:3] += dshift
                out = (hm[m, row] + dv).astype(bf16)
                if joint:
                    h[m, row] = out
                    grad_copy(m, i).start()
                else:
                    ob[m, row] = out
        if joint:
            gn = dot(kvT[m, :, R:KP], wq[:, D:], 0, 1)
            sm[0:1] += jnp.sum(gn * lx[m], 0, keepdims=True)
            sm[2:3] += jnp.sum(gn, 0, keepdims=True)

    UP, QKV, OUT = FF // D, 2 * (FF // D), 2 * (FF // D) + 3

    def cols(k):
        return pl.ds(pl.multiple_of(k * D, D), D)

    def put(u, t):
        G[u] = (G[u].astype(f32) + t).astype(bf16)

    def down_weights(ms, first, count, unroll=1, rows=slice(None)):
        def body(k, c):
            put(k, sum(dot(act[m, rows, cols(k)], dy[m, rows], 0, 0) for m in ms))
            return c
        lax.fori_loop(first, first + count, body, 0, unroll=unroll)

    def up_weights(ms, first, count, unroll=1):
        def body(k, c):
            put(UP + k, sum(dot(nm[m], gg[m, :, cols(k)], 0, 0) for m in ms))
            return c
        lax.fori_loop(first, first + count, body, 0, unroll=unroll)

    def attention_weights(ms, joint):
        keys = KP if joint else R
        put(QKV, sum(dot(nT[m, :, 0:R], qT[m], 1, 1) for m in ms))

        def body(k, c):
            put(QKV + 1 + k, sum(dot(nT[m, :, 0:keys], kvT[m, cols(k), 0:keys], 1, 1) for m in ms))
            return c
        lax.fori_loop(0, 2, body, 0)
        put(OUT, sum(dot(attT[m], gb[m], 1, 0) for m in ms))

    def small_sums():
        rows = [sm[i:i + 1] for i in range(6)] + [sb[:, k * D:(k + 1) * D] for k in range(FF // D)]
        GS[...] = jnp.zeros_like(GS)
        parts = [row[:, j * BLK:(j + 1) * BLK] for row in rows for j in range(D // BLK)]
        parts += [jnp.zeros((1, BLK), f32)] * (-len(parts) % 16)
        GS[0:len(parts)] = jnp.concatenate(parts, 0).astype(bf16)

    if tree:
        (t_send, t_recv, free) = rest
        dp = lax.axis_index("dp")
        bits = lax.axis_size("dp").bit_length() - 1
        bit = [lax.rem(dp // (1 << k), 2) for k in range(bits)]
        partner = [{"dp": dp + (1 - 2 * bit[k]) * (1 << k)} for k in range(bits)]

        def refs(g):
            return (GS, VS) if g == UNITS else (G.at[g], V.at[g])

        def order(g):
            return (0,) + tuple(range(2, bits)) + (1,) if g in LINE_FIRST else tuple(range(bits))

        def rows_of(ref, first, size):
            return ref.at[pl.ds(first, size)]

        def height(g):
            return GS.shape[0] if g == UNITS else D

        def offset(g, k):
            total = sum((bit[order(g)[j]] * (height(g) >> (j + 1)) for j in range(k + 1)), 0)
            return pl.multiple_of(total, 16)

        def tree_copy(g, k):
            mine, theirs = refs(g)
            rows = height(g)
            if k < bits:
                size = rows >> (k + 1)
                away = 1 - bit[order(g)[k]]
                src = rows_of(mine, pl.multiple_of(offset(g, k - 1) + away * size, 16), size)
                dst = rows_of(theirs, rows - (rows >> k), size)
                to = partner[order(g)[k]]
            else:
                j = 2 * bits - 1 - k
                size = rows >> (j + 1)
                src = dst = rows_of(mine, offset(g, j), size)
                to = partner[order(g)[j]]
            return pltpu.make_async_remote_copy(src_ref=src, dst_ref=dst, send_sem=t_send.at[g, k],
                                                recv_sem=t_recv.at[g, k], device_id=to, device_id_type=MESH)

        def event(g, k):
            rows = height(g)
            if k > 0:
                tree_copy(g, k - 1).wait_recv()
            if 0 < k <= bits:
                tree_copy(g, k - 1).wait_send()
                pl.semaphore_signal(free.at[g, k - 1], inc=1, device_id=partner[order(g)[k - 1]], device_id_type=MESH)
                size = rows >> k
                step = min(size, 64)
                first = offset(g, k - 1)

                def add(i, c):
                    here = pl.ds(pl.multiple_of(first + i * step, 16), step)
                    there = pl.ds(pl.multiple_of(rows - (rows >> (k - 1)) + i * step, 16), step)
                    if g == UNITS:
                        GS[here, :] = (GS[here, :].astype(f32) + VS[there, :].astype(f32)).astype(bf16)
                    else:
                        G[g, here, :] = (G[g, here, :].astype(f32) + V[g, there, :].astype(f32)).astype(bf16)
                    return c
                lax.fori_loop(0, size // step, add, 0)
            if bits <= k < 2 * bits:
                pl.semaphore_wait(free.at[g, 2 * bits - 1 - k], 1)
            if k < 2 * bits:
                tree_copy(g, k).start()

        def settle():
            for g in range(UNITS + 1):
                for k in range(bits, 2 * bits):
                    tree_copy(g, k).wait_send()

    def run(tokens):
        if tree:
            for token in tokens:
                event(token // 10, token % 10)

    @pl.when(sec == 0)
    def _():
        in_copy(0, h).start()
        w_copy(0).start()

    @pl.when(sec == 1)
    def _():
        for k in range(4):
            w_copy(k).start()
        for m in range(micro):
            in_copy(m, dy).start()

    barrier = pltpu.get_barrier_semaphore()
    greeted = [peer] + (partner if tree else [])
    for device in greeted:
        pl.semaphore_signal(barrier, inc=1, device_id=device, device_id_type=MESH)
    sm[...] = jnp.zeros_like(sm)
    sb[...] = jnp.zeros_like(sb)

    @pl.when(sec == 0)
    def _():
        def forward(m, c):
            in_copy(m, h).wait()

            @pl.when(m == 0)
            def _():
                w_copy(0).wait()
                for k in range(1, 4):
                    w_copy(k).start()
                for j in range(1, micro):
                    in_copy(j, h).start()

            def view(i, c):
                qkv_block(m, i)
                view_attention(m, i)

                @pl.when((m == 0) & (i == 0))
                def _():
                    w_copy(1).wait()
                    w_copy(2).wait()

                def late():
                    @pl.when((m == 0) & (i == 0))
                    def _():
                        w_copy(3).wait()
                mlp_block(m, i, late)

                @pl.when((m == 0) & (i == 0))
                def _():
                    pl.semaphore_wait(barrier, len(greeted))

                @pl.when((m > 0) & (i == 0))
                def _():
                    for j in range(NB):
                        act_copy(m - 1, j).wait_send()
                act_copy(m, i).start()
                return c
            lax.fori_loop(0, NB, view, 0)
            return c
        lax.fori_loop(0, micro, forward, 0)
        for j in range(NB):
            act_copy(micro - 1, j).wait_send()

        G[...] = jnp.zeros_like(G)

        def backward(m, c):
            final = m == micro - 1

            def when_final(tokens):
                if tree and tokens:
                    @pl.when(final)
                    def _():
                        run(tokens)

            def body(i, c):
                last = i == NB - 1

                @pl.when(last)
                def _():
                    down_weights([m], 0, FF // D, 1, slice(0, R - BLK))
                grad_copy(m, i).wait_recv()

                @pl.when(last)
                def _():
                    down_weights([m], 0, 2, 2, slice(R - BLK, R))
                    when_final((0, 10) + AFTER_DOWN)
                    down_weights([m], 2, 2, 2, slice(R - BLK, R))
                    when_final((20, 30) + AFTER_DOWN2)
                mlp_back_block(m, i)
                return c
            lax.fori_loop(0, NB, body, 0)
            when_final(AFTER_BLOCK)
            up_weights([m], 0, 2)
            when_final((40, 50) + AFTER_UP)
            up_weights([m], 2, 2)
            when_final((60, 70) + AFTER_UP2)
            att_grad(m)
            when_final(AFTER_GRAD)
            view_attention_back(m, 0, 2)
            when_final(AFTER_HALF)
            view_attention_back(m, 2, 4)
            when_final(AFTER_VIEWS)
            qkv_back(m, False)
            when_final(AFTER_QKV)
            attention_weights([m], False)
            return c
        lax.fori_loop(0, micro, backward, 0)

    @pl.when(sec == 1)
    def _():
        for k in range(4):
            w_copy(k).wait()
        for m in range(micro):
            in_copy(m, dy).wait()
        pl.semaphore_wait(barrier, len(greeted))
        for m in range(micro):
            lang_phase(m)

        def item(m, c):
            joint_qkv(m)
            joint_attention(m)
            joint_mlp(m)
            joint_mlp_back(m)
            att_grad(m)
            joint_attention_back(m)
            qkv_back(m, True)
            return c
        lax.fori_loop(0, micro, item, 0)
        G[...] = jnp.zeros_like(G)
        down_weights(range(micro), 0, 4)
        run((0, 10, 20, 30))
        up_weights(range(micro), 0, 4)
        run((40, 50, 60, 70) + BEFORE)
        attention_weights(range(micro), True)

    small_sums()
    if tree:
        run((80, 90, 100, 110, 120) + REST)
        settle()

    @pl.when(sec == 1)
    def _():
        for m in range(micro):
            for i in range(NB):
                grad_copy(m, i).wait_send()


def local(section_data, lang_feat, lang_ids, view_mask, norm_gains, shifts, fc1_bias, w_qkv, w_out, w_fc1, w_fc2):
    micro, rows, D = section_data.shape[1], section_data.shape[3], section_data.shape[4]
    FF = w_fc1.shape[2]
    lang = lang_feat.shape[2]
    lang_rows = jnp.transpose(lang_feat, (1, 2, 0, 3))
    KP = rows + -(-lang // 16) * 16
    NB = rows // BLK
    hbm = pl.BlockSpec(memory_space=pl.ANY)
    vmem = pl.BlockSpec(memory_space=pltpu.VMEM)
    smem = pl.BlockSpec(memory_space=pltpu.SMEM)
    V = pltpu.VMEM
    dma = pltpu.SemaphoreType.DMA
    sds = jax.ShapeDtypeStruct
    units = 2 * (FF // D) + 4
    tree = lax.axis_size("dp") == 16 and D % 256 == 0 and units == UNITS
    kept = ((micro, rows, D), (units, D, D), (256, BLK))
    scratch = [
        V((micro, rows, D), bf16),
        V((micro, rows, D), bf16),
        V((D, 3 * D), bf16), V((D, D), bf16), V((D, FF), bf16), V((FF, D), bf16),
        V((micro, D, KP), bf16),
        V((micro, D, rows), bf16),
        V((micro, 2 * D, KP), bf16),
        V((micro, KP, 2 * D), bf16),
        V((HEADS, KP, rows), bf16),
        V((micro, HEADS, 1, rows), f32),
        V((micro, D, rows), bf16),
        V((micro, rows, D), f32),
        V((micro, rows, D), bf16),
        V((micro, rows, FF), bf16),
        V((micro, rows, FF), bf16),
        V((micro, rows, D), bf16),
        V((D, rows), bf16),
        V((micro, KP, BLK), bf16),
        V((micro, KP - rows, D), f32),
        V((8, D), f32), V((1, FF), f32),
    ]
    if tree:
        scratch += [V((units, D - D // 16, D), bf16), V((256 - 16, BLK), bf16)]
    scratch += [dma((micro,)), dma((4,)),
                dma((micro, NB)), dma((micro, NB)), dma((micro, NB)), dma((micro, NB))]
    if tree:
        scratch += [dma((units + 1, 8)), dma((units + 1, 8)),
                    pltpu.SemaphoreType.REGULAR((units + 1, 4))]
    res, *grads = pl.pallas_call(
        step_kernel,
        out_shape=tuple((V if tree else sds)(shape, bf16) for shape in kept),
        in_specs=[hbm, vmem, vmem, smem, vmem, vmem, vmem, hbm, hbm, hbm, hbm],
        out_specs=(vmem,) * 3,
        scratch_shapes=scratch,
        compiler_params=pltpu.CompilerParams(
            collective_id=0, has_side_effects=True, vmem_limit_bytes=VMEM_LIMIT - (KEPT_BYTES if tree else 0)),
        name="two_layers",
    )(section_data, lang_rows, lang_ids, view_mask, norm_gains, shifts, fc1_bias, w_qkv, w_out, w_fc1, w_fc2)
    if not tree:
        grads = lax.psum(grads, "dp")
    return unpack(res, *grads, section_data.shape, FF)


def unpack_kernel(rows, low, small, out_res, gain, shift, b1, gq, go, g1, g2, wide, out_sem, res_sem):
    units, D = low.shape[0], low.shape[1]
    UP = g1.shape[2] // D
    micro = rows.shape[0]
    out = [pltpu.make_async_copy(rows.at[m], out_res.at[0, m, 0], res_sem.at[m]) for m in range(micro)]
    for copy in out:
        copy.start()
    width = D // BLK
    for i in range(6 + UP):
        for j in range(width):
            at = i * width + j
            part = small[at:at + 1].astype(f32)
            if i < 2:
                gain[0, i:i + 1, j * BLK:(j + 1) * BLK] = part
            elif i < 6:
                shift[0, i - 2:i - 1, j * BLK:(j + 1) * BLK] = part
            else:
                b1[0:1, (i - 6) * D + j * BLK:(i - 6) * D + (j + 1) * BLK] = part
    stores = []
    for u in range(units):
        wide[u] = low[u].astype(f32)
        if u < UP:
            dst = g2.at[0, pl.ds(u * D, D)]
        elif u < 2 * UP:
            dst = g1.at[0, :, pl.ds((u - UP) * D, D)]
        elif u < 2 * UP + 3:
            dst = gq.at[0, :, pl.ds((u - 2 * UP) * D, D)]
        else:
            dst = go.at[0]
        stores.append(pltpu.make_async_copy(wide.at[u], dst, out_sem.at[u]))
        stores[-1].start()
    for copy in stores + out:
        copy.wait()


def unpack(rows, low, small, shape, FF):
    sds = jax.ShapeDtypeStruct
    units, D = low.shape[0], low.shape[1]
    hbm = pl.BlockSpec(memory_space=pl.ANY)
    vmem = pl.BlockSpec(memory_space=pltpu.VMEM)
    dma = pltpu.SemaphoreType.DMA
    return pl.pallas_call(
        unpack_kernel,
        in_specs=[vmem, vmem, vmem],
        out_specs=(hbm, vmem, vmem, vmem, hbm, hbm, hbm, hbm),
        out_shape=(sds(shape, bf16), sds((1, 2, D), f32), sds((1, 4, D), f32), sds((1, FF), f32),
                   sds((1, D, 3 * D), f32), sds((1, D, D), f32), sds((1, D, FF), f32), sds((1, FF, D), f32)),
        scratch_shapes=[pltpu.VMEM(low.shape, f32), dma((units,)), dma((rows.shape[0],))],
        compiler_params=pltpu.CompilerParams(vmem_limit_bytes=32 * 2**20),
        name="unpack",
    )(rows, low, small)


def solution(mesh):
    weights = P("section", None, None)
    rows = P("section", None, "dp", None, None)
    return jax.shard_map(
        local,
        mesh=mesh,
        in_specs=(rows, P(None, "dp", None, None), P(None, "dp", None), P(None, "dp", None), weights, weights,
                  P("section", None), weights, weights, weights, weights),
        out_specs=(rows, weights, weights, P("section", None), weights, weights, weights, weights),
        check_vma=False,
    )
```

```python
import functools

import jax
import jax.numpy as jnp
from jax import lax
from jax.experimental import pallas as pl
from jax.experimental.pallas import tpu as pltpu
from jax.sharding import PartitionSpec as P

HEADS = 8
HEAD = 64
VIEWS = 5
BLK = 128
EPS = 1e-05
MASKED = -1e30
SCALE = HEAD**-0.5
LOG2E = 1.4426950408889634
MESH = pl.DeviceIdType.MESH
bf16 = jnp.bfloat16
f32 = jnp.float32
VMEM_LIMIT = 64 * 2**20 - 2**19
KEPT_BYTES = 15 * 2**19
UNITS = 12
LENT = 0
GUEST = 13
LINE_FIRST = (3, 4, 7)
AFTER_DOWN = ()
AFTER_DOWN2 = ()
AFTER_BLOCK = (11,)
AFTER_UP = (31,)
AFTER_UP2 = (51,)
AFTER_GRAD = (41, 1, 71, 21, 12)
AFTER_HALF = ()
AFTER_VIEWS = (32,)
AFTER_QKV = (61, 52, 42)
BEFORE = (AFTER_DOWN + AFTER_DOWN2 + AFTER_BLOCK + AFTER_UP + AFTER_UP2 + AFTER_GRAD + AFTER_HALF + AFTER_VIEWS + AFTER_QKV)
REST = (2, 13, 22, 81, 53, 131, 62, 72, 111, 101, 14, 121, 82, 23, 33, 54, 91, 3, 132, 112, 63, 83, 102, 4, 24, 43, 55, 133, 73, 64, 34, 113, 5, 44, 92, 103, 56, 25, 134, 74, 122, 65, 84, 45, 6, 135, 26, 123, 114, 85, 104, 66, 15, 124, 93, 115, 136, 105, 86, 125, 46, 67, 94, 137, 16, 57, 75, 126, 27, 106, 95, 116, 58, 35, 76, 96, 87, 127, 36, 47, 107, 48, 88, 117, 7, 128, 77, 17, 28, 68, 97, 18, 37, 108, 8, 118, 78, 98, 38)


def dot(a, b, ca, cb):
    return lax.dot_general(a, b, (((ca,), (cb,)), ((), ())), preferred_element_type=f32)


def normalise(v):
    centred = v - jnp.mean(v, -1, keepdims=True)
    r = lax.rsqrt(jnp.mean(centred * centred, -1, keepdims=True) + EPS)
    return centred * r, r


def norm_back(v, grad, gain):
    xhat, r = normalise(v)
    gm = grad * gain
    along = jnp.mean(gm * xhat, -1, keepdims=True)
    dv = r * (gm - jnp.mean(gm, -1, keepdims=True) - xhat * along)
    return dv, jnp.sum(grad * xhat, 0, keepdims=True), jnp.sum(grad, 0, keepdims=True)


def gelu_pair(x):
    phi = 0.5 + 0.5 * lax.erf(x * 0.7071067811865476)
    gelu = x * phi
    return gelu, phi + (x * 0.3989422804014327) * jnp.exp2(x * (x * (-0.5 * LOG2E)))


def blk(i):
    return pl.ds(pl.multiple_of(i * BLK, BLK), BLK)


def step_kernel(sd, lf, ids, vm, ng, sh, fb, wq_h, wo_h, w1_h, w2_h,
                ob, G, GS,
                h, dy, wq, wo, w1, w2, nT, qT, kvT, kv, PT, linv, attT, hm, nm, act, gg, gb, dOT,
                bias, lx, sm, sb, *rest):
    tree = len(rest) > 6
    if tree:
        V, VS, VG, rest = rest[0], rest[1], rest[2], rest[3:]
    (in_sem, w_sem, act_send, act_recv, grad_send, grad_recv), rest = rest[:6], rest[6:]
    sec = lax.axis_index("section")
    D = wo.shape[0]
    FF = w1.shape[1]
    R = h.shape[1]
    NB = R // BLK
    LROWS = lf.shape[1]
    KP = kvT.shape[2]
    LP = KP - R
    micro = h.shape[0]
    peer = {"section": 1 - sec}

    def w_copy(k):
        src, dst = ((wq_h, wq), (wo_h, wo), (w1_h, w1), (w2_h, w2))[k]
        return pltpu.make_async_copy(src.at[0], dst, w_sem.at[k])

    def in_copy(m, dst):
        return pltpu.make_async_copy(sd.at[0, m, 0], dst.at[m], in_sem.at[m])

    def act_copy(m, i):
        return pltpu.make_async_remote_copy(
            src_ref=ob.at[m, blk(i)], dst_ref=h.at[m, blk(i)], send_sem=act_send.at[m, i],
            recv_sem=act_recv.at[m, i], device_id=peer, device_id_type=MESH)

    def grad_copy(m, i):
        return pltpu.make_async_remote_copy(
            src_ref=h.at[m, blk(i)], dst_ref=dy.at[m, blk(i)], send_sem=grad_send.at[m, i],
            recv_sem=grad_recv.at[m, i], device_id=peer, device_id_type=MESH)

    gain0, gain1 = ng[0, 0:1], ng[0, 1:2]
    shift = [sh[0, k:k + 1] for k in range(4)]

    def qkv_block(m, i):
        xhat, _ = normalise(h[m, blk(i)].astype(f32))
        n = (xhat * gain0 + shift[0]).astype(bf16)
        nT[m, :, blk(i)] = n.T
        rows = dot(n, wq[...], 1, 0).astype(bf16)
        qT[m, :, blk(i)] = rows[:, :D].T
        kvT[m, :, blk(i)] = rows[:, D:].T
        kv[m, blk(i), :] = rows[:, D:]

    def joint_qkv(m):
        def body(i, c):
            act_copy(m, i).wait_recv()
            qkv_block(m, i)
            return c
        lax.fori_loop(0, NB, body, 0, unroll=True)

    def lang_phase(m):
        rows = jnp.concatenate([lf[0].astype(f32)[:, m, :], jnp.zeros((LP - LROWS, D), f32)], 0)
        xhat, _ = normalise(rows)
        lx[m] = xhat
        n = (xhat * gain0 + shift[0]).astype(bf16)
        nT[m, :, R:KP] = n.T
        rows = dot(n, wq[:, D:], 1, 0).astype(bf16)
        kvT[m, :, R:KP] = rows.T
        kv[m, R:KP, :] = rows
        for v in range(VIEWS):
            seen = (vm[m, 0, v] > 0).astype(f32)
            bias[m, v * BLK:(v + 1) * BLK, :] = (jnp.full((BLK, BLK), MASKED, f32) * (1.0 - seen)).astype(bf16)
        count = jnp.sum((ids[m] != 0).astype(jnp.int32), -1, keepdims=True)
        place = lax.broadcasted_iota(jnp.int32, (LP, BLK), 0)
        bias[m, R:KP, :] = jnp.where(place < count, 0.0, MASKED).astype(bf16)

    def paired(block):
        zero = jnp.zeros((HEAD, block.shape[1]), block.dtype)
        return jnp.concatenate([jnp.concatenate([block[:HEAD], zero], 0),
                                jnp.concatenate([zero, block[HEAD:]], 0)], 1)

    def joint_attention(m):
        def body(hp, c):
            q2 = paired(qT[m, blk(hp), :])
            s = dot(kv[m, :, blk(hp)], q2, 1, 0)
            s = s + jnp.concatenate([bias[m].astype(f32)] * (2 * NB), 1)
            top = jnp.max(s, 0, keepdims=True) * (SCALE * LOG2E)
            p = jnp.exp2(s * (SCALE * LOG2E) - top)
            inv = 1.0 / jnp.sum(p, 0, keepdims=True)
            pb = p.astype(bf16)
            for j in range(2):
                head = 2 * hp + j
                PT[head] = pb[:, j * R:(j + 1) * R]
                linv[m, head] = inv[:, j * R:(j + 1) * R]
                rows = pl.ds(pl.multiple_of(head * HEAD, HEAD), HEAD)
                vT = kvT[m, pl.ds(pl.multiple_of(D + head * HEAD, HEAD), HEAD), :]
                out = dot(vT, pb[:, j * R:(j + 1) * R], 1, 0) * inv[:, j * R:(j + 1) * R]
                attT[m, rows, :] = out.astype(bf16)
            return c
        lax.fori_loop(0, HEADS // 2, body, 0)

    def view_attention(m, v):
        col = blk(v)
        for hp in range(HEADS // 2):
            pair = slice(hp * BLK, (hp + 1) * BLK)
            q2 = paired(qT[m, pair, col])
            s = dot(kv[m, col, pair], q2, 1, 0)
            top = jnp.max(s, 0, keepdims=True) * (SCALE * LOG2E)
            p = jnp.exp2(s * (SCALE * LOG2E) - top)
            inv = 1.0 / jnp.sum(p, 0, keepdims=True)
            pb = p.astype(bf16)
            PT[4 * m + hp, col, 0:2 * BLK] = pb
            for j in range(2):
                linv[m, 2 * hp + j, :, col] = inv[:, j * BLK:(j + 1) * BLK]
            out = dot(kvT[m, D + hp * BLK:D + (hp + 1) * BLK, col], pb, 1, 0) * inv
            attT[m, pair, col] = jnp.concatenate([out[:HEAD, :BLK], out[HEAD:, BLK:]], 0).astype(bf16)

    def mlp_block(m, i, late):
        mid = h[m, blk(i)].astype(f32) + dot(attT[m, :, blk(i)], wo[...], 0, 0) + shift[1]
        hm[m, blk(i)] = mid
        xhat, _ = normalise(mid)
        n = (xhat * gain1 + shift[2]).astype(bf16)
        nm[m, blk(i)] = n
        for k in range(0, FF, 256):
            a, slope = gelu_pair(dot(n, w1[:, k:k + 256], 1, 0) + fb[:, k:k + 256])
            act[m, blk(i), k:k + 256] = a.astype(bf16)
            gg[m, blk(i), k:k + 256] = slope.astype(bf16)
        late()
        out = mid + dot(act[m, blk(i)], w2[...], 1, 0) + shift[3]
        ob[m, blk(i)] = out.astype(bf16)

    def joint_mlp(m):
        hm[m] = h[m].astype(f32) + dot(attT[m], wo[...], 0, 0) + shift[1]
        for i in range(NB):
            row = slice(i * BLK, (i + 1) * BLK)
            xhat, _ = normalise(hm[m, row])
            nm[m, row] = (xhat * gain1 + shift[2]).astype(bf16)
        for k in range(0, FF, 256):
            a, slope = gelu_pair(dot(nm[m], w1[:, k:k + 256], 1, 0) + fb[:, k:k + 256])
            act[m, :, k:k + 256] = a.astype(bf16)
            gg[m, :, k:k + 256] = slope.astype(bf16)
        ob[m] = (hm[m] + dot(act[m], w2[...], 1, 0) + shift[3]).astype(bf16)

    def mid_back(m, row, gn):
        dv, dgain, dshift = norm_back(hm[m, row], gn, gain1)
        d32 = dy[m, row].astype(f32)
        mid = d32 + dv
        hm[m, row] = mid
        low = mid.astype(bf16)
        gb[m, row] = low
        sm[1:2] += dgain
        sm[4:5] += dshift
        sm[5:6] += jnp.sum(d32, 0, keepdims=True)
        sm[3:4] += jnp.sum(low.astype(f32), 0, keepdims=True)

    def pre_back(m, row, width):
        d = dy[m, row]
        for k in range(0, FF, width):
            gp = (dot(d, w2[k:k + width], 1, 1) * gg[m, row, k:k + width].astype(f32)).astype(bf16)
            gg[m, row, k:k + width] = gp
            sb[:, k:k + width] += jnp.sum(gp.astype(f32), 0, keepdims=True)

    def mlp_back_block(m, i):
        pre_back(m, blk(i), 512)
        mid_back(m, blk(i), dot(gg[m, blk(i)], w1[...], 1, 1))

    def joint_mlp_back(m):
        pre_back(m, slice(0, R), 256)
        gn = dot(gg[m], w1[...], 1, 1)
        for i in range(NB):
            row = slice(i * BLK, (i + 1) * BLK)
            mid_back(m, row, gn[row])

    def att_grad(m):
        dOT[...] = dot(wo[...], gb[m], 1, 1).astype(bf16)

    def joint_attention_back(m):
        def body(hp, c):
            pair = blk(hp)
            inv = jnp.concatenate([linv[m, 2 * hp], linv[m, 2 * hp + 1]], 1)
            d2 = (paired(dOT[pair, :]).astype(f32) * inv).astype(bf16)
            vcol = pl.ds(pl.multiple_of(D + hp * BLK, BLK), BLK)
            dp = dot(kv[m, :, vcol], d2, 1, 0)
            pb = jnp.concatenate([PT[2 * hp], PT[2 * hp + 1]], 1)
            p = pb.astype(f32)
            inner = jnp.sum(p * dp, 0, keepdims=True) * inv
            ds = (p * (dp - inner)).astype(bf16)
            q2 = paired(qT[m, pair, :])
            kvT[m, vcol, :] = dot(d2, pb, 1, 1).astype(bf16)
            dq = dot(kvT[m, pair, :], ds, 1, 0) * SCALE
            dq0, dq1 = dq[:HEAD, :R], dq[HEAD:, R:]
            kvT[m, pair, :] = (dot(q2, ds, 1, 1) * SCALE).astype(bf16)
            qT[m, pair, :] = jnp.concatenate([dq0, dq1], 0).astype(bf16)
            return c
        lax.fori_loop(0, HEADS // 2, body, 0)

    def view_attention_back(m, first, last):
        def body(hp, c):
            vrow = pl.ds(pl.multiple_of(D + hp * BLK, BLK), BLK)
            pair = blk(hp)
            for v in range(NB):
                col = slice(v * BLK, (v + 1) * BLK)
                inv = jnp.concatenate([linv[m, 2 * hp, :, col], linv[m, 2 * hp + 1, :, col]], 1)
                d2 = (paired(dOT[pair, col]).astype(f32) * inv).astype(bf16)
                dp = dot(kv[m, col, vrow], d2, 1, 0)
                pb = PT[4 * m + hp, col, 0:2 * BLK]
                p = pb.astype(f32)
                inner = jnp.sum(p * dp, 0, keepdims=True) * inv
                ds = (p * (dp - inner)).astype(bf16)
                q2 = paired(qT[m, pair, col])
                dv = dot(d2, pb, 1, 1).astype(bf16)
                dq = dot(kvT[m, pair, col], ds, 1, 0) * SCALE
                dk = (dot(q2, ds, 1, 1) * SCALE).astype(bf16)
                kvT[m, vrow, col] = dv
                kvT[m, pair, col] = dk
                qT[m, pair, col] = jnp.concatenate([dq[:HEAD, :BLK], dq[HEAD:, BLK:]], 0).astype(bf16)
            return c
        lax.fori_loop(first, last, body, 0)

    def qkv_back(m, joint):
        for first, last in ((0, 1), (1, NB)):
            rows = slice(first * BLK, last * BLK)
            gn = dot(qT[m, :, rows], wq[:, :D], 0, 1) + dot(kvT[m, :, rows], wq[:, D:], 0, 1)
            for i in range(first, last):
                row = slice(i * BLK, (i + 1) * BLK)
                part = gn[(i - first) * BLK:(i - first + 1) * BLK]
                dv, dgain, dshift = norm_back(h[m, row].astype(f32), part, gain0)
                sm[0:1] += dgain
                sm[2:3] += dshift
                out = (hm[m, row] + dv).astype(bf16)
                if joint:
                    h[m, row] = out
                    grad_copy(m, i).start()
                else:
                    ob[m, row] = out
        if joint:
            gn = dot(kvT[m, :, R:KP], wq[:, D:], 0, 1)
            sm[0:1] += jnp.sum(gn * lx[m], 0, keepdims=True)
            sm[2:3] += jnp.sum(gn, 0, keepdims=True)

    UP, QKV, OUT = FF // D, 2 * (FF // D), 2 * (FF // D) + 3

    def cols(k):
        return pl.ds(pl.multiple_of(k * D, D), D)

    def put(u, t):
        G[u] = (G[u].astype(f32) + t).astype(bf16)

    def down_weights(ms, first, count, unroll=1, rows=slice(None)):
        def body(k, c):
            put(k, sum(dot(act[m, rows, cols(k)], dy[m, rows], 0, 0) for m in ms))
            return c
        lax.fori_loop(first, first + count, body, 0, unroll=unroll)

    def up_weights(ms, first, count, unroll=1):
        def body(k, c):
            put(UP + k, sum(dot(nm[m], gg[m, :, cols(k)], 0, 0) for m in ms))
            return c
        lax.fori_loop(first, first + count, body, 0, unroll=unroll)

    def attention_weights(ms, joint):
        keys = KP if joint else R
        put(QKV, sum(dot(nT[m, :, 0:R], qT[m], 1, 1) for m in ms))

        def body(k, c):
            put(QKV + 1 + k, sum(dot(nT[m, :, 0:keys], kvT[m, cols(k), 0:keys], 1, 1) for m in ms))
            return c
        lax.fori_loop(0, 2, body, 0)
        put(OUT, sum(dot(attT[m], gb[m], 1, 0) for m in ms))

    def small_sums():
        rows = [sm[i:i + 1] for i in range(6)] + [sb[:, k * D:(k + 1) * D] for k in range(FF // D)]
        GS[...] = jnp.zeros_like(GS)
        parts = [row[:, j * BLK:(j + 1) * BLK] for row in rows for j in range(D // BLK)]
        parts += [jnp.zeros((1, BLK), f32)] * (-len(parts) % 16)
        GS[0:len(parts)] = jnp.concatenate(parts, 0).astype(bf16)

    if tree:
        (t_send, t_recv, free) = rest
        dp = lax.axis_index("dp")
        bits = lax.axis_size("dp").bit_length() - 1
        bit = [lax.rem(dp // (1 << k), 2) for k in range(bits)]
        partner = [{"dp": dp + (1 - 2 * bit[k]) * (1 << k)} for k in range(bits)]

        def refs(g):
            return (GS, VS) if g == UNITS else (G.at[g], V.at[g])

        def order(g):
            return (0,) + tuple(range(2, bits)) + (1,) if g in LINE_FIRST else tuple(range(bits))

        def rows_of(ref, first, size):
            return ref.at[pl.ds(first, size)]

        def height(g):
            return GS.shape[0] if g == UNITS else D

        def offset(g, k):
            total = sum((bit[order(g)[j]] * (height(g) >> (j + 1)) for j in range(k + 1)), 0)
            return pl.multiple_of(total, 16)

        def tree_copy(g, k):
            mine, theirs = refs(g)
            rows = height(g)
            if k < bits:
                size = rows >> (k + 1)
                away = 1 - bit[order(g)[k]]
                src = rows_of(mine, pl.multiple_of(offset(g, k - 1) + away * size, 16), size)
                dst = rows_of(theirs, rows - (rows >> k), size)
                to = partner[order(g)[k]]
            else:
                j = 2 * bits - 1 - k
                size = rows >> (j + 1)
                src = dst = rows_of(mine, offset(g, j), size)
                to = partner[order(g)[j]]
            return pltpu.make_async_remote_copy(src_ref=src, dst_ref=dst, send_sem=t_send.at[g, k],
                                                recv_sem=t_recv.at[g, k], device_id=to, device_id_type=MESH)

        def add_rows(put_to, first, taken, there, size):
            step = min(size, 64)

            def add(i, c):
                here = pl.ds(pl.multiple_of(first + i * step, 16), step)
                part = pl.ds(pl.multiple_of(there + i * step, 16), step)
                put_to[here, :] = (put_to[here, :].astype(f32) + taken[part, :].astype(f32)).astype(bf16)
                return c
            lax.fori_loop(0, size // step, add, 0)

        def take(g, k):
            tree_copy(g, k - 1).wait_recv()
            if k <= bits:
                tree_copy(g, k - 1).wait_send()
                pl.semaphore_signal(free.at[g, k - 1], inc=1, device_id=partner[order(g)[k - 1]], device_id_type=MESH)
                rows = height(g)
                mine, theirs = refs(g)
                add_rows(mine, offset(g, k - 1), theirs, rows - (rows >> (k - 1)), rows >> k)

        def give(g, k):
            if k >= bits:
                pl.semaphore_wait(free.at[g, 2 * bits - 1 - k], 1)
            if k < 2 * bits:
                tree_copy(g, k).start()

        def event(g, k):
            if g == GUEST:
                pl.when(sec == 1)(functools.partial(guest_event, k))
            elif g == LENT and 0 < k < 2 * bits:
                lent_event(k)
            else:
                if k > 0:
                    take(g, k)
                if k < 2 * bits:
                    give(g, k)

        half = D // 2
        guest = PT.at[0, pl.ds(0, half), pl.ds(0, D)]
        lent = G.at[LENT, pl.ds(pl.multiple_of(bit[0] * half, 16), half)]

        def lend():
            return pltpu.make_async_remote_copy(src_ref=lent, dst_ref=guest, send_sem=t_send.at[GUEST, 0],
                                                recv_sem=t_recv.at[GUEST, 0], device_id=peer, device_id_type=MESH)

        def hand_back():
            return pltpu.make_async_remote_copy(src_ref=guest, dst_ref=lent, send_sem=t_send.at[GUEST, 7],
                                                recv_sem=t_recv.at[GUEST, 7], device_id=peer, device_id_type=MESH)

        def lent_event(k):
            if k == 1:
                take(LENT, 1)

                @pl.when(sec == 0)
                def _():
                    lend().start()

                @pl.when(sec == 1)
                def _():
                    give(LENT, 1)
            elif k < 2 * bits - 1:
                @pl.when(sec == 1)
                def _():
                    take(LENT, k)
                    give(LENT, k)
                if k == 4:
                    @pl.when(sec == 0)
                    def _():
                        lend().wait_send()
                        pl.semaphore_signal(free.at[GUEST, 0], inc=1, device_id=peer, device_id_type=MESH)
            else:
                @pl.when(sec == 0)
                def _():
                    hand_back().wait_recv()

                @pl.when(sec == 1)
                def _():
                    take(LENT, k)
                give(LENT, k)

        def guest_offset(k):
            total = sum((bit[j] * (D >> (j + 1)) for j in range(1, k + 1)), 0)
            return pl.multiple_of(total, 16)

        def guest_copy(k):
            j = k if k < bits else 2 * bits - 1 - k
            size = D >> (j + 1)
            if k < bits:
                first = pl.multiple_of(guest_offset(k - 1) + (1 - bit[k]) * size, 16)
                dst = VG.at[pl.ds(half - (half >> (k - 1)), size)]
            else:
                first = guest_offset(j)
                dst = PT.at[0, pl.ds(first, size), pl.ds(0, D)]
            return pltpu.make_async_remote_copy(
                src_ref=PT.at[0, pl.ds(first, size), pl.ds(0, D)], dst_ref=dst, send_sem=t_send.at[GUEST, k],
                recv_sem=t_recv.at[GUEST, k], device_id=partner[j], device_id_type=MESH)

        def guest_event(k):
            if k == 1:
                lend().wait_recv()
            else:
                guest_copy(k - 1).wait_recv()
                if k <= bits:
                    guest_copy(k - 1).wait_send()
                    pl.semaphore_signal(free.at[GUEST, k - 1], inc=1, device_id=partner[k - 1], device_id_type=MESH)
                    add_rows(guest, guest_offset(k - 1), VG, half - (half >> (k - 2)), D >> k)
            if k < 2 * bits - 1:
                if k >= bits:
                    pl.semaphore_wait(free.at[GUEST, 2 * bits - 1 - k], 1)
                guest_copy(k).start()
            else:
                pl.semaphore_wait(free.at[GUEST, 0], 1)
                hand_back().start()

        def settle():
            for g in range(UNITS + 1):
                for k in range(bits, 2 * bits):
                    if g == LENT and k < 2 * bits - 1:
                        pl.when(sec == 1)(tree_copy(g, k).wait_send)
                    else:
                        tree_copy(g, k).wait_send()

            @pl.when(sec == 1)
            def _():
                for k in range(bits, 2 * bits - 1):
                    guest_copy(k).wait_send()
                hand_back().wait_send()

    def run(tokens):
        if tree:
            for token in tokens:
                event(token // 10, token % 10)

    @pl.when(sec == 0)
    def _():
        in_copy(0, h).start()
        w_copy(0).start()

    @pl.when(sec == 1)
    def _():
        for k in range(4):
            w_copy(k).start()
        for m in range(micro):
            in_copy(m, dy).start()

    barrier = pltpu.get_barrier_semaphore()
    greeted = [peer] + (partner if tree else [])
    for device in greeted:
        pl.semaphore_signal(barrier, inc=1, device_id=device, device_id_type=MESH)
    sm[...] = jnp.zeros_like(sm)
    sb[...] = jnp.zeros_like(sb)

    @pl.when(sec == 0)
    def _():
        def forward(m, c):
            in_copy(m, h).wait()

            @pl.when(m == 0)
            def _():
                w_copy(0).wait()
                for k in range(1, 4):
                    w_copy(k).start()
                for j in range(1, micro):
                    in_copy(j, h).start()

            def view(i, c):
                qkv_block(m, i)
                view_attention(m, i)

                @pl.when((m == 0) & (i == 0))
                def _():
                    w_copy(1).wait()
                    w_copy(2).wait()

                def late():
                    @pl.when((m == 0) & (i == 0))
                    def _():
                        w_copy(3).wait()
                mlp_block(m, i, late)

                @pl.when((m == 0) & (i == 0))
                def _():
                    pl.semaphore_wait(barrier, len(greeted))

                @pl.when((m > 0) & (i == 0))
                def _():
                    for j in range(NB):
                        act_copy(m - 1, j).wait_send()
                act_copy(m, i).start()
                return c
            lax.fori_loop(0, NB, view, 0)
            return c
        lax.fori_loop(0, micro, forward, 0)
        for j in range(NB):
            act_copy(micro - 1, j).wait_send()

        G[...] = jnp.zeros_like(G)

        def backward(m, c):
            final = m == micro - 1

            def when_final(tokens):
                if tree and tokens:
                    @pl.when(final)
                    def _():
                        run(tokens)

            def body(i, c):
                last = i == NB - 1

                @pl.when(last)
                def _():
                    down_weights([m], 0, FF // D, 1, slice(0, R - BLK))
                grad_copy(m, i).wait_recv()

                @pl.when(last)
                def _():
                    down_weights([m], 0, 2, 2, slice(R - BLK, R))
                    when_final((0, 10) + AFTER_DOWN)
                    down_weights([m], 2, 2, 2, slice(R - BLK, R))
                    when_final((20, 30) + AFTER_DOWN2)
                mlp_back_block(m, i)
                return c
            lax.fori_loop(0, NB, body, 0)
            when_final(AFTER_BLOCK)
            up_weights([m], 0, 2)
            when_final((40, 50) + AFTER_UP)
            up_weights([m], 2, 2)
            when_final((60, 70) + AFTER_UP2)
            att_grad(m)
            when_final(AFTER_GRAD)
            view_attention_back(m, 0, 2)
            when_final(AFTER_HALF)
            view_attention_back(m, 2, 4)
            when_final(AFTER_VIEWS)
            qkv_back(m, False)
            when_final(AFTER_QKV)
            attention_weights([m], False)
            return c
        lax.fori_loop(0, micro, backward, 0)

    @pl.when(sec == 1)
    def _():
        for k in range(4):
            w_copy(k).wait()
        for m in range(micro):
            in_copy(m, dy).wait()
        pl.semaphore_wait(barrier, len(greeted))
        for m in range(micro):
            lang_phase(m)

        def item(m, c):
            joint_qkv(m)
            joint_attention(m)
            joint_mlp(m)
            joint_mlp_back(m)
            att_grad(m)
            joint_attention_back(m)
            qkv_back(m, True)
            return c
        lax.fori_loop(0, micro, item, 0)
        G[...] = jnp.zeros_like(G)
        down_weights(range(micro), 0, 4)
        run((0, 10, 20, 30))
        up_weights(range(micro), 0, 4)
        run((40, 50, 60, 70) + BEFORE)
        attention_weights(range(micro), True)

    small_sums()
    if tree:
        run((80, 90, 100, 110, 120) + REST)
        settle()

    @pl.when(sec == 1)
    def _():
        for m in range(micro):
            for i in range(NB):
                grad_copy(m, i).wait_send()


def local(section_data, lang_feat, lang_ids, view_mask, norm_gains, shifts, fc1_bias, w_qkv, w_out, w_fc1, w_fc2):
    micro, rows, D = section_data.shape[1], section_data.shape[3], section_data.shape[4]
    FF = w_fc1.shape[2]
    lang = lang_feat.shape[2]
    lang_rows = jnp.transpose(lang_feat, (1, 2, 0, 3))
    KP = rows + -(-lang // 16) * 16
    NB = rows // BLK
    hbm = pl.BlockSpec(memory_space=pl.ANY)
    vmem = pl.BlockSpec(memory_space=pltpu.VMEM)
    smem = pl.BlockSpec(memory_space=pltpu.SMEM)
    V = pltpu.VMEM
    dma = pltpu.SemaphoreType.DMA
    sds = jax.ShapeDtypeStruct
    units = 2 * (FF // D) + 4
    tree = lax.axis_size("dp") == 16 and D % 256 == 0 and units == UNITS
    kept = ((micro, rows, D), (units, D, D), (256, BLK))
    scratch = [
        V((micro, rows, D), bf16),
        V((micro, rows, D), bf16),
        V((D, 3 * D), bf16), V((D, D), bf16), V((D, FF), bf16), V((FF, D), bf16),
        V((micro, D, KP), bf16),
        V((micro, D, rows), bf16),
        V((micro, 2 * D, KP), bf16),
        V((micro, KP, 2 * D), bf16),
        V((HEADS, KP, rows), bf16),
        V((micro, HEADS, 1, rows), f32),
        V((micro, D, rows), bf16),
        V((micro, rows, D), f32),
        V((micro, rows, D), bf16),
        V((micro, rows, FF), bf16),
        V((micro, rows, FF), bf16),
        V((micro, rows, D), bf16),
        V((D, rows), bf16),
        V((micro, KP, BLK), bf16),
        V((micro, KP - rows, D), f32),
        V((8, D), f32), V((1, FF), f32),
    ]
    if tree:
        scratch += [V((units, D - D // 16, D), bf16), V((256 - 16, BLK), bf16),
                    V((D // 2 - D // 16, D), bf16)]
    scratch += [dma((micro,)), dma((4,)),
                dma((micro, NB)), dma((micro, NB)), dma((micro, NB)), dma((micro, NB))]
    if tree:
        scratch += [dma((units + 2, 8)), dma((units + 2, 8)),
                    pltpu.SemaphoreType.REGULAR((units + 2, 4))]
    res, *grads = pl.pallas_call(
        step_kernel,
        out_shape=tuple((V if tree else sds)(shape, bf16) for shape in kept),
        in_specs=[hbm, vmem, vmem, smem, vmem, vmem, vmem, hbm, hbm, hbm, hbm],
        out_specs=(vmem,) * 3,
        scratch_shapes=scratch,
        compiler_params=pltpu.CompilerParams(
            collective_id=0, has_side_effects=True, vmem_limit_bytes=VMEM_LIMIT - (KEPT_BYTES if tree else 0)),
        name="two_layers",
    )(section_data, lang_rows, lang_ids, view_mask, norm_gains, shifts, fc1_bias, w_qkv, w_out, w_fc1, w_fc2)
    if not tree:
        grads = lax.psum(grads, "dp")
    return unpack(res, *grads, section_data.shape, FF)


def unpack_kernel(rows, low, small, out_res, gain, shift, b1, gq, go, g1, g2, wide, out_sem, res_sem):
    units, D = low.shape[0], low.shape[1]
    UP = g1.shape[2] // D
    micro = rows.shape[0]
    out = [pltpu.make_async_copy(rows.at[m], out_res.at[0, m, 0], res_sem.at[m]) for m in range(micro)]
    for copy in out:
        copy.start()
    width = D // BLK
    for i in range(6 + UP):
        for j in range(width):
            at = i * width + j
            part = small[at:at + 1].astype(f32)
            if i < 2:
                gain[0, i:i + 1, j * BLK:(j + 1) * BLK] = part
            elif i < 6:
                shift[0, i - 2:i - 1, j * BLK:(j + 1) * BLK] = part
            else:
                b1[0:1, (i - 6) * D + j * BLK:(i - 6) * D + (j + 1) * BLK] = part
    stores = []
    for u in range(units):
        wide[u] = low[u].astype(f32)
        if u < UP:
            dst = g2.at[0, pl.ds(u * D, D)]
        elif u < 2 * UP:
            dst = g1.at[0, :, pl.ds((u - UP) * D, D)]
        elif u < 2 * UP + 3:
            dst = gq.at[0, :, pl.ds((u - 2 * UP) * D, D)]
        else:
            dst = go.at[0]
        stores.append(pltpu.make_async_copy(wide.at[u], dst, out_sem.at[u]))
        stores[-1].start()
    for copy in stores + out:
        copy.wait()


def unpack(rows, low, small, shape, FF):
    sds = jax.ShapeDtypeStruct
    units, D = low.shape[0], low.shape[1]
    hbm = pl.BlockSpec(memory_space=pl.ANY)
    vmem = pl.BlockSpec(memory_space=pltpu.VMEM)
    dma = pltpu.SemaphoreType.DMA
    return pl.pallas_call(
        unpack_kernel,
        in_specs=[vmem, vmem, vmem],
        out_specs=(hbm, vmem, vmem, vmem, hbm, hbm, hbm, hbm),
        out_shape=(sds(shape, bf16), sds((1, 2, D), f32), sds((1, 4, D), f32), sds((1, FF), f32),
                   sds((1, D, 3 * D), f32), sds((1, D, D), f32), sds((1, D, FF), f32), sds((1, FF, D), f32)),
        scratch_shapes=[pltpu.VMEM(low.shape, f32), dma((units,)), dma((rows.shape[0],))],
        compiler_params=pltpu.CompilerParams(vmem_limit_bytes=32 * 2**20),
        name="unpack",
    )(rows, low, small)


def solution(mesh):
    weights = P("section", None, None)
    rows = P("section", None, "dp", None, None)
    return jax.shard_map(
        local,
        mesh=mesh,
        in_specs=(rows, P(None, "dp", None, None), P(None, "dp", None), P(None, "dp", None), weights, weights,
                  P("section", None), weights, weights, weights, weights),
        out_specs=(rows, weights, weights, P("section", None), weights, weights, weights, weights),
        check_vma=False,
    )
```

```python
import functools

import jax
import jax.numpy as jnp
from jax import lax
from jax.experimental import pallas as pl
from jax.experimental.pallas import tpu as pltpu
from jax.sharding import PartitionSpec as P

HEADS = 8
HEAD = 64
VIEWS = 5
BLK = 128
EPS = 1e-05
MASKED = -1e30
SCALE = HEAD**-0.5
LOG2E = 1.4426950408889634
MESH = pl.DeviceIdType.MESH
bf16 = jnp.bfloat16
f32 = jnp.float32
VMEM_LIMIT = 64 * 2**20 - 2**19
KEPT_BYTES = 15 * 2**19
UNITS = 12
LENT = 0
GUEST = 13
LINE_FIRST = (3, 4, 7)
AFTER_DOWN = ()
AFTER_DOWN2 = ()
AFTER_BLOCK = (11,)
AFTER_UP = (31,)
AFTER_UP2 = (51,)
AFTER_GRAD = (41, 1, 71, 21, 12)
AFTER_HALF = ()
AFTER_VIEWS = (32,)
AFTER_QKV = (61, 52, 42)
BEFORE = (AFTER_DOWN + AFTER_DOWN2 + AFTER_BLOCK + AFTER_UP + AFTER_UP2 + AFTER_GRAD + AFTER_HALF + AFTER_VIEWS + AFTER_QKV)
REST = (2, 13, 22, 81, 53, 131, 62, 72, 111, 101, 14, 121, 82, 23, 33, 54, 91, 3, 132, 112, 63, 83, 102, 4, 24, 43, 55, 133, 73, 64, 34, 113, 5, 44, 92, 103, 56, 25, 134, 74, 122, 65, 84, 45, 6, 135, 26, 123, 114, 85, 104, 66, 15, 124, 93, 115, 136, 105, 86, 125, 46, 67, 94, 137, 16, 57, 75, 126, 27, 106, 95, 116, 58, 35, 76, 96, 87, 127, 36, 47, 107, 48, 88, 117, 7, 128, 77, 17, 28, 68, 97, 18, 37, 108, 8, 118, 78, 98, 38)


def dot(a, b, ca, cb):
    return lax.dot_general(a, b, (((ca,), (cb,)), ((), ())), preferred_element_type=f32)


def normalise(v):
    centred = v - jnp.mean(v, -1, keepdims=True)
    r = lax.rsqrt(jnp.mean(centred * centred, -1, keepdims=True) + EPS)
    return centred * r, r


def norm_back(v, grad, gain):
    xhat, r = normalise(v)
    gm = grad * gain
    along = jnp.mean(gm * xhat, -1, keepdims=True)
    dv = r * (gm - jnp.mean(gm, -1, keepdims=True) - xhat * along)
    return dv, jnp.sum(grad * xhat, 0, keepdims=True), jnp.sum(grad, 0, keepdims=True)


def gelu_pair(x):
    phi = 0.5 + 0.5 * lax.erf(x * 0.7071067811865476)
    gelu = x * phi
    return gelu, phi + (x * 0.3989422804014327) * jnp.exp2(x * (x * (-0.5 * LOG2E)))


def blk(i):
    return pl.ds(pl.multiple_of(i * BLK, BLK), BLK)


def step_kernel(sd, lf, ids, vm, ng, sh, fb, wq_h, wo_h, w1_h, w2_h,
                ob, G, GS,
                h, dy, wq, wo, w1, w2, nT, qT, kvT, kv, PT, linv, attT, hm, nm, act, gg, gb, dOT,
                bias, lx, sm, sb, *rest):
    tree = len(rest) > 6
    if tree:
        V, VS, VG, rest = rest[0], rest[1], rest[2], rest[3:]
    (in_sem, w_sem, act_send, act_recv, grad_send, grad_recv), rest = rest[:6], rest[6:]
    sec = lax.axis_index("section")
    D = wo.shape[0]
    FF = w1.shape[1]
    R = h.shape[1]
    NB = R // BLK
    LROWS = lf.shape[1]
    KP = kvT.shape[2]
    LP = KP - R
    micro = h.shape[0]
    peer = {"section": 1 - sec}

    def w_copy(k):
        src, dst = ((wq_h, wq), (wo_h, wo), (w1_h, w1), (w2_h, w2))[k]
        return pltpu.make_async_copy(src.at[0], dst, w_sem.at[k])

    def in_copy(m, dst):
        return pltpu.make_async_copy(sd.at[0, m, 0], dst.at[m], in_sem.at[m])

    def act_copy(m, i):
        return pltpu.make_async_remote_copy(
            src_ref=ob.at[m, blk(i)], dst_ref=h.at[m, blk(i)], send_sem=act_send.at[m, i],
            recv_sem=act_recv.at[m, i], device_id=peer, device_id_type=MESH)

    def grad_copy(m, i):
        return pltpu.make_async_remote_copy(
            src_ref=h.at[m, blk(i)], dst_ref=dy.at[m, blk(i)], send_sem=grad_send.at[m, i],
            recv_sem=grad_recv.at[m, i], device_id=peer, device_id_type=MESH)

    gain0, gain1 = ng[0, 0:1], ng[0, 1:2]
    shift = [sh[0, k:k + 1] for k in range(4)]

    def qkv_block(m, i):
        xhat, _ = normalise(h[m, blk(i)].astype(f32))
        n = (xhat * gain0 + shift[0]).astype(bf16)
        nT[m, :, blk(i)] = n.T
        rows = dot(n, wq[...], 1, 0).astype(bf16)
        qT[m, :, blk(i)] = rows[:, :D].T
        kvT[m, :, blk(i)] = rows[:, D:].T
        kv[m, blk(i), :] = rows[:, D:]

    def joint_qkv(m):
        def body(i, c):
            act_copy(m, i).wait_recv()
            qkv_block(m, i)
            return c
        lax.fori_loop(0, NB, body, 0, unroll=True)

    def lang_phase(m):
        rows = jnp.concatenate([lf[0].astype(f32)[:, m, :], jnp.zeros((LP - LROWS, D), f32)], 0)
        xhat, _ = normalise(rows)
        lx[m] = xhat
        n = (xhat * gain0 + shift[0]).astype(bf16)
        nT[m, :, R:KP] = n.T
        rows = dot(n, wq[:, D:], 1, 0).astype(bf16)
        kvT[m, :, R:KP] = rows.T
        kv[m, R:KP, :] = rows
        for v in range(VIEWS):
            seen = (vm[m, 0, v] > 0).astype(f32)
            bias[m, v * BLK:(v + 1) * BLK, :] = (jnp.full((BLK, BLK), MASKED, f32) * (1.0 - seen)).astype(bf16)
        count = jnp.sum((ids[m] != 0).astype(jnp.int32), -1, keepdims=True)
        place = lax.broadcasted_iota(jnp.int32, (LP, BLK), 0)
        bias[m, R:KP, :] = jnp.where(place < count, 0.0, MASKED).astype(bf16)

    def paired(block):
        zero = jnp.zeros((HEAD, block.shape[1]), block.dtype)
        return jnp.concatenate([jnp.concatenate([block[:HEAD], zero], 0),
                                jnp.concatenate([zero, block[HEAD:]], 0)], 1)

    def joint_attention(m):
        def body(hp, c):
            q2 = paired(qT[m, blk(hp), :])
            s = dot(kv[m, :, blk(hp)], q2, 1, 0)
            s = s + jnp.concatenate([bias[m].astype(f32)] * (2 * NB), 1)
            top = jnp.max(s, 0, keepdims=True) * (SCALE * LOG2E)
            p = jnp.exp2(s * (SCALE * LOG2E) - top)
            inv = 1.0 / jnp.sum(p, 0, keepdims=True)
            pb = p.astype(bf16)
            for j in range(2):
                head = 2 * hp + j
                PT[head] = pb[:, j * R:(j + 1) * R]
                linv[m, head] = inv[:, j * R:(j + 1) * R]
                rows = pl.ds(pl.multiple_of(head * HEAD, HEAD), HEAD)
                vT = kvT[m, pl.ds(pl.multiple_of(D + head * HEAD, HEAD), HEAD), :]
                out = dot(vT, pb[:, j * R:(j + 1) * R], 1, 0) * inv[:, j * R:(j + 1) * R]
                attT[m, rows, :] = out.astype(bf16)
            return c
        lax.fori_loop(0, HEADS // 2, body, 0)

    def view_attention(m, v):
        col = blk(v)
        for hp in range(HEADS // 2):
            pair = slice(hp * BLK, (hp + 1) * BLK)
            q2 = paired(qT[m, pair, col])
            s = dot(kv[m, col, pair], q2, 1, 0)
            top = jnp.max(s, 0, keepdims=True) * (SCALE * LOG2E)
            p = jnp.exp2(s * (SCALE * LOG2E) - top)
            inv = 1.0 / jnp.sum(p, 0, keepdims=True)
            pb = p.astype(bf16)
            PT[4 * m + hp, col, 0:2 * BLK] = pb
            for j in range(2):
                linv[m, 2 * hp + j, :, col] = inv[:, j * BLK:(j + 1) * BLK]
            out = dot(kvT[m, D + hp * BLK:D + (hp + 1) * BLK, col], pb, 1, 0) * inv
            attT[m, pair, col] = jnp.concatenate([out[:HEAD, :BLK], out[HEAD:, BLK:]], 0).astype(bf16)

    def mlp_block(m, i, late):
        mid = h[m, blk(i)].astype(f32) + dot(attT[m, :, blk(i)], wo[...], 0, 0) + shift[1]
        hm[m, blk(i)] = mid
        xhat, _ = normalise(mid)
        n = (xhat * gain1 + shift[2]).astype(bf16)
        nm[m, blk(i)] = n
        for k in range(0, FF, 256):
            a, slope = gelu_pair(dot(n, w1[:, k:k + 256], 1, 0) + fb[:, k:k + 256])
            act[m, blk(i), k:k + 256] = a.astype(bf16)
            gg[m, blk(i), k:k + 256] = slope.astype(bf16)
        late()
        out = mid + dot(act[m, blk(i)], w2[...], 1, 0) + shift[3]
        ob[m, blk(i)] = out.astype(bf16)

    def joint_mlp(m):
        hm[m] = h[m].astype(f32) + dot(attT[m], wo[...], 0, 0) + shift[1]
        for i in range(NB):
            row = slice(i * BLK, (i + 1) * BLK)
            xhat, _ = normalise(hm[m, row])
            nm[m, row] = (xhat * gain1 + shift[2]).astype(bf16)
        for k in range(0, FF, 256):
            a, slope = gelu_pair(dot(nm[m], w1[:, k:k + 256], 1, 0) + fb[:, k:k + 256])
            act[m, :, k:k + 256] = a.astype(bf16)
            gg[m, :, k:k + 256] = slope.astype(bf16)
        ob[m] = (hm[m] + dot(act[m], w2[...], 1, 0) + shift[3]).astype(bf16)

    def mid_back(m, row, gn):
        dv, dgain, dshift = norm_back(hm[m, row], gn, gain1)
        d32 = dy[m, row].astype(f32)
        mid = d32 + dv
        hm[m, row] = mid
        low = mid.astype(bf16)
        gb[m, row] = low
        sm[1:2] += dgain
        sm[4:5] += dshift
        sm[5:6] += jnp.sum(d32, 0, keepdims=True)
        sm[3:4] += jnp.sum(low.astype(f32), 0, keepdims=True)

    def pre_back(m, row, width):
        d = dy[m, row]
        for k in range(0, FF, width):
            gp = (dot(d, w2[k:k + width], 1, 1) * gg[m, row, k:k + width].astype(f32)).astype(bf16)
            gg[m, row, k:k + width] = gp
            sb[:, k:k + width] += jnp.sum(gp.astype(f32), 0, keepdims=True)

    def mlp_back_block(m, i):
        pre_back(m, blk(i), 512)
        mid_back(m, blk(i), dot(gg[m, blk(i)], w1[...], 1, 1))

    def joint_mlp_back(m):
        pre_back(m, slice(0, R), 256)
        gn = dot(gg[m], w1[...], 1, 1)
        for i in range(NB):
            row = slice(i * BLK, (i + 1) * BLK)
            mid_back(m, row, gn[row])

    def att_grad(m):
        dOT[...] = dot(wo[...], gb[m], 1, 1).astype(bf16)

    def joint_attention_back(m):
        def body(hp, c):
            pair = blk(hp)
            inv = jnp.concatenate([linv[m, 2 * hp], linv[m, 2 * hp + 1]], 1)
            d2 = (paired(dOT[pair, :]).astype(f32) * inv).astype(bf16)
            vcol = pl.ds(pl.multiple_of(D + hp * BLK, BLK), BLK)
            dp = dot(kv[m, :, vcol], d2, 1, 0)
            pb = jnp.concatenate([PT[2 * hp], PT[2 * hp + 1]], 1)
            p = pb.astype(f32)
            inner = jnp.sum(p * dp, 0, keepdims=True) * inv
            ds = (p * (dp - inner)).astype(bf16)
            q2 = paired(qT[m, pair, :])
            kvT[m, vcol, :] = dot(d2, pb, 1, 1).astype(bf16)
            dq = dot(kvT[m, pair, :], ds, 1, 0) * SCALE
            dq0, dq1 = dq[:HEAD, :R], dq[HEAD:, R:]
            kvT[m, pair, :] = (dot(q2, ds, 1, 1) * SCALE).astype(bf16)
            qT[m, pair, :] = jnp.concatenate([dq0, dq1], 0).astype(bf16)
            return c
        lax.fori_loop(0, HEADS // 2, body, 0)

    def view_attention_back(m, first, last):
        def body(hp, c):
            vrow = pl.ds(pl.multiple_of(D + hp * BLK, BLK), BLK)
            pair = blk(hp)
            for v in range(NB):
                col = slice(v * BLK, (v + 1) * BLK)
                inv = jnp.concatenate([linv[m, 2 * hp, :, col], linv[m, 2 * hp + 1, :, col]], 1)
                d2 = (paired(dOT[pair, col]).astype(f32) * inv).astype(bf16)
                dp = dot(kv[m, col, vrow], d2, 1, 0)
                pb = PT[4 * m + hp, col, 0:2 * BLK]
                p = pb.astype(f32)
                inner = jnp.sum(p * dp, 0, keepdims=True) * inv
                ds = (p * (dp - inner)).astype(bf16)
                q2 = paired(qT[m, pair, col])
                dv = dot(d2, pb, 1, 1).astype(bf16)
                dq = dot(kvT[m, pair, col], ds, 1, 0) * SCALE
                dk = (dot(q2, ds, 1, 1) * SCALE).astype(bf16)
                kvT[m, vrow, col] = dv
                kvT[m, pair, col] = dk
                qT[m, pair, col] = jnp.concatenate([dq[:HEAD, :BLK], dq[HEAD:, BLK:]], 0).astype(bf16)
            return c
        lax.fori_loop(first, last, body, 0)

    def qkv_back(m, joint):
        for first, last in ((0, 1), (1, NB)):
            rows = slice(first * BLK, last * BLK)
            gn = dot(qT[m, :, rows], wq[:, :D], 0, 1) + dot(kvT[m, :, rows], wq[:, D:], 0, 1)
            for i in range(first, last):
                row = slice(i * BLK, (i + 1) * BLK)
                part = gn[(i - first) * BLK:(i - first + 1) * BLK]
                dv, dgain, dshift = norm_back(h[m, row].astype(f32), part, gain0)
                sm[0:1] += dgain
                sm[2:3] += dshift
                out = (hm[m, row] + dv).astype(bf16)
                if joint:
                    h[m, row] = out
                    grad_copy(m, i).start()
                else:
                    ob[m, row] = out
        if joint:
            gn = dot(kvT[m, :, R:KP], wq[:, D:], 0, 1)
            sm[0:1] += jnp.sum(gn * lx[m], 0, keepdims=True)
            sm[2:3] += jnp.sum(gn, 0, keepdims=True)

    UP, QKV, OUT = FF // D, 2 * (FF // D), 2 * (FF // D) + 3

    def cols(k):
        return pl.ds(pl.multiple_of(k * D, D), D)

    def put(u, t):
        G[u] = (G[u].astype(f32) + t).astype(bf16)

    def down_weights(ms, first, count, unroll=1, rows=slice(None)):
        def body(k, c):
            put(k, sum(dot(act[m, rows, cols(k)], dy[m, rows], 0, 0) for m in ms))
            return c
        lax.fori_loop(first, first + count, body, 0, unroll=unroll)

    def up_weights(ms, first, count, unroll=1):
        def body(k, c):
            put(UP + k, sum(dot(nm[m], gg[m, :, cols(k)], 0, 0) for m in ms))
            return c
        lax.fori_loop(first, first + count, body, 0, unroll=unroll)

    def attention_weights(ms, joint):
        keys = KP if joint else R
        put(QKV, sum(dot(nT[m, :, 0:R], qT[m], 1, 1) for m in ms))

        def body(k, c):
            put(QKV + 1 + k, sum(dot(nT[m, :, 0:keys], kvT[m, cols(k), 0:keys], 1, 1) for m in ms))
            return c
        lax.fori_loop(0, 2, body, 0, unroll=len(ms) == 1)
        put(OUT, sum(dot(attT[m], gb[m], 1, 0) for m in ms))

    def small_sums():
        rows = [sm[i:i + 1] for i in range(6)] + [sb[:, k * D:(k + 1) * D] for k in range(FF // D)]
        GS[...] = jnp.zeros_like(GS)
        parts = [row[:, j * BLK:(j + 1) * BLK] for row in rows for j in range(D // BLK)]
        parts += [jnp.zeros((1, BLK), f32)] * (-len(parts) % 16)
        GS[0:len(parts)] = jnp.concatenate(parts, 0).astype(bf16)

    if tree:
        (t_send, t_recv, free) = rest
        dp = lax.axis_index("dp")
        bits = lax.axis_size("dp").bit_length() - 1
        bit = [lax.rem(dp // (1 << k), 2) for k in range(bits)]
        partner = [{"dp": dp + (1 - 2 * bit[k]) * (1 << k)} for k in range(bits)]

        def refs(g):
            return (GS, VS) if g == UNITS else (G.at[g], V.at[g])

        def order(g):
            return (0,) + tuple(range(2, bits)) + (1,) if g in LINE_FIRST else tuple(range(bits))

        def rows_of(ref, first, size):
            return ref.at[pl.ds(first, size)]

        def height(g):
            return GS.shape[0] if g == UNITS else D

        def offset(g, k):
            total = sum((bit[order(g)[j]] * (height(g) >> (j + 1)) for j in range(k + 1)), 0)
            return pl.multiple_of(total, 16)

        def tree_copy(g, k):
            mine, theirs = refs(g)
            rows = height(g)
            if k < bits:
                size = rows >> (k + 1)
                away = 1 - bit[order(g)[k]]
                src = rows_of(mine, pl.multiple_of(offset(g, k - 1) + away * size, 16), size)
                dst = rows_of(theirs, rows - (rows >> k), size)
                to = partner[order(g)[k]]
            else:
                j = 2 * bits - 1 - k
                size = rows >> (j + 1)
                src = dst = rows_of(mine, offset(g, j), size)
                to = partner[order(g)[j]]
            return pltpu.make_async_remote_copy(src_ref=src, dst_ref=dst, send_sem=t_send.at[g, k],
                                                recv_sem=t_recv.at[g, k], device_id=to, device_id_type=MESH)

        def add_rows(put_to, first, taken, there, size):
            step = min(size, 64)

            def add(i, c):
                here = pl.ds(pl.multiple_of(first + i * step, 16), step)
                part = pl.ds(pl.multiple_of(there + i * step, 16), step)
                put_to[here, :] = (put_to[here, :].astype(f32) + taken[part, :].astype(f32)).astype(bf16)
                return c
            lax.fori_loop(0, size // step, add, 0)

        def take(g, k):
            tree_copy(g, k - 1).wait_recv()
            if k <= bits:
                tree_copy(g, k - 1).wait_send()
                pl.semaphore_signal(free.at[g, k - 1], inc=1, device_id=partner[order(g)[k - 1]], device_id_type=MESH)
                rows = height(g)
                mine, theirs = refs(g)
                add_rows(mine, offset(g, k - 1), theirs, rows - (rows >> (k - 1)), rows >> k)

        def give(g, k):
            if k >= bits:
                pl.semaphore_wait(free.at[g, 2 * bits - 1 - k], 1)
            if k < 2 * bits:
                tree_copy(g, k).start()

        def event(g, k):
            if g == GUEST:
                pl.when(sec == 1)(functools.partial(guest_event, k))
            elif g == LENT and 0 < k < 2 * bits:
                lent_event(k)
            else:
                if k > 0:
                    take(g, k)
                if k < 2 * bits:
                    give(g, k)

        half = D // 2
        guest = PT.at[0, pl.ds(0, half), pl.ds(0, D)]
        lent = G.at[LENT, pl.ds(pl.multiple_of(bit[0] * half, 16), half)]

        def lend():
            return pltpu.make_async_remote_copy(src_ref=lent, dst_ref=guest, send_sem=t_send.at[GUEST, 0],
                                                recv_sem=t_recv.at[GUEST, 0], device_id=peer, device_id_type=MESH)

        def hand_back():
            return pltpu.make_async_remote_copy(src_ref=guest, dst_ref=lent, send_sem=t_send.at[GUEST, 7],
                                                recv_sem=t_recv.at[GUEST, 7], device_id=peer, device_id_type=MESH)

        def lent_event(k):
            if k == 1:
                take(LENT, 1)

                @pl.when(sec == 0)
                def _():
                    lend().start()

                @pl.when(sec == 1)
                def _():
                    give(LENT, 1)
            elif k < 2 * bits - 1:
                @pl.when(sec == 1)
                def _():
                    take(LENT, k)
                    give(LENT, k)
                if k == 4:
                    @pl.when(sec == 0)
                    def _():
                        lend().wait_send()
                        pl.semaphore_signal(free.at[GUEST, 0], inc=1, device_id=peer, device_id_type=MESH)
            else:
                @pl.when(sec == 0)
                def _():
                    hand_back().wait_recv()

                @pl.when(sec == 1)
                def _():
                    take(LENT, k)
                give(LENT, k)

        def guest_offset(k):
            total = sum((bit[j] * (D >> (j + 1)) for j in range(1, k + 1)), 0)
            return pl.multiple_of(total, 16)

        def guest_copy(k):
            j = k if k < bits else 2 * bits - 1 - k
            size = D >> (j + 1)
            if k < bits:
                first = pl.multiple_of(guest_offset(k - 1) + (1 - bit[k]) * size, 16)
                dst = VG.at[pl.ds(half - (half >> (k - 1)), size)]
            else:
                first = guest_offset(j)
                dst = PT.at[0, pl.ds(first, size), pl.ds(0, D)]
            return pltpu.make_async_remote_copy(
                src_ref=PT.at[0, pl.ds(first, size), pl.ds(0, D)], dst_ref=dst, send_sem=t_send.at[GUEST, k],
                recv_sem=t_recv.at[GUEST, k], device_id=partner[j], device_id_type=MESH)

        def guest_event(k):
            if k == 1:
                lend().wait_recv()
            else:
                guest_copy(k - 1).wait_recv()
                if k <= bits:
                    guest_copy(k - 1).wait_send()
                    pl.semaphore_signal(free.at[GUEST, k - 1], inc=1, device_id=partner[k - 1], device_id_type=MESH)
                    add_rows(guest, guest_offset(k - 1), VG, half - (half >> (k - 2)), D >> k)
            if k < 2 * bits - 1:
                if k >= bits:
                    pl.semaphore_wait(free.at[GUEST, 2 * bits - 1 - k], 1)
                guest_copy(k).start()
            else:
                pl.semaphore_wait(free.at[GUEST, 0], 1)
                hand_back().start()

        def settle():
            for g in range(UNITS + 1):
                for k in range(bits, 2 * bits):
                    if g == LENT and k < 2 * bits - 1:
                        pl.when(sec == 1)(tree_copy(g, k).wait_send)
                    else:
                        tree_copy(g, k).wait_send()

            @pl.when(sec == 1)
            def _():
                for k in range(bits, 2 * bits - 1):
                    guest_copy(k).wait_send()
                hand_back().wait_send()

    def run(tokens):
        if tree:
            for token in tokens:
                event(token // 10, token % 10)

    @pl.when(sec == 0)
    def _():
        in_copy(0, h).start()
        w_copy(0).start()

    @pl.when(sec == 1)
    def _():
        for k in range(4):
            w_copy(k).start()
        for m in range(micro):
            in_copy(m, dy).start()

    barrier = pltpu.get_barrier_semaphore()
    greeted = [peer] + (partner if tree else [])
    for device in greeted:
        pl.semaphore_signal(barrier, inc=1, device_id=device, device_id_type=MESH)
    sm[...] = jnp.zeros_like(sm)
    sb[...] = jnp.zeros_like(sb)

    @pl.when(sec == 0)
    def _():
        def forward(m, c):
            in_copy(m, h).wait()

            @pl.when(m == 0)
            def _():
                w_copy(0).wait()
                for k in range(1, 4):
                    w_copy(k).start()
                for j in range(1, micro):
                    in_copy(j, h).start()

            def view(i, c):
                qkv_block(m, i)
                view_attention(m, i)

                @pl.when((m == 0) & (i == 0))
                def _():
                    w_copy(1).wait()
                    w_copy(2).wait()

                def late():
                    @pl.when((m == 0) & (i == 0))
                    def _():
                        w_copy(3).wait()
                mlp_block(m, i, late)

                @pl.when((m == 0) & (i == 0))
                def _():
                    pl.semaphore_wait(barrier, len(greeted))

                @pl.when((m > 0) & (i == 0))
                def _():
                    for j in range(NB):
                        act_copy(m - 1, j).wait_send()
                act_copy(m, i).start()
                return c
            lax.fori_loop(0, NB, view, 0)
            return c
        lax.fori_loop(0, micro, forward, 0)
        for j in range(NB):
            act_copy(micro - 1, j).wait_send()

        G[...] = jnp.zeros_like(G)

        def backward(m, c):
            final = m == micro - 1

            def when_final(tokens):
                if tree and tokens:
                    @pl.when(final)
                    def _():
                        run(tokens)

            def body(i, c):
                last = i == NB - 1

                @pl.when(last)
                def _():
                    down_weights([m], 0, FF // D, 1, slice(0, R - BLK))
                grad_copy(m, i).wait_recv()

                @pl.when(last)
                def _():
                    down_weights([m], 0, 2, 2, slice(R - BLK, R))
                    when_final((0, 10) + AFTER_DOWN)
                    down_weights([m], 2, 2, 2, slice(R - BLK, R))
                    when_final((20, 30) + AFTER_DOWN2)
                mlp_back_block(m, i)
                return c
            lax.fori_loop(0, NB, body, 0)
            when_final(AFTER_BLOCK)
            up_weights([m], 0, 2, 2)
            when_final((40, 50) + AFTER_UP)
            up_weights([m], 2, 2, 2)
            when_final((60, 70) + AFTER_UP2)
            att_grad(m)
            when_final(AFTER_GRAD)
            view_attention_back(m, 0, 2)
            when_final(AFTER_HALF)
            view_attention_back(m, 2, 4)
            when_final(AFTER_VIEWS)
            qkv_back(m, False)
            when_final(AFTER_QKV)
            attention_weights([m], False)
            return c
        lax.fori_loop(0, micro, backward, 0)

    @pl.when(sec == 1)
    def _():
        for k in range(4):
            w_copy(k).wait()
        for m in range(micro):
            in_copy(m, dy).wait()
        pl.semaphore_wait(barrier, len(greeted))
        for m in range(micro):
            lang_phase(m)

        def item(m, c):
            joint_qkv(m)
            joint_attention(m)
            joint_mlp(m)
            joint_mlp_back(m)
            att_grad(m)
            joint_attention_back(m)
            qkv_back(m, True)
            return c
        lax.fori_loop(0, micro, item, 0)
        G[...] = jnp.zeros_like(G)
        down_weights(range(micro), 0, 4)
        run((0, 10, 20, 30))
        up_weights(range(micro), 0, 4)
        run((40, 50, 60, 70) + BEFORE)
        attention_weights(range(micro), True)

    small_sums()
    if tree:
        run((80, 90, 100, 110, 120) + REST)
        settle()

    @pl.when(sec == 1)
    def _():
        for m in range(micro):
            for i in range(NB):
                grad_copy(m, i).wait_send()


def local(section_data, lang_feat, lang_ids, view_mask, norm_gains, shifts, fc1_bias, w_qkv, w_out, w_fc1, w_fc2):
    micro, rows, D = section_data.shape[1], section_data.shape[3], section_data.shape[4]
    FF = w_fc1.shape[2]
    lang = lang_feat.shape[2]
    lang_rows = jnp.transpose(lang_feat, (1, 2, 0, 3))
    KP = rows + -(-lang // 16) * 16
    NB = rows // BLK
    hbm = pl.BlockSpec(memory_space=pl.ANY)
    vmem = pl.BlockSpec(memory_space=pltpu.VMEM)
    smem = pl.BlockSpec(memory_space=pltpu.SMEM)
    V = pltpu.VMEM
    dma = pltpu.SemaphoreType.DMA
    sds = jax.ShapeDtypeStruct
    units = 2 * (FF // D) + 4
    tree = lax.axis_size("dp") == 16 and D % 256 == 0 and units == UNITS
    kept = ((micro, rows, D), (units, D, D), (256, BLK))
    scratch = [
        V((micro, rows, D), bf16),
        V((micro, rows, D), bf16),
        V((D, 3 * D), bf16), V((D, D), bf16), V((D, FF), bf16), V((FF, D), bf16),
        V((micro, D, KP), bf16),
        V((micro, D, rows), bf16),
        V((micro, 2 * D, KP), bf16),
        V((micro, KP, 2 * D), bf16),
        V((HEADS, KP, rows), bf16),
        V((micro, HEADS, 1, rows), f32),
        V((micro, D, rows), bf16),
        V((micro, rows, D), f32),
        V((micro, rows, D), bf16),
        V((micro, rows, FF), bf16),
        V((micro, rows, FF), bf16),
        V((micro, rows, D), bf16),
        V((D, rows), bf16),
        V((micro, KP, BLK), bf16),
        V((micro, KP - rows, D), f32),
        V((8, D), f32), V((1, FF), f32),
    ]
    if tree:
        scratch += [V((units, D - D // 16, D), bf16), V((256 - 16, BLK), bf16),
                    V((D // 2 - D // 16, D), bf16)]
    scratch += [dma((micro,)), dma((4,)),
                dma((micro, NB)), dma((micro, NB)), dma((micro, NB)), dma((micro, NB))]
    if tree:
        scratch += [dma((units + 2, 8)), dma((units + 2, 8)),
                    pltpu.SemaphoreType.REGULAR((units + 2, 4))]
    res, *grads = pl.pallas_call(
        step_kernel,
        out_shape=tuple((V if tree else sds)(shape, bf16) for shape in kept),
        in_specs=[hbm, vmem, vmem, smem, vmem, vmem, vmem, hbm, hbm, hbm, hbm],
        out_specs=(vmem,) * 3,
        scratch_shapes=scratch,
        compiler_params=pltpu.CompilerParams(
            collective_id=0, has_side_effects=True, vmem_limit_bytes=VMEM_LIMIT - (KEPT_BYTES if tree else 0)),
        name="two_layers",
    )(section_data, lang_rows, lang_ids, view_mask, norm_gains, shifts, fc1_bias, w_qkv, w_out, w_fc1, w_fc2)
    if not tree:
        grads = lax.psum(grads, "dp")
    return unpack(res, *grads, section_data.shape, FF)


def unpack_kernel(rows, low, small, out_res, gain, shift, b1, gq, go, g1, g2, wide, out_sem, res_sem):
    units, D = low.shape[0], low.shape[1]
    UP = g1.shape[2] // D
    micro = rows.shape[0]
    out = [pltpu.make_async_copy(rows.at[m], out_res.at[0, m, 0], res_sem.at[m]) for m in range(micro)]
    for copy in out:
        copy.start()
    stores = []
    for u in range(units):
        wide[u] = low[u].astype(f32)
        if u < UP:
            dst = g2.at[0, pl.ds(u * D, D)]
        elif u < 2 * UP:
            dst = g1.at[0, :, pl.ds((u - UP) * D, D)]
        elif u < 2 * UP + 3:
            dst = gq.at[0, :, pl.ds((u - 2 * UP) * D, D)]
        else:
            dst = go.at[0]
        stores.append(pltpu.make_async_copy(wide.at[u], dst, out_sem.at[u]))
        stores[-1].start()
    width = D // BLK
    for i in range(6 + UP):
        for j in range(width):
            at = i * width + j
            part = small[at:at + 1].astype(f32)
            if i < 2:
                gain[0, i:i + 1, j * BLK:(j + 1) * BLK] = part
            elif i < 6:
                shift[0, i - 2:i - 1, j * BLK:(j + 1) * BLK] = part
            else:
                b1[0:1, (i - 6) * D + j * BLK:(i - 6) * D + (j + 1) * BLK] = part
    for copy in stores + out:
        copy.wait()


def unpack(rows, low, small, shape, FF):
    sds = jax.ShapeDtypeStruct
    units, D = low.shape[0], low.shape[1]
    hbm = pl.BlockSpec(memory_space=pl.ANY)
    vmem = pl.BlockSpec(memory_space=pltpu.VMEM)
    dma = pltpu.SemaphoreType.DMA
    return pl.pallas_call(
        unpack_kernel,
        in_specs=[vmem, vmem, vmem],
        out_specs=(hbm, vmem, vmem, vmem, hbm, hbm, hbm, hbm),
        out_shape=(sds(shape, bf16), sds((1, 2, D), f32), sds((1, 4, D), f32), sds((1, FF), f32),
                   sds((1, D, 3 * D), f32), sds((1, D, D), f32), sds((1, D, FF), f32), sds((1, FF, D), f32)),
        scratch_shapes=[pltpu.VMEM(low.shape, f32), dma((units,)), dma((rows.shape[0],))],
        compiler_params=pltpu.CompilerParams(vmem_limit_bytes=32 * 2**20),
        name="unpack",
    )(rows, low, small)


def solution(mesh):
    weights = P("section", None, None)
    rows = P("section", None, "dp", None, None)
    return jax.shard_map(
        local,
        mesh=mesh,
        in_specs=(rows, P(None, "dp", None, None), P(None, "dp", None), P(None, "dp", None), weights, weights,
                  P("section", None), weights, weights, weights, weights),
        out_specs=(rows, weights, weights, P("section", None), weights, weights, weights, weights),
        check_vma=False,
    )
```
